256 devices in a mesh: gx: 32 (over y, z), gy: 8 (over x, core).
Axes of the slice: x: 4, y: 4, z: 8, core: 2. Of those that a mesh axis runs over, the one named last changes fastest.
Arguments:
- tracer_cotangent: float32 [25, 512, 4096], P(None, 'gy', 'gx'), may hold values from -6 to 6
- height_cotangent: float32 [512, 4096], P('gy', 'gx'), may hold values from -6 to 6
- east_velocity: float32 [25, 512, 4096], P(None, 'gy', 'gx'), may hold values from -4 to 4
- north_velocity: float32 [25, 512, 4096], P(None, 'gy', 'gx'), may hold values from -4 to 4
- diffusivity: float32 [25, 512, 4096], P(None, 'gy', 'gx'), may hold values from 0.1 to 1
- thickness: float32 [25], replicated, may hold values from 0.5 to 2
- depth_levels: int32 [512, 4096], P('gy', 'gx'), may hold values from 0 to 25
- fold_partner: int32 [4096], P('gx'), may hold values from 0 to 4095, as said below
Outputs:
- tracer_adjoint: float32 [25, 512, 4096], P(None, 'gy', 'gx')
- height_adjoint: float32 [512, 4096], P('gy', 'gx')
The draws below stay inside these ranges and needn't reach their ends.
Inputs may be any that keep to these rules, and one draw needn't show every extreme that they name: fold_partner[i] = (s - 1 - i) mod 4096 for one s, so the map is its own inverse.
All inputs are finite; a program needn't handle non-finite values.
Results may differ from the reference program's by a relative error of at most 0.00013.
Values sent between devices are 32-bit elements; how exact they have to be, the bound alone decides.
A program may use at most 128 MiB of HBM per device.

```python
import math
import jax
import jax.numpy as jnp
from jax import lax

K = 25
CX = 128
CY = 64
ITERS = 3
NX = 4096
NY = 512


def draw_depth_levels(key, part):
    key = jax.random.fold_in(key, 11)
    key_block, key_cell = jax.random.split(key)
    ceilings = jax.random.randint(key_block, (NY // CY, NX // CX), 1, K + 1)
    ceilings = ceilings.at[0, 0].set(K)
    spread = jnp.repeat(jnp.repeat(ceilings, CY, axis=0), CX, axis=1)
    cells = jax.random.randint(key_cell, (NY, NX), 0, K + 1)
    levels = jnp.minimum(cells, spread)
    levels = levels.at[0, 0].set(K).at[0, 1].set(0)
    return levels.astype(jnp.int32)


def draw_fold_partner(key, part):
    key = jax.random.fold_in(key, 23)
    seam = jax.random.randint(key, (), 0, NX)
    columns = jnp.arange(NX, dtype=jnp.int32)
    return jnp.mod(seam - 1 - columns, NX).astype(jnp.int32)


def steps_of(stream_key, extent, cuts, least, top_value):
    loudness = 1.0
    for axis_at, parts in cuts:
        draws = jax.random.uniform(jax.random.fold_in(jax.random.fold_in(stream_key, 6), axis_at), (parts,), jnp.float32, least / len(cuts), top_value / len(cuts))
        loudness = loudness * jnp.repeat(jnp.exp(draws), extent[axis_at] // parts).reshape((-1,) + (1,) * (len(extent) - 1 - axis_at))
    return loudness


def centred(key, extent, width, bound, cuts=(), kind=jnp.bfloat16):
    values = jax.random.normal(key, extent, jnp.float32) * width
    if len(cuts) > 0:
        values = steps_of(key, extent, cuts, -0.22, 0.18) * values
    return jnp.clip(values, min=-bound, max=bound).astype(kind)


def setup_inputs(seed: int = 0) -> dict:
    key_list = jax.random.split(jax.random.key(seed), 9)
    tracer_cotangent = centred(key_list[0], (K, NY, NX), 1.0, 6.0, ((1, 8), (2, 32)), jnp.float32)
    height_cotangent = centred(key_list[1], (NY, NX), 1.0, 6.0, ((0, 8), (1, 32)), jnp.float32)
    east_velocity = centred(key_list[2], (K, NY, NX), 0.6, 4.0, ((1, 8), (2, 32)), jnp.float32)
    north_velocity = centred(key_list[3], (K, NY, NX), 0.6, 4.0, ((1, 8), (2, 32)), jnp.float32)
    diffusivity = jnp.clip(jnp.exp(math.log(1.0) - 2.3025851 * jax.random.uniform(key_list[4], (K, NY, NX), jnp.float32) ** steps_of(key_list[4], (K, NY, NX), ((1, 8), (2, 32)), -0.2, 0.2)), 0.1, 1.0)
    thickness = jnp.clip(jnp.exp(jax.random.uniform(key_list[5], (K,), jnp.float32, math.log(0.5), math.log(2.0))), 0.5, 2.0)
    depth_levels = draw_depth_levels(jax.random.fold_in(key_list[8], 71), 0)
    fold_partner = draw_fold_partner(jax.random.fold_in(key_list[8], 71), 0)
    return dict(tracer_cotangent=tracer_cotangent, height_cotangent=height_cotangent, east_velocity=east_velocity, north_velocity=north_velocity, diffusivity=diffusivity, thickness=thickness, depth_levels=depth_levels, fold_partner=fold_partner)


damping = 0.1
conduct = 1.0
time_step = 0.3

def extend(field, sign, partner):
    north = jnp.take(field[-1, :], partner, axis=0) * sign
    south = jnp.zeros_like(north)
    rows = jnp.concatenate([south[None, :], field, north[None, :]], axis=0)
    return jnp.concatenate([rows[:, -1:], rows, rows[:, :1]], axis=1)

def sides(padded):
    return (padded[1:-1, 2:], padded[1:-1, :-2], padded[2:, 1:-1], padded[:-2, 1:-1])

def face_flux(t_a, t_b, w_a, w_b, s_a, s_b, k_a, k_b):
    return w_a * w_b * ((s_a + s_b) * 0.25 * (t_a + t_b) - 0.5 * (k_a + k_b) * (t_b - t_a))

def level_step(tracer, wet, east, north, kappa, partner):
    t_pad = extend(tracer, 1.0, partner)
    w_pad = extend(wet, 1.0, partner)
    u_pad = extend(east, 1.0, partner)
    v_pad = extend(north, -1.0, partner)
    k_pad = extend(kappa, 1.0, partner)
    t_e, t_w, t_n, t_s = sides(t_pad)
    w_e, w_w, w_n, w_s = sides(w_pad)
    u_e, u_w, u_n, u_s = sides(u_pad)
    v_e, v_w, v_n, v_s = sides(v_pad)
    k_e, k_w, k_n, k_s = sides(k_pad)
    flux_east = face_flux(tracer, t_e, wet, w_e, east, u_e, kappa, k_e)
    flux_west = face_flux(t_w, tracer, w_w, wet, u_w, east, k_w, kappa)
    flux_north = face_flux(tracer, t_n, wet, w_n, north, v_n, kappa, k_n)
    flux_south = face_flux(t_s, tracer, w_s, wet, v_s, north, k_s, kappa)
    return tracer + time_step * wet * (flux_west - flux_east + flux_south - flux_north)

def operator(field, conductances, partner):
    nbrs = sides(extend(field, 1.0, partner))
    total = damping * field
    for cond, nbr in zip(conductances, nbrs):
        total = total + cond * (field - nbr)
    return total

def reference(tracer_cotangent, height_cotangent, east_velocity, north_velocity, diffusivity, thickness, depth_levels, fold_partner):
    levels_f = depth_levels.astype(jnp.float32)
    wet = (jnp.arange(K, dtype=jnp.int32)[:, None, None] < depth_levels[None]).astype(jnp.float32)
    d_pad = extend(levels_f, 1.0, fold_partner)
    conductances = [conduct * jnp.minimum(levels_f, nbr) / K for nbr in sides(d_pad)]
    height_adjoint = jnp.zeros_like(height_cotangent)
    residual = height_cotangent
    direction = residual
    norm_now = jnp.sum(residual * residual)
    for step in range(ITERS):
        image = operator(direction, conductances, fold_partner)
        alpha = norm_now / jnp.sum(direction * image)
        height_adjoint = height_adjoint + alpha * direction
        residual = residual - alpha * image
        norm_next = jnp.sum(residual * residual)
        direction = residual + norm_next / norm_now * direction
        norm_now = norm_next
    total = tracer_cotangent + thickness[:, None, None] * wet * height_adjoint[None]

    def one_level(items):
        cot, wet_l, east_l, north_l, kappa_l = items
        _, pull = jax.vjp(lambda t: level_step(t, wet_l, east_l, north_l, kappa_l, fold_partner), cot)
        return pull(cot)[0]
    tracer_adjoint = lax.map(one_level, (total, wet, east_velocity, north_velocity, diffusivity))
    return (tracer_adjoint, height_adjoint)
```

```python
import functools

import jax
import jax.numpy as jnp
from jax import lax
from jax.experimental import pallas as pl
from jax.experimental.pallas import tpu as pltpu
from jax.sharding import PartitionSpec as P

MESH = pl.DeviceIdType.MESH
damping = 0.1
time_step = 0.3
ROWS = 64
LANES = 128
PAD = 16
FOLD = 56


def roll_lanes(x, shift):
    return pltpu.roll(x, shift, 1)


def kernel(
    nz, ny, nc, nx, levels,
    cot_h, b_h, u_h, v_h, k_h, th_s, dep_h, fp_s, out_h, hadj_h,
    cot, u, v, kap, dint, plane, wide, pack2, got2, dmin, vec1, vec2,
    edge_ew, got_ew, edge_n, edge_s, got_n, got_s,
    mir2, all2, foldz, fold_stage, fold_y, fold_rows,
    qn, qs, coef_e, coef_w, coef_n, coef_s, base, outv, hv,
    mom, red1, mom2, red2, tot,
    load_sem, store_sem, send_sem, halo_sem, edge_sem, red_sem, fold_sem,
):
    gx, gy = lax.axis_index("gx"), lax.axis_index("gy")
    ngx, ngy = ny * nz, nx * nc
    y, z, x, c = gx // nz, gx % nz, gy // nc, gy % nc
    top = gy == ngy - 1
    lane = lax.broadcasted_iota(jnp.int32, (ROWS, LANES), 1)
    lane80 = lax.broadcasted_iota(jnp.int32, (80, LANES), 1)
    f32 = jnp.float32

    def at(dx, dy):
        return (gx + dx + ngx) % ngx, (gy + dy + ngy) % ngy

    compass = [(1, 0), (-1, 0), (0, 1), (0, -1), (1, 1), (-1, 1), (1, -1), (-1, -1)]

    loads = [
        pltpu.make_async_copy(b_h, plane.at[0, pl.ds(PAD, ROWS)], load_sem.at[0]),
        pltpu.make_async_copy(dep_h, dint, load_sem.at[1]),
        pltpu.make_async_copy(cot_h, cot.at[:, pl.ds(8, ROWS)], load_sem.at[2]),
        pltpu.make_async_copy(u_h, u, load_sem.at[3]),
        pltpu.make_async_copy(k_h, kap, load_sem.at[4]),
        pltpu.make_async_copy(v_h, v, load_sem.at[5]),
    ]
    for load in loads:
        load.start()

    barrier = pltpu.get_barrier_semaphore()

    def greet(device):
        pl.semaphore_signal(barrier, inc=1, device_id=device, device_id_type=MESH)

    n1, n2 = nz * nc, nx * ny
    me1, me2 = z * nc + c, x * ny + y

    def peer1(j):
        p = (me1 + j) % n1
        return y * nz + p // nc, x * nc + p % nc

    def peer2(j):
        p = (me2 + j) % n2
        return (p % ny) * nz + z, (p // ny) * nc + c

    for d in compass:
        greet(at(*d))

    @pl.loop(1, n1)
    def _(j):
        greet(peer1(j))

    @pl.loop(1, n2)
    def _(j):
        greet(peer2(j))

    @pl.when(top)
    def _():
        @pl.loop(1, ngx)
        def _(j):
            greet(at(j, 0))

    zero8 = jnp.zeros((8, LANES), f32)
    for f in range(2):
        for part in (plane, wide, vec1, vec2):
            part[f, 0:8] = zero8
            part[f, 88:96] = zero8
    loads[0].wait()
    loads[1].wait()
    depth_f = dint[...].astype(f32)
    plane[1, PAD:PAD + ROWS] = depth_f
    pack2[...] = jnp.where(
        (lane < 32) | (lane >= 96), plane[0, PAD:PAD + ROWS], roll_lanes(depth_f, 64)
    )

    pl.semaphore_wait(barrier, 8 + n1 - 1 + n2 - 1 + jnp.where(top, ngx - 1, 0))

    def send(src, dst, sem_out, sem_in, device):
        copy = pltpu.make_async_remote_copy(
            src_ref=src, dst_ref=dst, send_sem=sem_out, recv_sem=sem_in,
            device_id=device, device_id_type=MESH,
        )
        return copy

    first, last = pl.ds(PAD, 8), pl.ds(PAD + ROWS - 8, 8)
    south, north = pl.ds(PAD - 8, 8), pl.ds(PAD + ROWS, 8)
    halos = []
    for i, (dx, dy) in enumerate(compass):
        if dx == 0:
            src = plane.at[:, last if dy == 1 else first]
            dst = plane.at[:, south if dy == 1 else north]
        else:
            side = 0 if dx == 1 else 1
            if dy == 0:
                src, dst = pack2, got2.at[side, pl.ds(8, ROWS)]
            elif dy == 1:
                src, dst = pack2.at[pl.ds(ROWS - 8, 8)], got2.at[side, pl.ds(0, 8)]
            else:
                src, dst = pack2.at[pl.ds(0, 8)], got2.at[side, pl.ds(ROWS + 8, 8)]
        halos.append(send(src, dst, send_sem.at[i], halo_sem.at[i], at(dx, dy)))

    @pl.when(top)
    def _():
        for j in range(3):
            row = PAD + ROWS - 1 - j
            mir2[j:j + 1] = plane[0, row:row + 1]
            mir2[3 + j:4 + j] = plane[1, row:row + 1]
        mir2[6:8] = jnp.zeros((2, LANES), f32)
        all2[pl.ds(gx, 1)] = mir2[...][None]

        @pl.loop(1, ngx)
        def _(j):
            send(mir2, all2.at[gx], fold_sem.at[0], fold_sem.at[1], at(j, 0)).start()

    for halo in halos:
        halo.start()

    for load in loads[2:]:
        load.wait()
    half = jnp.where(lane < 64, 0.5, -0.5).astype(f32)
    edge_n[2 * levels:FOLD] = jnp.zeros((FOLD - 2 * levels, LANES), f32)
    edge_s[2 * levels:FOLD] = jnp.zeros((FOLD - 2 * levels, LANES), f32)

    def pack_level(k, acc):
        face = 0.25 * u[k] + half * kap[k]
        place = lane >> 1
        acc = jnp.where(place == k, roll_lanes(cot[k, 8:8 + ROWS], 2 * k + 1), acc)
        acc = jnp.where(place == k + 32, roll_lanes(face, 2 * k + 65), acc)
        edge_n[pl.ds(k, 1)] = cot[k, 7 + ROWS:8 + ROWS]
        edge_s[pl.ds(k, 1)] = cot[k, 8:9]
        edge_n[pl.ds(levels + k, 1)] = 0.25 * v[k, ROWS - 1:ROWS] - 0.5 * kap[k, ROWS - 1:ROWS]
        edge_s[pl.ds(levels + k, 1)] = 0.25 * v[k, 0:1] + 0.5 * kap[k, 0:1]
        return acc

    edge_ew[...] = lax.fori_loop(0, levels, pack_level, jnp.zeros((ROWS, LANES), f32))
    edges = [
        send(edge_ew, got_ew.at[0], send_sem.at[8], edge_sem.at[0], at(1, 0)),
        send(edge_ew, got_ew.at[1], send_sem.at[9], edge_sem.at[1], at(-1, 0)),
        send(edge_n, got_s, send_sem.at[10], edge_sem.at[2], at(0, 1)),
        send(edge_s, got_n, send_sem.at[11], edge_sem.at[3], at(0, -1)),
    ]
    for edge in edges:
        edge.start()

    @pl.when(top)
    def _():
        foldz[pl.ds(z, 1)] = edge_n[...][None]

        @pl.loop(1, nz)
        def _(j):
            p = y * nz + (z + j) % nz
            send(edge_n, foldz.at[z], fold_sem.at[2], fold_sem.at[3], (p, gy)).start()

    for halo in halos:
        halo.wait_recv()
    hw, he = got2[0], got2[1]
    wide[0, 8:88] = jnp.where(lane80 < 64, he, hw)
    wide[1, 8:88] = roll_lanes(jnp.where(lane80 < 64, hw, he), 64)

    seam = fp_s[0] + gx * LANES + 1

    @pl.when(gy == 0)
    def _():
        plane[1, 8:16] = zero8
        wide[1, 8:16] = zero8

    @pl.when(top)
    def _():
        pltpu.make_async_copy(all2.at[pl.ds(0, ngx - 1)], all2.at[pl.ds(0, ngx - 1)], fold_sem.at[1]).wait()
        start = (seam - 1 - gx * LANES - (LANES + 2) + 2 * ngx * LANES) % (ngx * LANES)
        blk, off = start // LANES, start % LANES
        window = jnp.concatenate([all2[(blk + i) % ngx] for i in range(3)], axis=1)
        col = lax.broadcasted_iota(jnp.int32, (3 * LANES, 2 * LANES), 1)
        src = lax.broadcasted_iota(jnp.int32, (3 * LANES, 2 * LANES), 0)
        col = jnp.where(col < 192, col, col - 256)
        pick = (src == off + (LANES + 2) - col).astype(f32)
        got = lax.dot(window, pick, precision=lax.Precision.HIGHEST, preferred_element_type=f32)
        edge_row = PAD + ROWS
        plane[0, edge_row:edge_row + 3] = got[0:3, :LANES]
        wide[0, edge_row:edge_row + 3] = got[0:3, LANES:]
        plane[1, edge_row:edge_row + 3] = got[3:6, :LANES]
        wide[1, edge_row:edge_row + 3] = got[3:6, LANES:]

    first_lane, last_lane = lane80 == 0, lane80 == LANES - 1

    def neighbours(mid, beside, rows):
        return [
            jnp.where(last_lane[:rows], roll_lanes(beside, LANES - 1), roll_lanes(mid, LANES - 1)),
            jnp.where(first_lane[:rows], roll_lanes(beside, 1), roll_lanes(mid, 1)),
        ]

    def both(mid, beside):
        return neighbours(mid, beside, 80), neighbours(beside, mid, 80)

    body, up, down = pl.ds(8, 80), pl.ds(9, 80), pl.ds(7, 80)
    dm, db = plane[1, body], wide[1, body]
    (d_e, d_w), (db_e, db_w) = both(dm, db)
    for i, (a, o) in enumerate(
        [(d_e, db_e), (d_w, db_w), (plane[1, up], wide[1, up]), (plane[1, down], wide[1, down])]
    ):
        dmin[i, 0] = jnp.minimum(dm, a)
        dmin[i, 1] = jnp.minimum(db, o)

    def apply(mid_ref, beside_ref, out_ref):
        mid, beside = mid_ref[body], beside_ref[body]
        (m_e, m_w), (s_e, s_w) = both(mid, beside)
        for i, (centre, nbrs) in enumerate(
            [
                (mid, (m_e, m_w, mid_ref[up], mid_ref[down])),
                (beside, (s_e, s_w, beside_ref[up], beside_ref[down])),
            ]
        ):
            total = jnp.zeros_like(centre)
            for j in range(4):
                total = total + dmin[j, i] * (centre - nbrs[j])
            out_ref[i, body] = damping * centre + (1.0 / levels) * total

    apply(plane.at[0], wide.at[0], vec1)
    apply(vec1.at[0], vec1.at[1], vec2)
    inner = pl.ds(PAD, ROWS)
    mid2 = vec2[0, inner]
    m_e, m_w = neighbours(mid2, vec2[1, inner], ROWS)
    nbrs = (m_e, m_w, vec2[0, PAD + 1:PAD + 1 + ROWS], vec2[0, PAD - 1:PAD - 1 + ROWS])
    mid3 = jnp.zeros_like(mid2)
    for j in range(4):
        mid3 = mid3 + dmin[j, 0, 8:8 + ROWS] * (mid2 - nbrs[j])
    mid3 = damping * mid2 + (1.0 / levels) * mid3
    mid0, mid1 = plane[0, inner], vec1[0, inner]

    def tile_sum(a):
        s = a[0:8]
        for i in range(1, ROWS // 8):
            s = s + a[8 * i:8 * i + 8]
        return jnp.sum(s, axis=0, keepdims=True)

    for j, (a, o) in enumerate(
        [(mid0, mid0), (mid0, mid1), (mid1, mid1), (mid1, mid2), (mid2, mid2), (mid2, mid3)]
    ):
        mom[j:j + 1] = tile_sum(a * o)
    mom[6:8] = jnp.zeros((2, LANES), f32)
    mom[...] = jnp.broadcast_to(jnp.sum(mom[...], axis=1, keepdims=True), (8, LANES))

    red1[pl.ds(me1, 1)] = mom[...][None]

    @pl.loop(1, n1)
    def _(j):
        send(mom, red1.at[me1], red_sem.at[0], red_sem.at[1], peer1(j)).start()

    for edge in edges:
        edge.wait_recv()

    @pl.when(top)
    def _():
        pltpu.make_async_copy(foldz.at[pl.ds(0, nz - 1)], foldz.at[pl.ds(0, nz - 1)], fold_sem.at[3]).wait()
        start = (seam - 1 - gx * LANES - (LANES - 1) + 2 * ngx * LANES) % (ngx * LANES)
        blk, off = start // LANES, start % LANES
        fold_stage[0] = foldz[blk % nz]
        fold_stage[1] = foldz[(blk + 1) % nz]
        fold_y[pl.ds(y, 1)] = fold_stage[...][None]

        @pl.loop(1, ny)
        def _(j):
            p = ((y + j) % ny) * nz + z
            send(fold_stage, fold_y.at[y], fold_sem.at[4], fold_sem.at[5], (p, gy)).start()

    def wait_red(buf, n, sem):
        pltpu.make_async_copy(buf.at[pl.ds(0, n - 1)], buf.at[pl.ds(0, n - 1)], sem).wait()

    def total_of(buf, n):
        parts = [buf[i] for i in range(n)]
        while len(parts) > 1:
            parts = [parts[i] + parts[i + 1] if i + 1 < len(parts) else parts[i] for i in range(0, len(parts), 2)]
        return parts[0]

    wait_red(red1, n1, red_sem.at[1])
    mom2[...] = total_of(red1, n1)
    red2[pl.ds(me2, 1)] = mom2[...][None]

    @pl.loop(1, n2)
    def _(j):
        send(mom2, red2.at[me2], red_sem.at[2], red_sem.at[3], peer2(j)).start()

    @pl.when(top)
    def _():
        pltpu.make_async_copy(fold_y.at[pl.ds(0, ny - 1)], fold_y.at[pl.ds(0, ny - 1)], fold_sem.at[5]).wait()
        start = (seam - 1 - gx * LANES - (LANES - 1) + 2 * ngx * LANES) % (ngx * LANES)
        blk, off = start // LANES, start % LANES
        after = (blk + 1) % ngx
        window = jnp.concatenate([fold_y[blk // nz, 0], fold_y[after // nz, 1]], axis=1)
        col = lax.broadcasted_iota(jnp.int32, (2 * LANES, LANES), 1)
        src = lax.broadcasted_iota(jnp.int32, (2 * LANES, LANES), 0)
        pick = (src == off + (LANES - 1) - col).astype(f32)
        got = lax.dot(window, pick, precision=lax.Precision.HIGHEST, preferred_element_type=f32)
        row = lax.broadcasted_iota(jnp.int32, (FOLD, LANES), 0)
        got_n[...] = jnp.where(row < levels, got, -got)

    fold_rows[...] = jnp.where((lane & 1) == 1, got_ew[1], got_ew[0])
    lane16 = lax.broadcasted_iota(jnp.int32, (16, LANES), 1)

    def level(k, carry):
        kf = k.astype(f32)
        cot[k, 7:8] = got_s[pl.ds(k, 1)]
        cot[k, 8 + ROWS:9 + ROWS] = got_n[pl.ds(k, 1)]
        qs[7:8] = got_s[pl.ds(levels + k, 1)]
        qn[8 + ROWS:9 + ROWS] = got_n[pl.ds(levels + k, 1)]
        for r in range(0, ROWS, 16):
            rows = slice(r, r + 16)
            vq, kq = 0.25 * v[k, rows], 0.5 * kap[k, rows]
            qn[8 + r:24 + r] = vq + kq
            qs[8 + r:24 + r] = vq - kq
        for r in range(0, ROWS, 16):
            rows, mid = slice(r, r + 16), slice(8 + r, 24 + r)
            ct = cot[k, mid]
            uq, kq = 0.25 * u[k, rows], 0.5 * kap[k, rows]
            qe, qw = uq + kq, uq - kq
            edge = fold_rows[rows]
            ec = roll_lanes(edge, (LANES - 1) - 2 * k)
            eq = roll_lanes(edge, 63 - 2 * k)
            c_e = roll_lanes(jnp.where(lane16 == 0, ec, ct), LANES - 1)
            c_w = roll_lanes(jnp.where(lane16 == LANES - 1, ec, ct), 1)
            q_e = roll_lanes(jnp.where(lane16 == 0, eq, qe), LANES - 1)
            q_w = roll_lanes(jnp.where(lane16 == LANES - 1, eq, qw), 1)
            c_n, c_s = cot[k, 9 + r:25 + r], cot[k, 7 + r:23 + r]
            ke = jnp.where(dmin[0, 0, mid] > kf, time_step * (qe + q_e), 0.0)
            kw = jnp.where(dmin[1, 0, mid] > kf, time_step * (qw + q_w), 0.0)
            kn = jnp.where(dmin[2, 0, mid] > kf, time_step * (qn[8 + r:24 + r] + qn[9 + r:25 + r]), 0.0)
            ks = jnp.where(dmin[3, 0, mid] > kf, time_step * (qs[8 + r:24 + r] + qs[7 + r:23 + r]), 0.0)
            coef_e[k, rows], coef_w[k, rows], coef_n[k, rows], coef_s[k, rows] = ke, kw, kn, ks
            base[k, rows] = ct + (ke * (c_e - ct) + kw * (ct - c_w)) + (kn * (c_n - ct) + ks * (ct - c_s))
        return carry

    lax.fori_loop(0, levels, level, 0)

    wait_red(red2, n2, red_sem.at[3])
    tot[...] = total_of(red2, n2)
    m = [jnp.broadcast_to(tot[j:j + 1], (8, LANES)) for j in range(6)]
    lo, hi = 0.0999, 8.2
    rho = m[1] / m[0]
    s1 = [m[j + 1] - rho * m[j] for j in range(5)]
    n = [s1[j + 1] - rho * s1[j] for j in range(4)]
    n[0] = jnp.maximum(n[0], 0.0)

    def bounded(t, least, most):
        return jnp.where(t >= least, jnp.minimum(t, most), least)

    e1 = n[0] / m[0]
    rho1 = bounded(n[1] / n[0], lo, hi)
    p1 = bounded(rho1 - e1 / rho, lo, hi)
    k0 = n[2] - rho1 * n[1] - e1 * n[0]
    k1 = n[3] - 2.0 * rho1 * n[2] + rho1 * rho1 * n[1] - 2.0 * e1 * rho * n[0] + e1 * e1 * m[1]
    e2 = bounded(k0 / n[0], 0.0, 70.0)
    rho2 = bounded(k1 / k0, lo, hi)
    p2 = bounded(rho2 - e2 / p1, lo, hi)
    z0 = 1.0 / rho
    z1 = -z0 / p1
    y2 = -z1 / p2
    y1 = z1 - e2 / p1 * y2
    y0 = z0 - e1 / rho * y1
    a0 = y0 - rho * y1 + (rho1 * rho - e1) * y2
    a1 = y1 - (rho + rho1) * y2

    def spread(a, rows):
        return jnp.broadcast_to(a[0:1], (rows, LANES))

    rows80 = [spread(a, 80) for a in (a0, a1, y2)]
    h_mid = rows80[0] * plane[0, body] + rows80[1] * vec1[0, body] + rows80[2] * vec2[0, body]
    h_side = rows80[0] * wide[0, body] + rows80[1] * vec1[1, body] + rows80[2] * vec2[1, body]
    hv[0, body] = h_mid
    inner_mid, inner_side = h_mid[8:8 + ROWS], h_side[8:8 + ROWS]
    h_e, h_w = neighbours(inner_mid, inner_side, ROWS)
    hv[1, inner] = h_e - inner_mid
    hv[2, inner] = inner_mid - h_w
    hv[3, inner] = hv[0, PAD + 1:PAD + 1 + ROWS] - inner_mid
    hv[4, inner] = inner_mid - hv[0, PAD - 1:PAD - 1 + ROWS]
    height = pltpu.make_async_copy(hv.at[0, inner], hadj_h, store_sem.at[0])
    height.start()
    stores = []
    for r in range(0, ROWS, 8):
        rows, mid = slice(r, r + 8), slice(PAD + r, PAD + r + 8)
        hc, de, dw, dn, ds_ = [hv[i, mid] for i in range(5)]
        wet = plane[1, mid]

        def finish(k, carry):
            grown = (
                jnp.where(wet > k.astype(f32), hc, 0.0)
                + (coef_e[k, rows] * de + coef_w[k, rows] * dw)
                + (coef_n[k, rows] * dn + coef_s[k, rows] * ds_)
            )
            outv[k, rows] = base[k, rows] + th_s[k] * grown
            return carry

        lax.fori_loop(0, levels, finish, 0, unroll=5)
        store = pltpu.make_async_copy(
            outv.at[:, pl.ds(r, 8)], out_h.at[:, pl.ds(r, 8)], store_sem.at[1 + r // 8]
        )
        store.start()
        stores.append(store)

    for halo in halos:
        halo.wait_send()
    for edge in edges:
        edge.wait_send()
    wait_red(red1, n1, red_sem.at[0])
    wait_red(red2, n2, red_sem.at[2])

    @pl.when(top)
    def _():
        pltpu.make_async_copy(all2.at[pl.ds(0, ngx - 1)], all2.at[pl.ds(0, ngx - 1)], fold_sem.at[0]).wait()
        pltpu.make_async_copy(foldz.at[pl.ds(0, nz - 1)], foldz.at[pl.ds(0, nz - 1)], fold_sem.at[2]).wait()
        pltpu.make_async_copy(fold_y.at[pl.ds(0, ny - 1)], fold_y.at[pl.ds(0, ny - 1)], fold_sem.at[4]).wait()

    height.wait()
    for store in stores:
        store.wait()


def solution(mesh):
    ngx, ngy = mesh.shape["gx"], mesh.shape["gy"]
    nc = 2
    nx = ngy // nc
    ny = 4 if ngx == 32 else 2
    nz = ngx // ny

    def local(cot, b, u, v, kap, th, dep, fp):
        levels = cot.shape[0]
        f32 = jnp.float32

        def vmem(*shape, dtype=f32):
            return pltpu.VMEM(shape, dtype)

        n1, n2 = nz * nc, nx * ny
        cube = (levels, ROWS, LANES)
        scratch = [
            vmem(levels, 80, LANES), vmem(*cube), vmem(*cube), vmem(*cube),
            vmem(ROWS, LANES, dtype=jnp.int32),
            vmem(2, 96, LANES), vmem(2, 96, LANES),
            vmem(ROWS, LANES), vmem(2, 80, LANES), vmem(4, 2, 80, LANES),
            vmem(2, 96, LANES), vmem(2, 96, LANES),
            vmem(ROWS, LANES), vmem(2, ROWS, LANES),
            vmem(FOLD, LANES), vmem(FOLD, LANES), vmem(FOLD, LANES), vmem(FOLD, LANES),
            vmem(8, LANES), vmem(ngx, 8, LANES),
            vmem(nz, FOLD, LANES), vmem(2, FOLD, LANES), vmem(ny, 2, FOLD, LANES),
            vmem(ROWS, LANES),
            vmem(80, LANES), vmem(80, LANES),
            vmem(*cube), vmem(*cube), vmem(*cube), vmem(*cube), vmem(*cube), vmem(*cube),
            vmem(5, 96, LANES),
            vmem(8, LANES), vmem(n1, 8, LANES), vmem(8, LANES), vmem(n2, 8, LANES), vmem(8, LANES),
            pltpu.SemaphoreType.DMA((6,)), pltpu.SemaphoreType.DMA((9,)),
            pltpu.SemaphoreType.DMA((12,)), pltpu.SemaphoreType.DMA((8,)),
            pltpu.SemaphoreType.DMA((4,)), pltpu.SemaphoreType.DMA((4,)),
            pltpu.SemaphoreType.DMA((6,)),
        ]
        hbm = pl.BlockSpec(memory_space=pl.ANY)
        smem = pl.BlockSpec(memory_space=pltpu.SMEM)
        return pl.pallas_call(
            functools.partial(kernel, nz, ny, nc, nx, levels),
            out_shape=(jax.ShapeDtypeStruct(cube, f32), jax.ShapeDtypeStruct((ROWS, LANES), f32)),
            in_specs=[hbm, hbm, hbm, hbm, hbm, smem, hbm, smem],
            out_specs=(hbm, hbm),
            scratch_shapes=scratch,
            compiler_params=pltpu.CompilerParams(
                collective_id=0, has_side_effects=True, vmem_limit_bytes=40 * 1024 * 1024
            ),
        )(cot, b, u, v, kap, th, dep, fp)

    in_specs = (
        P(None, "gy", "gx"), P("gy", "gx"), P(None, "gy", "gx"), P(None, "gy", "gx"),
        P(None, "gy", "gx"), P(), P("gy", "gx"), P("gx"),
    )
    out_specs = (P(None, "gy", "gx"), P("gy", "gx"))
    return jax.shard_map(local, mesh=mesh, in_specs=in_specs, out_specs=out_specs, check_vma=False)
```

```python
import functools

import jax
import jax.numpy as jnp
from jax import lax
from jax.experimental import pallas as pl
from jax.experimental.pallas import tpu as pltpu
from jax.sharding import PartitionSpec as P

MESH = pl.DeviceIdType.MESH
damping = 0.1
time_step = 0.3
ROWS = 64
LANES = 128
PAD = 16
FOLD = 56


def roll_lanes(x, shift):
    return pltpu.roll(x, shift, 1)


def two_sum(a, b):
    total = a + b
    t = total - a
    return total, (a - (total - t)) + (b - t)


def split(a):
    t = 4097.0 * a
    high = t - (t - a)
    return a, high, a - high


def two_product(a, b):
    (a, ah, al), (b, bh, bl) = a, b
    p = a * b
    return p, ((ah * bh - p) + ah * bl + al * bh) + al * bl


def pair_add(a, b):
    total, rest = two_sum(a[0], b[0])
    return total, rest + (a[1] + b[1])


def renormal(a):
    total = a[0] + a[1]
    return total, a[1] - (total - a[0])


def folded_rows(a):
    rows = a[0].shape[0]
    while rows > 8:
        keep = rows // 2 if rows % 16 == 0 else rows - 8
        rest = pair_add([t[:rows - keep] for t in a], [t[keep:] for t in a])
        a = [jnp.concatenate([t, o[rows - keep:keep]]) if 2 * keep > rows else t for t, o in zip(rest, a)]
        rows = keep
    for shift in (4, 2, 1):
        a = pair_add(a, [pltpu.roll(t, shift, 0) for t in a])
    return a


def kernel(
    nz, ny, nc, nx, levels,
    cot_h, b_h, u_h, v_h, k_h, dep_h, fp_h, faces_h, height_h,
    fp_s, cot, u, v, kap, dint, plane, wide, pack2, got2, dmin, vec1, vec2,
    edge_ew, got_ew, edge_n, edge_s, got_n, got_s,
    top2, all2, mir, foldz, fold_stage, fold_y, sides,
    qn, qs, faces, hv,
    mom, red1, mom2, red2, band, tot,
    load_sem, store_sem, send_sem, halo_sem, edge_sem, red_sem, fold_sem, band_sem,
):
    gx, gy = lax.axis_index("gx"), lax.axis_index("gy")
    ngx, ngy = ny * nz, nx * nc
    y, z, x, c = gx // nz, gx % nz, gy // nc, gy % nc
    top = gy == ngy - 1
    lane = lax.broadcasted_iota(jnp.int32, (ROWS, LANES), 1)
    lane80 = lax.broadcasted_iota(jnp.int32, (80, LANES), 1)
    f32 = jnp.float32

    def at(dx, dy):
        return (gx + dx + ngx) % ngx, (gy + dy + ngy) % ngy

    compass = [(1, 0), (-1, 0), (0, 1), (0, -1), (1, 1), (-1, 1), (1, -1), (-1, -1)]

    loads = [
        pltpu.make_async_copy(b_h, plane.at[0, pl.ds(PAD, ROWS)], load_sem.at[0]),
        pltpu.make_async_copy(dep_h, dint, load_sem.at[1]),
        pltpu.make_async_copy(cot_h, cot.at[:, pl.ds(8, ROWS)], load_sem.at[2]),
        pltpu.make_async_copy(u_h, u, load_sem.at[3]),
        pltpu.make_async_copy(k_h, kap, load_sem.at[4]),
        pltpu.make_async_copy(v_h, v, load_sem.at[5]),
        pltpu.make_async_copy(fp_h, fp_s, load_sem.at[6]),
    ]
    for load in loads:
        load.start()

    barrier = pltpu.get_barrier_semaphore()

    def greet(device):
        pl.semaphore_signal(barrier, inc=1, device_id=device, device_id_type=MESH)

    def far_first(n):
        return sorted(range(n), key=lambda d: (-min(d, n - d), d))

    far_y = [((y + d) % ny) * nz for d in far_first(ny)]
    n1, n2 = nz * nc, nx * ny
    me1, me2 = z * nc + c, y * nx + x
    far_z = [(z + d) % nz for d in far_first(nz)]
    far_yx = sorted(
        [(d, e) for d in range(ny) for e in range(nx)],
        key=lambda t: -min(t[0], ny - t[0]) - min(t[1], nx - t[1]),
    )

    def group1(act):
        for d, pz in zip(far_first(nz), far_z):
            for e in range(nc - 1, -1, -1):
                if (d, e) != (0, 0):
                    act((y * nz + pz, x * nc + (c + e) % nc))

    def group2(act):
        for d, e in far_yx:
            if (d, e) != (0, 0):
                act(((y + d) % ny * nz + z, (x + e) % nx * nc + c))

    def everyone_on_top(act):
        for pz in far_z[:-1]:
            for py in far_y:
                act((py + pz, gy))
        for py in far_y[:-1]:
            act((py + z, gy))

    for d in compass:
        greet(at(*d))
    group1(greet)
    group2(greet)

    @pl.when(top)
    def _():
        everyone_on_top(greet)

    @pl.when(gy != ngy - 1)
    def _():
        greet((gx, ngy - 1))

    zero8 = jnp.zeros((8, LANES), f32)
    for part, n in ((red1, n1), (red2, n2 + 1)):
        if n < part.shape[0]:
            part[n:] = jnp.zeros((part.shape[0] - n, LANES), f32)
    for f in range(2):
        for part in (plane, wide, vec1, vec2):
            part[f, 0:8] = zero8
            part[f, 88:96] = zero8
    loads[0].wait()
    loads[1].wait()
    depth_f = dint[...].astype(f32)
    plane[1, PAD:PAD + ROWS] = depth_f
    pack2[...] = jnp.where(
        (lane < 32) | (lane >= 96), plane[0, PAD:PAD + ROWS], roll_lanes(depth_f, 64)
    )

    pl.semaphore_wait(barrier, 8 + n1 - 1 + n2 - 1 + jnp.where(top, ngx - 1 + ngy - 1, 0))

    def send(src, dst, sem_out, sem_in, device):
        copy = pltpu.make_async_remote_copy(
            src_ref=src, dst_ref=dst, send_sem=sem_out, recv_sem=sem_in,
            device_id=device, device_id_type=MESH,
        )
        return copy

    first, last = pl.ds(PAD, 8), pl.ds(PAD + ROWS - 8, 8)
    south, north = pl.ds(PAD - 8, 8), pl.ds(PAD + ROWS, 8)
    halos = []
    for i, (dx, dy) in enumerate(compass):
        if dx == 0:
            src = plane.at[:, last if dy == 1 else first]
            dst = plane.at[:, south if dy == 1 else north]
        else:
            side = 0 if dx == 1 else 1
            if dy == 0:
                src, dst = pack2, got2.at[side, pl.ds(8, ROWS)]
            elif dy == 1:
                src, dst = pack2.at[pl.ds(ROWS - 8, 8)], got2.at[side, pl.ds(0, 8)]
            else:
                src, dst = pack2.at[pl.ds(0, 8)], got2.at[side, pl.ds(ROWS + 8, 8)]
        halos.append(send(src, dst, send_sem.at[i], halo_sem.at[i], at(dx, dy)))

    @pl.when(top)
    def _():
        top2[0:8] = plane[0, last]
        top2[8:16] = plane[1, last]
        mine = pl.ds(pl.multiple_of(gx * 16, 16), 16)
        all2[mine] = top2[...]
        everyone_on_top(lambda d: send(top2, all2.at[mine], fold_sem.at[0], fold_sem.at[1], d).start())

    for halo in halos:
        halo.start()

    for load in loads[2:6]:
        load.wait()
    half = jnp.where(lane < 64, 0.5, -0.5).astype(f32)
    edge_n[2 * levels:FOLD] = jnp.zeros((FOLD - 2 * levels, LANES), f32)
    edge_s[2 * levels:FOLD] = jnp.zeros((FOLD - 2 * levels, LANES), f32)

    def pack_level(k, acc):
        face = 0.25 * u[k] + half * kap[k]
        place = lane >> 1
        acc = jnp.where(place == k, roll_lanes(cot[k, 8:8 + ROWS], 2 * k + 1), acc)
        acc = jnp.where(place == k + 32, roll_lanes(face, 2 * k + 65), acc)
        edge_n[pl.ds(k, 1)] = cot[k, 7 + ROWS:8 + ROWS]
        edge_s[pl.ds(k, 1)] = cot[k, 8:9]
        edge_n[pl.ds(levels + k, 1)] = 0.25 * v[k, ROWS - 1:ROWS] - 0.5 * kap[k, ROWS - 1:ROWS]
        edge_s[pl.ds(levels + k, 1)] = 0.25 * v[k, 0:1] + 0.5 * kap[k, 0:1]
        return acc

    edge_ew[...] = lax.fori_loop(0, levels, pack_level, jnp.zeros((ROWS, LANES), f32))
    edges = [
        send(edge_ew, got_ew.at[0], send_sem.at[8], edge_sem.at[0], at(1, 0)),
        send(edge_ew, got_ew.at[1], send_sem.at[9], edge_sem.at[1], at(-1, 0)),
        send(edge_n, got_s, send_sem.at[10], edge_sem.at[2], at(0, 1)),
        send(edge_s, got_n, send_sem.at[11], edge_sem.at[3], at(0, -1)),
    ]
    for edge in edges:
        edge.start()

    @pl.when(top)
    def _():
        foldz[pl.ds(z, 1)] = edge_n[...][None]

        @pl.loop(1, nz)
        def _(j):
            p = y * nz + (z + j) % nz
            send(edge_n, foldz.at[z], fold_sem.at[2], fold_sem.at[3], (p, gy)).start()

    for halo in halos:
        halo.wait_recv()
    hw, he = got2[0], got2[1]
    wide[0, 8:88] = jnp.where(lane80 < 64, he, hw)
    wide[1, 8:88] = roll_lanes(jnp.where(lane80 < 64, hw, he), 64)

    loads[6].wait()
    seam = fp_s[0] + gx * LANES + 1

    @pl.when(gy == 0)
    def _():
        plane[1, 8:16] = zero8
        wide[1, 8:16] = zero8

    first_lane, last_lane = lane80 == 0, lane80 == LANES - 1

    def neighbours(mid, beside, rows):
        return [
            jnp.where(last_lane[:rows], roll_lanes(beside, LANES - 1), roll_lanes(mid, LANES - 1)),
            jnp.where(first_lane[:rows], roll_lanes(beside, 1), roll_lanes(mid, 1)),
        ]

    def both(mid, beside):
        return neighbours(mid, beside, 80), neighbours(beside, mid, 80)

    body, up, down = pl.ds(8, 80), pl.ds(9, 80), pl.ds(7, 80)

    def least_depths():
        dm, db = plane[1, body], wide[1, body]
        (d_e, d_w), (db_e, db_w) = both(dm, db)
        for i, (a, o) in enumerate(
            [(d_e, db_e), (d_w, db_w), (plane[1, up], wide[1, up]), (plane[1, down], wide[1, down])]
        ):
            dmin[i, 0] = jnp.minimum(dm, a)
            dmin[i, 1] = jnp.minimum(db, o)

    def apply(mid_ref, beside_ref, out_ref):
        mid, beside = mid_ref[body], beside_ref[body]
        (m_e, m_w), (s_e, s_w) = both(mid, beside)
        for i, (centre, nbrs) in enumerate(
            [
                (mid, (m_e, m_w, mid_ref[up], mid_ref[down])),
                (beside, (s_e, s_w, beside_ref[up], beside_ref[down])),
            ]
        ):
            total = jnp.zeros_like(centre)
            for j in range(4):
                total = total + dmin[j, i] * (centre - nbrs[j])
            out_ref[i, body] = damping * centre + (1.0 / levels) * total

    least_depths()
    apply(plane.at[0], wide.at[0], vec1)
    apply(vec1.at[0], vec1.at[1], vec2)
    inner = pl.ds(PAD, ROWS)
    mid2 = vec2[0, inner]
    m_e, m_w = neighbours(mid2, vec2[1, inner], ROWS)
    nbrs = (m_e, m_w, vec2[0, PAD + 1:PAD + 1 + ROWS], vec2[0, PAD - 1:PAD - 1 + ROWS])
    mid3 = jnp.zeros_like(mid2)
    for j in range(4):
        mid3 = mid3 + dmin[j, 0, 8:8 + ROWS] * (mid2 - nbrs[j])
    mid3 = damping * mid2 + (1.0 / levels) * mid3
    mid0, mid1 = plane[0, inner], vec1[0, inner]

    sub8 = lax.broadcasted_iota(jnp.int32, (8, LANES), 0)
    lane8 = lax.broadcasted_iota(jnp.int32, (8, LANES), 1)

    def moment_row(fields):
        f0, f1, f2, f3 = [split(f) for f in fields]
        for j, (a, o) in enumerate([(f0, f0), (f0, f1), (f1, f1), (f1, f2), (f2, f2), (f2, f3)]):
            high, low = folded_rows(two_product(a, o))
            tot[j:j + 1] = high[0:1]
            tot[8 + j:9 + j] = low[0:1]
        tot[6:8] = jnp.zeros((2, LANES), f32)
        tot[14:16] = jnp.zeros((2, LANES), f32)
        high, low = tot[0:8], tot[8:16]
        scale = 256.0 * jnp.max(jnp.abs(high), axis=1, keepdims=True)
        coarse = (high + scale) - scale
        rest = jnp.sum((high - coarse) + low, axis=1, keepdims=True)
        high, low = renormal((jnp.sum(coarse, axis=1, keepdims=True), rest))
        row = jnp.where(lane8 == sub8, high, 0.0) + jnp.where(lane8 == sub8 + 8, low, 0.0)
        return jnp.sum(row, axis=0, keepdims=True)

    apart = top & (lax.broadcasted_iota(jnp.int32, (ROWS, LANES), 0) >= ROWS - 3)
    mom[...] = moment_row([jnp.where(apart, 0.0, f) for f in (mid0, mid1, mid2, mid3)])

    red1[pl.ds(me1, 1)] = mom[...]
    group1(lambda d: send(mom, red1.at[pl.ds(me1, 1)], red_sem.at[0], red_sem.at[1], d).start())

    for edge in edges:
        edge.wait_recv()

    @pl.when(top)
    def _():
        dmin[2, 0, 7 + ROWS:8 + ROWS] = jnp.zeros((1, LANES), f32)

    sides[...] = jnp.where((lane & 1) == 1, got_ew[1], got_ew[0])
    lane16 = lax.broadcasted_iota(jnp.int32, (16, LANES), 1)

    def level(k, carry):
        kf = k.astype(f32)
        cot[k, 7:8] = got_s[pl.ds(k, 1)]
        cot[k, 8 + ROWS:9 + ROWS] = got_n[pl.ds(k, 1)]
        qs[7:8] = got_s[pl.ds(levels + k, 1)]
        qn[8 + ROWS:9 + ROWS] = got_n[pl.ds(levels + k, 1)]
        for r in range(0, ROWS, 16):
            rows = slice(r, r + 16)
            vq, kq = 0.25 * v[k, rows], 0.5 * kap[k, rows]
            qn[8 + r:24 + r] = vq + kq
            qs[8 + r:24 + r] = vq - kq
        for r in range(0, ROWS, 16):
            rows, mid = slice(r, r + 16), slice(8 + r, 24 + r)
            ct = cot[k, mid]
            uq, kq = 0.25 * u[k, rows], 0.5 * kap[k, rows]
            qe, qw = uq + kq, uq - kq
            edge = sides[rows]
            ec = roll_lanes(edge, (LANES - 1) - 2 * k)
            eq = roll_lanes(edge, 63 - 2 * k)
            c_e = roll_lanes(jnp.where(lane16 == 0, ec, ct), LANES - 1)
            c_w = roll_lanes(jnp.where(lane16 == LANES - 1, ec, ct), 1)
            q_e = roll_lanes(jnp.where(lane16 == 0, eq, qe), LANES - 1)
            q_w = roll_lanes(jnp.where(lane16 == LANES - 1, eq, qw), 1)
            c_n, c_s = cot[k, 9 + r:25 + r], cot[k, 7 + r:23 + r]
            ke = jnp.where(dmin[0, 0, mid] > kf, time_step * (qe + q_e), 0.0)
            kw = jnp.where(dmin[1, 0, mid] > kf, time_step * (qw + q_w), 0.0)
            kn = jnp.where(dmin[2, 0, mid] > kf, time_step * (qn[8 + r:24 + r] + qn[9 + r:25 + r]), 0.0)
            ks = jnp.where(dmin[3, 0, mid] > kf, time_step * (qs[8 + r:24 + r] + qs[7 + r:23 + r]), 0.0)
            for i, face in enumerate((ke, kw, kn, ks)):
                faces[k, 1 + i, rows] = face
            faces[k, 0, rows] = ct + (ke * (c_e - ct) + kw * (ct - c_w)) + (kn * (c_n - ct) + ks * (ct - c_s))
        return carry

    lax.fori_loop(0, levels, level, 0)

    def wait_red(buf, n, sem):
        pltpu.make_async_copy(buf.at[pl.ds(0, n - 1)], buf.at[pl.ds(0, n - 1)], sem).wait()

    wait_red(red1, n1, red_sem.at[1])
    sums = red1[...]
    sums, rest = folded_rows((sums, jnp.zeros_like(sums)))
    mom2[...] = (sums + roll_lanes(rest, 8))[0:1]
    red2[pl.ds(me2, 1)] = mom2[...]
    group2(lambda d: send(mom2, red2.at[pl.ds(me2, 1)], red_sem.at[2], red_sem.at[3], d).start())

    below = sorted(range(ngy - 1), key=lambda g: -min(nx - 1 - g // nc, g // nc + 1))

    @pl.when(top)
    def _():
        pltpu.make_async_copy(foldz.at[pl.ds(0, nz - 1)], foldz.at[pl.ds(0, nz - 1)], fold_sem.at[3]).wait()
        whole = ngx * LANES
        start = (seam - LANES - gx * LANES + 2 * whole) % whole
        blk, off = start // LANES, start % LANES
        after = (blk + 1) % ngx
        fold_stage[0] = foldz[blk % nz]
        fold_stage[1] = foldz[after % nz]
        fold_y[pl.ds(y, 1)] = fold_stage[...][None]

        @pl.loop(1, ny)
        def _(j):
            p = ((y + j) % ny) * nz + z
            send(fold_stage, fold_y.at[y], fold_sem.at[4], fold_sem.at[5], (p, gy)).start()

        others = all2.at[pl.ds(0, (ngx - 1) * 16)]
        pltpu.make_async_copy(others, others, fold_sem.at[1]).wait()

        def exact_dot(a, o):
            return lax.dot(a, o, precision=lax.Precision.HIGHEST, preferred_element_type=f32)

        col = lax.broadcasted_iota(jnp.int32, (2 * LANES, LANES), 1)
        src = lax.broadcasted_iota(jnp.int32, (2 * LANES, LANES), 0)
        pick = (src == off + (LANES - 1) - col).astype(f32)
        block = lax.broadcasted_iota(jnp.int32, (ngx, ngx), 0)
        source = lax.broadcasted_iota(jnp.int32, (ngx, ngx), 1)
        order = ((block + source - blk - gx + 2 * ngx) % ngx == 0).astype(f32)
        fields = [[all2[pl.ds(8 * f + q, ngx, stride=16)] for q in range(2, 8)] for f in range(2)]
        mirror = [fields[f][q] for f in range(2) for q in (5, 4, 3)]
        turned = exact_dot(order, jnp.concatenate(mirror, axis=1))
        turned = [turned[:, i * LANES:(i + 1) * LANES] for i in range(6)]
        turned = [jnp.concatenate([t, pltpu.roll(t, 1, 0)], axis=1) for t in turned]
        mir[...] = exact_dot(jnp.concatenate(turned, axis=0), pick)
        mirror = [mir[i * ngx:(i + 1) * ngx] for i in range(6)]
        values, depth = fields[0] + mirror[:3], fields[1] + mirror[3:]
        spot = lax.broadcasted_iota(jnp.int32, (ngx, LANES), 1)

        def beside(t):
            ahead, behind = roll_lanes(t, LANES - 1), roll_lanes(t, 1)
            return (
                jnp.where(spot == LANES - 1, pltpu.roll(ahead, ngx - 1, 0), ahead),
                jnp.where(spot == 0, pltpu.roll(behind, 1, 0), behind),
            )

        least = {
            i: [jnp.minimum(depth[i], t) for t in (*beside(depth[i]), depth[i + 1], depth[i - 1])]
            for i in range(1, 8)
        }

        def step(f, rows):
            out = {}
            for i in rows:
                total = jnp.zeros_like(f[i])
                for d, t in zip(least[i], (*beside(f[i]), f[i + 1], f[i - 1])):
                    total = total + d * (f[i] - t)
                out[i] = damping * f[i] + (1.0 / levels) * total
            return out

        band1 = step(values, range(1, 8))
        band2 = step(band1, range(2, 7))
        band3 = step(band2, range(3, 6))
        band[...] = moment_row(
            [jnp.concatenate([f[i] for i in (3, 4, 5)], axis=0) for f in (values, band1, band2, band3)]
        )
        red2[n2:n2 + 1] = band[...]
        for g in below:
            send(band, red2.at[pl.ds(n2, 1)], band_sem.at[0], band_sem.at[1], (gx, g)).start()

        for i in range(6):
            f, row = i // 3, PAD + ROWS + i % 3
            mine, ahead, behind = [mir[pl.ds(i * ngx + (gx + d) % ngx, 1)] for d in (0, 1, ngx - 1)]
            plane[f, row:row + 1] = mine
            wide[f, row:row + 1] = jnp.where(lane8[0:1] < 64, ahead, behind)
        least_depths()
        apply(plane.at[0], wide.at[0], vec1)
        apply(vec1.at[0], vec1.at[1], vec2)

        pltpu.make_async_copy(fold_y.at[pl.ds(0, ny - 1)], fold_y.at[pl.ds(0, ny - 1)], fold_sem.at[5]).wait()
        got_n[...] = exact_dot(jnp.concatenate([fold_y[blk // nz, 0], fold_y[after // nz, 1]], axis=1), pick)
        here = slice(ROWS - 1, ROWS)

        def across(k, carry):
            ct = cot[k, 7 + ROWS:8 + ROWS]
            half = 0.25 * v[k, here] + 0.5 * kap[k, here] - got_n[pl.ds(levels + k, 1)]
            kn = jnp.where(dmin[2, 0, 7 + ROWS:8 + ROWS] > k.astype(f32), time_step * half, 0.0)
            faces[k, 3, here] = kn
            faces[k, 0, here] += kn * (got_n[pl.ds(k, 1)] - ct)
            return carry

        lax.fori_loop(0, levels, across, 0)

    store = pltpu.make_async_copy(faces, faces_h, store_sem.at[0])
    store.start()

    wait_red(red2, n2, red_sem.at[3])

    @pl.when(gy != ngy - 1)
    def _():
        one = red2.at[pl.ds(n2, 1)]
        pltpu.make_async_copy(one, one, band_sem.at[1]).wait()

    sums = red2[...]
    sums, rest = folded_rows((sums, jnp.zeros_like(sums)))
    rest = rest + pltpu.roll(sums, LANES - 8, 1)
    parts = []
    for part in (sums, rest):
        part = jnp.sum(jnp.where(lane8 == sub8, part, 0.0), axis=1, keepdims=True)
        parts.append(jnp.broadcast_to(part, (8, LANES)))
    tot[0:8], tot[8:16] = renormal(parts)
    pairs = [[jnp.broadcast_to(tot[i:i + 1], (8, LANES)) for i in (j, 8 + j)] for j in range(6)]
    m = [high for high, low in pairs]
    lo, hi = 0.0999, 8.2
    rho = m[1] / m[0]
    rho_parts = split(rho)

    def centred(a, o):
        p, rest = two_product(rho_parts, split(o[0]))
        return renormal(pair_add(a, (-p, -(rest + rho * o[1]))))

    s1 = [centred(pairs[j + 1], pairs[j]) for j in range(5)]
    n = [centred(s1[j + 1], s1[j])[0] for j in range(4)]
    n[0] = jnp.maximum(n[0], 0.0)

    def bounded(t, least, most):
        return jnp.where(t >= least, jnp.minimum(t, most), least)

    e1 = n[0] / m[0]
    rho1 = bounded(n[1] / n[0], lo, hi)
    p1 = bounded(rho1 - e1 / rho, lo, hi)
    k0 = n[2] - rho1 * n[1] - e1 * n[0]
    k1 = n[3] - 2.0 * rho1 * n[2] + rho1 * rho1 * n[1] - 2.0 * e1 * rho * n[0] + e1 * e1 * m[1]
    e2 = bounded(k0 / n[0], 0.0, 70.0)
    rho2 = bounded(k1 / k0, lo, hi)
    p2 = bounded(rho2 - e2 / p1, lo, hi)
    z0 = 1.0 / rho
    z1 = -z0 / p1
    y2 = -z1 / p2
    y1 = z1 - e2 / p1 * y2
    y0 = z0 - e1 / rho * y1
    a0 = y0 - rho * y1 + (rho1 * rho - e1) * y2
    a1 = y1 - (rho + rho1) * y2

    def spread(a, rows):
        return jnp.broadcast_to(a[0:1], (rows, LANES))

    rows80 = [spread(a, 80) for a in (a0, a1, y2)]
    h_mid = rows80[0] * plane[0, body] + rows80[1] * vec1[0, body] + rows80[2] * vec2[0, body]
    h_side = rows80[0] * wide[0, body] + rows80[1] * vec1[1, body] + rows80[2] * vec2[1, body]
    hv[0, body] = h_mid
    inner_mid, inner_side = h_mid[8:8 + ROWS], h_side[8:8 + ROWS]
    h_e, h_w = neighbours(inner_mid, inner_side, ROWS)
    hv[1, inner] = h_e - inner_mid
    hv[2, inner] = inner_mid - h_w
    hv[3, inner] = hv[0, PAD + 1:PAD + 1 + ROWS] - inner_mid
    hv[4, inner] = inner_mid - hv[0, PAD - 1:PAD - 1 + ROWS]
    hv[5, inner] = plane[1, inner]
    height = pltpu.make_async_copy(hv.at[:, inner], height_h, store_sem.at[1])
    height.start()

    for halo in halos:
        halo.wait_send()
    for edge in edges:
        edge.wait_send()
    wait_red(red1, n1, red_sem.at[0])
    wait_red(red2, n2, red_sem.at[2])

    @pl.when(top)
    def _():
        others = all2.at[pl.ds(0, (ngx - 1) * 16)]
        pltpu.make_async_copy(others, others, fold_sem.at[0]).wait()
        some = red2.at[pl.ds(0, ngy - 1)]
        pltpu.make_async_copy(some, some, band_sem.at[0]).wait()
        pltpu.make_async_copy(foldz.at[pl.ds(0, nz - 1)], foldz.at[pl.ds(0, nz - 1)], fold_sem.at[2]).wait()
        pltpu.make_async_copy(fold_y.at[pl.ds(0, ny - 1)], fold_y.at[pl.ds(0, ny - 1)], fold_sem.at[4]).wait()

    height.wait()
    store.wait()


def finish(levels, group, faces_h, height_h, th_h, out_h, hadj_h, th, faces, height, out, sem):
    parts = [pl.ds(k, group) for k in range(0, levels, group)]
    first = [
        pltpu.make_async_copy(height_h, height, sem.at[0]),
        pltpu.make_async_copy(th_h, th, sem.at[1]),
    ]
    loads = [
        pltpu.make_async_copy(faces_h.at[p], faces.at[p], sem.at[2 + i]) for i, p in enumerate(parts)
    ]
    for load in first + loads:
        load.start()
    first[0].wait()
    stores = [pltpu.make_async_copy(height.at[0], hadj_h, sem.at[0])]
    stores[0].start()
    first[1].wait()
    for i, p in enumerate(parts):
        loads[i].wait()
        for r in range(0, ROWS, 8):
            rows = slice(r, r + 8)
            hc, de, dw, dn, ds_, wet = [height[j, rows] for j in range(6)]
            for k in range(i * group, (i + 1) * group):
                grown = (
                    jnp.where(wet > float(k), hc, 0.0)
                    + (faces[k, 1, rows] * de + faces[k, 2, rows] * dw)
                    + (faces[k, 3, rows] * dn + faces[k, 4, rows] * ds_)
                )
                out[k, rows] = faces[k, 0, rows] + th[k] * grown
        stores.append(pltpu.make_async_copy(out.at[p], out_h.at[p], sem.at[2 + i]))
        stores[-1].start()
    for store in stores:
        store.wait()


def solution(mesh):
    ngx, ngy = mesh.shape["gx"], mesh.shape["gy"]
    nc = 2
    nx = ngy // nc
    ny = 4 if ngx == 32 else 2
    nz = ngx // ny

    def local(cot, b, u, v, kap, th, dep, fp):
        levels = cot.shape[0]
        f32 = jnp.float32

        def vmem(*shape, dtype=f32):
            return pltpu.VMEM(shape, dtype)

        cube = (levels, ROWS, LANES)
        scratch = [
            pltpu.SMEM((LANES,), jnp.int32),
            vmem(levels, 80, LANES), vmem(*cube), vmem(*cube), vmem(*cube),
            vmem(ROWS, LANES, dtype=jnp.int32),
            vmem(2, 96, LANES), vmem(2, 96, LANES),
            vmem(ROWS, LANES), vmem(2, 80, LANES), vmem(4, 2, 80, LANES),
            vmem(2, 96, LANES), vmem(2, 96, LANES),
            vmem(ROWS, LANES), vmem(2, ROWS, LANES),
            vmem(FOLD, LANES), vmem(FOLD, LANES), vmem(FOLD, LANES), vmem(FOLD, LANES),
            vmem(16, LANES), vmem(ngx * 16, LANES), vmem(ngx * 6, LANES),
            vmem(nz, FOLD, LANES), vmem(2, FOLD, LANES), vmem(ny, 2, FOLD, LANES),
            vmem(ROWS, LANES),
            vmem(80, LANES), vmem(80, LANES),
            vmem(levels, 5, ROWS, LANES), vmem(6, 96, LANES),
            vmem(1, LANES), vmem(max(8, nz * nc), LANES), vmem(1, LANES), vmem(8 if nx * ny < 8 else 32, LANES), vmem(1, LANES), vmem(16, LANES),
            pltpu.SemaphoreType.DMA((7,)), pltpu.SemaphoreType.DMA((2,)),
            pltpu.SemaphoreType.DMA((12,)), pltpu.SemaphoreType.DMA((8,)),
            pltpu.SemaphoreType.DMA((4,)), pltpu.SemaphoreType.DMA((4,)),
            pltpu.SemaphoreType.DMA((6,)), pltpu.SemaphoreType.DMA((2,)),
        ]
        hbm = pl.BlockSpec(memory_space=pltpu.HBM)
        limit = 62 * 1024 * 1024
        faces, height = pl.pallas_call(
            functools.partial(kernel, nz, ny, nc, nx, levels),
            out_shape=(
                jax.ShapeDtypeStruct((levels, 5, ROWS, LANES), f32),
                jax.ShapeDtypeStruct((6, ROWS, LANES), f32),
            ),
            in_specs=[hbm] * 7,
            out_specs=(hbm, hbm),
            scratch_shapes=scratch,
            compiler_params=pltpu.CompilerParams(
                collective_id=0, has_side_effects=True, vmem_limit_bytes=limit
            ),
        )(cot, b, u, v, kap, dep, fp)
        group = 5 if levels % 5 == 0 else 1
        return pl.pallas_call(
            functools.partial(finish, levels, group),
            out_shape=(jax.ShapeDtypeStruct(cube, f32), jax.ShapeDtypeStruct((ROWS, LANES), f32)),
            in_specs=[hbm] * 3,
            out_specs=(hbm, hbm),
            scratch_shapes=[
                pltpu.SMEM((levels,), f32), vmem(levels, 5, ROWS, LANES), vmem(6, ROWS, LANES), vmem(*cube),
                pltpu.SemaphoreType.DMA((2 + levels // group,)),
            ],
            compiler_params=pltpu.CompilerParams(vmem_limit_bytes=limit),
        )(faces, height, th)

    in_specs = (
        P(None, "gy", "gx"), P("gy", "gx"), P(None, "gy", "gx"), P(None, "gy", "gx"),
        P(None, "gy", "gx"), P(), P("gy", "gx"), P("gx"),
    )
    out_specs = (P(None, "gy", "gx"), P("gy", "gx"))
    return jax.shard_map(local, mesh=mesh, in_specs=in_specs, out_specs=out_specs, check_vma=False)
```

```python
import functools

import jax
import jax.numpy as jnp
from jax import lax
from jax.experimental import pallas as pl
from jax.experimental.pallas import tpu as pltpu
from jax.sharding import PartitionSpec as P

MESH = pl.DeviceIdType.MESH
damping = 0.1
time_step = 0.3
ROWS = 64
LANES = 128
PAD = 16
FOLD = 56


def roll_lanes(x, shift):
    return pltpu.roll(x, shift, 1)


def two_sum(a, b):
    total = a + b
    t = total - a
    return total, (a - (total - t)) + (b - t)


def split(a):
    t = 4097.0 * a
    high = t - (t - a)
    return a, high, a - high


def two_product(a, b):
    (a, ah, al), (b, bh, bl) = a, b
    p = a * b
    return p, ((ah * bh - p) + ah * bl + al * bh) + al * bl


def pair_add(a, b):
    total, rest = two_sum(a[0], b[0])
    return total, rest + (a[1] + b[1])


def renormal(a):
    total = a[0] + a[1]
    return total, a[1] - (total - a[0])


def folded_rows(a):
    rows = a[0].shape[0]
    while rows > 8:
        keep = rows // 2 if rows % 16 == 0 else rows - 8
        rest = pair_add([t[:rows - keep] for t in a], [t[keep:] for t in a])
        a = [jnp.concatenate([t, o[rows - keep:keep]]) if 2 * keep > rows else t for t, o in zip(rest, a)]
        rows = keep
    for shift in (4, 2, 1):
        a = pair_add(a, [pltpu.roll(t, shift, 0) for t in a])
    return a


def kernel(
    nz, ny, nc, nx, levels,
    cot_h, b_h, u_h, v_h, k_h, dep_h, fp_h, faces_h, height_h,
    fp_s, cot, u, v, kap, dint, plane, wide, pack2, got2, dmin, vec1, vec2,
    edge_ew, got_ew, edge_n, edge_s, got_n, got_s,
    top2, all2, mir, foldz, fold_stage, fold_y, sides,
    qn, qs, faces, hv,
    mom, red1, mom2, red2, band, tot,
    load_sem, store_sem, send_sem, halo_sem, edge_sem, red_sem, fold_sem, band_sem, ready_sem,
):
    gx, gy = lax.axis_index("gx"), lax.axis_index("gy")
    ngx, ngy = ny * nz, nx * nc
    y, z, x, c = gx // nz, gx % nz, gy // nc, gy % nc
    top = gy == ngy - 1
    lane = lax.broadcasted_iota(jnp.int32, (ROWS, LANES), 1)
    lane80 = lax.broadcasted_iota(jnp.int32, (80, LANES), 1)
    f32 = jnp.float32

    def at(dx, dy):
        return (gx + dx + ngx) % ngx, (gy + dy + ngy) % ngy

    compass = [(1, 0), (-1, 0), (0, 1), (0, -1), (1, 1), (-1, 1), (1, -1), (-1, -1)]

    loads = [
        pltpu.make_async_copy(b_h, plane.at[0, pl.ds(PAD, ROWS)], load_sem.at[0]),
        pltpu.make_async_copy(dep_h, dint, load_sem.at[1]),
        pltpu.make_async_copy(cot_h, cot.at[:, pl.ds(8, ROWS)], load_sem.at[2]),
        pltpu.make_async_copy(u_h, u, load_sem.at[3]),
        pltpu.make_async_copy(k_h, kap, load_sem.at[4]),
        pltpu.make_async_copy(v_h, v, load_sem.at[5]),
        pltpu.make_async_copy(fp_h, fp_s, load_sem.at[6]),
    ]
    for load in loads:
        load.start()

    barrier = pltpu.get_barrier_semaphore()

    def greet(device):
        pl.semaphore_signal(barrier, inc=1, device_id=device, device_id_type=MESH)

    def far_first(n):
        return sorted(range(n), key=lambda d: (-min(d, n - d), d))

    far_y = [((y + d) % ny) * nz for d in far_first(ny)]
    def ready(device):
        pl.semaphore_signal(ready_sem, inc=1, device_id=device, device_id_type=MESH)

    n1, n2 = nz * nc, nx * ny
    me1, me2 = z * nc + c, y * nx + x
    far_z = [(z + d) % nz for d in far_first(nz)]
    far_yx = sorted(
        [(d, e) for d in range(ny) for e in range(nx)],
        key=lambda t: -min(t[0], ny - t[0]) - min(t[1], nx - t[1]),
    )

    def group1(act):
        for d, pz in zip(far_first(nz), far_z):
            for e in range(nc - 1, -1, -1):
                if (d, e) != (0, 0):
                    act((y * nz + pz, x * nc + (c + e) % nc))

    def group2(act):
        for d, e in far_yx:
            if (d, e) != (0, 0):
                act(((y + d) % ny * nz + z, (x + e) % nx * nc + c))

    def everyone_on_top(act):
        for pz in far_z[:-1]:
            for py in far_y:
                act((py + pz, gy))
        for py in far_y[:-1]:
            act((py + z, gy))

    for d in compass:
        greet(at(*d))
    group1(greet)
    group2(greet)

    zero8 = jnp.zeros((8, LANES), f32)
    for part, n in ((red1, n1), (red2, n2 + 1)):
        if n < part.shape[0]:
            part[n:] = jnp.zeros((part.shape[0] - n, LANES), f32)
    for f in range(2):
        for part in (plane, wide, vec1, vec2):
            part[f, 0:8] = zero8
            part[f, 88:96] = zero8
    loads[0].wait()
    loads[1].wait()
    depth_f = dint[...].astype(f32)
    plane[1, PAD:PAD + ROWS] = depth_f
    pack2[...] = jnp.where(
        (lane < 32) | (lane >= 96), plane[0, PAD:PAD + ROWS], roll_lanes(depth_f, 64)
    )

    pl.semaphore_wait(barrier, 8 + n1 - 1 + n2 - 1)

    def send(src, dst, sem_out, sem_in, device):
        copy = pltpu.make_async_remote_copy(
            src_ref=src, dst_ref=dst, send_sem=sem_out, recv_sem=sem_in,
            device_id=device, device_id_type=MESH,
        )
        return copy

    first, last = pl.ds(PAD, 8), pl.ds(PAD + ROWS - 8, 8)
    south, north = pl.ds(PAD - 8, 8), pl.ds(PAD + ROWS, 8)
    halos = []
    for i, (dx, dy) in enumerate(compass):
        if dx == 0:
            src = plane.at[:, last if dy == 1 else first]
            dst = plane.at[:, south if dy == 1 else north]
        else:
            side = 0 if dx == 1 else 1
            if dy == 0:
                src, dst = pack2, got2.at[side, pl.ds(8, ROWS)]
            elif dy == 1:
                src, dst = pack2.at[pl.ds(ROWS - 8, 8)], got2.at[side, pl.ds(0, 8)]
            else:
                src, dst = pack2.at[pl.ds(0, 8)], got2.at[side, pl.ds(ROWS + 8, 8)]
        halos.append(send(src, dst, send_sem.at[i], halo_sem.at[i], at(dx, dy)))

    for halo in halos:
        halo.start()

    @pl.when(c == nc - 1)
    def _():
        @pl.when(top)
        def _():
            for d in range(1, ny):
                ready(((y + d) % ny * nz + z, gy))

        @pl.when(x < nx - 1)
        def _():
            ready((gx, ngy - 1))

    for load in loads[2:6]:
        load.wait()
    half = jnp.where(lane < 64, 0.5, -0.5).astype(f32)
    edge_n[2 * levels:FOLD] = jnp.zeros((FOLD - 2 * levels, LANES), f32)
    edge_s[2 * levels:FOLD] = jnp.zeros((FOLD - 2 * levels, LANES), f32)

    def pack_level(k, acc):
        face = 0.25 * u[k] + half * kap[k]
        place = lane >> 1
        acc = jnp.where(place == k, roll_lanes(cot[k, 8:8 + ROWS], 2 * k + 1), acc)
        acc = jnp.where(place == k + 32, roll_lanes(face, 2 * k + 65), acc)
        edge_n[pl.ds(k, 1)] = cot[k, 7 + ROWS:8 + ROWS]
        edge_s[pl.ds(k, 1)] = cot[k, 8:9]
        edge_n[pl.ds(levels + k, 1)] = 0.25 * v[k, ROWS - 1:ROWS] - 0.5 * kap[k, ROWS - 1:ROWS]
        edge_s[pl.ds(levels + k, 1)] = 0.25 * v[k, 0:1] + 0.5 * kap[k, 0:1]
        return acc

    edge_ew[...] = lax.fori_loop(0, levels, pack_level, jnp.zeros((ROWS, LANES), f32))
    edges = [
        send(edge_ew, got_ew.at[0], send_sem.at[8], edge_sem.at[0], at(1, 0)),
        send(edge_ew, got_ew.at[1], send_sem.at[9], edge_sem.at[1], at(-1, 0)),
        send(edge_n, got_s, send_sem.at[10], edge_sem.at[2], at(0, 1)),
        send(edge_s, got_n, send_sem.at[11], edge_sem.at[3], at(0, -1)),
    ]
    for edge in edges:
        edge.start()

    @pl.when(top)
    def _():
        pl.semaphore_wait(ready_sem, ny - 1 + nx - 1)
        top2[0:8] = plane[0, last]
        top2[8:16] = plane[1, last]
        mine = pl.ds(pl.multiple_of(gx * 16, 16), 16)
        all2[mine] = top2[...]
        everyone_on_top(lambda d: send(top2, all2.at[mine], fold_sem.at[0], fold_sem.at[1], d).start())

        foldz[pl.ds(z, 1)] = edge_n[...][None]

        @pl.loop(1, nz)
        def _(j):
            p = y * nz + (z + j) % nz
            send(edge_n, foldz.at[z], fold_sem.at[2], fold_sem.at[3], (p, gy)).start()

    for halo in halos:
        halo.wait_recv()
    hw, he = got2[0], got2[1]
    wide[0, 8:88] = jnp.where(lane80 < 64, he, hw)
    wide[1, 8:88] = roll_lanes(jnp.where(lane80 < 64, hw, he), 64)

    loads[6].wait()
    seam = fp_s[0] + gx * LANES + 1

    @pl.when(gy == 0)
    def _():
        plane[1, 8:16] = zero8
        wide[1, 8:16] = zero8

    first_lane, last_lane = lane80 == 0, lane80 == LANES - 1

    def neighbours(mid, beside, rows):
        return [
            jnp.where(last_lane[:rows], roll_lanes(beside, LANES - 1), roll_lanes(mid, LANES - 1)),
            jnp.where(first_lane[:rows], roll_lanes(beside, 1), roll_lanes(mid, 1)),
        ]

    def both(mid, beside):
        return neighbours(mid, beside, 80), neighbours(beside, mid, 80)

    body, up, down = pl.ds(8, 80), pl.ds(9, 80), pl.ds(7, 80)

    def least_depths():
        dm, db = plane[1, body], wide[1, body]
        (d_e, d_w), (db_e, db_w) = both(dm, db)
        for i, (a, o) in enumerate(
            [(d_e, db_e), (d_w, db_w), (plane[1, up], wide[1, up]), (plane[1, down], wide[1, down])]
        ):
            dmin[i, 0] = jnp.minimum(dm, a)
            dmin[i, 1] = jnp.minimum(db, o)

    def apply(mid_ref, beside_ref, out_ref):
        mid, beside = mid_ref[body], beside_ref[body]
        (m_e, m_w), (s_e, s_w) = both(mid, beside)
        for i, (centre, nbrs) in enumerate(
            [
                (mid, (m_e, m_w, mid_ref[up], mid_ref[down])),
                (beside, (s_e, s_w, beside_ref[up], beside_ref[down])),
            ]
        ):
            total = jnp.zeros_like(centre)
            for j in range(4):
                total = total + dmin[j, i] * (centre - nbrs[j])
            out_ref[i, body] = damping * centre + (1.0 / levels) * total

    least_depths()
    apply(plane.at[0], wide.at[0], vec1)
    apply(vec1.at[0], vec1.at[1], vec2)
    inner = pl.ds(PAD, ROWS)
    mid2 = vec2[0, inner]
    m_e, m_w = neighbours(mid2, vec2[1, inner], ROWS)
    nbrs = (m_e, m_w, vec2[0, PAD + 1:PAD + 1 + ROWS], vec2[0, PAD - 1:PAD - 1 + ROWS])
    mid3 = jnp.zeros_like(mid2)
    for j in range(4):
        mid3 = mid3 + dmin[j, 0, 8:8 + ROWS] * (mid2 - nbrs[j])
    mid3 = damping * mid2 + (1.0 / levels) * mid3
    mid0, mid1 = plane[0, inner], vec1[0, inner]

    sub8 = lax.broadcasted_iota(jnp.int32, (8, LANES), 0)
    lane8 = lax.broadcasted_iota(jnp.int32, (8, LANES), 1)

    def moment_row(fields):
        f0, f1, f2, f3 = [split(f) for f in fields]
        for j, (a, o) in enumerate([(f0, f0), (f0, f1), (f1, f1), (f1, f2), (f2, f2), (f2, f3)]):
            high, low = folded_rows(two_product(a, o))
            tot[j:j + 1] = high[0:1]
            tot[8 + j:9 + j] = low[0:1]
        tot[6:8] = jnp.zeros((2, LANES), f32)
        tot[14:16] = jnp.zeros((2, LANES), f32)
        high, low = tot[0:8], tot[8:16]
        scale = 256.0 * jnp.max(jnp.abs(high), axis=1, keepdims=True)
        coarse = (high + scale) - scale
        rest = jnp.sum((high - coarse) + low, axis=1, keepdims=True)
        high, low = renormal((jnp.sum(coarse, axis=1, keepdims=True), rest))
        row = jnp.where(lane8 == sub8, high, 0.0) + jnp.where(lane8 == sub8 + 8, low, 0.0)
        return jnp.sum(row, axis=0, keepdims=True)

    apart = top & (lax.broadcasted_iota(jnp.int32, (ROWS, LANES), 0) >= ROWS - 3)
    mom[...] = moment_row([jnp.where(apart, 0.0, f) for f in (mid0, mid1, mid2, mid3)])

    red1[pl.ds(me1, 1)] = mom[...]
    group1(lambda d: send(mom, red1.at[pl.ds(me1, 1)], red_sem.at[0], red_sem.at[1], d).start())

    for edge in edges:
        edge.wait_recv()

    @pl.when(top)
    def _():
        dmin[2, 0, 7 + ROWS:8 + ROWS] = jnp.zeros((1, LANES), f32)

    sides[...] = jnp.where((lane & 1) == 1, got_ew[1], got_ew[0])
    lane16 = lax.broadcasted_iota(jnp.int32, (16, LANES), 1)

    def level(k, carry):
        kf = k.astype(f32)
        cot[k, 7:8] = got_s[pl.ds(k, 1)]
        cot[k, 8 + ROWS:9 + ROWS] = got_n[pl.ds(k, 1)]
        qs[7:8] = got_s[pl.ds(levels + k, 1)]
        qn[8 + ROWS:9 + ROWS] = got_n[pl.ds(levels + k, 1)]
        for r in range(0, ROWS, 16):
            rows = slice(r, r + 16)
            vq, kq = 0.25 * v[k, rows], 0.5 * kap[k, rows]
            qn[8 + r:24 + r] = vq + kq
            qs[8 + r:24 + r] = vq - kq
        for r in range(0, ROWS, 16):
            rows, mid = slice(r, r + 16), slice(8 + r, 24 + r)
            ct = cot[k, mid]
            uq, kq = 0.25 * u[k, rows], 0.5 * kap[k, rows]
            qe, qw = uq + kq, uq - kq
            edge = sides[rows]
            ec = roll_lanes(edge, (LANES - 1) - 2 * k)
            eq = roll_lanes(edge, 63 - 2 * k)
            c_e = roll_lanes(jnp.where(lane16 == 0, ec, ct), LANES - 1)
            c_w = roll_lanes(jnp.where(lane16 == LANES - 1, ec, ct), 1)
            q_e = roll_lanes(jnp.where(lane16 == 0, eq, qe), LANES - 1)
            q_w = roll_lanes(jnp.where(lane16 == LANES - 1, eq, qw), 1)
            c_n, c_s = cot[k, 9 + r:25 + r], cot[k, 7 + r:23 + r]
            ke = jnp.where(dmin[0, 0, mid] > kf, time_step * (qe + q_e), 0.0)
            kw = jnp.where(dmin[1, 0, mid] > kf, time_step * (qw + q_w), 0.0)
            kn = jnp.where(dmin[2, 0, mid] > kf, time_step * (qn[8 + r:24 + r] + qn[9 + r:25 + r]), 0.0)
            ks = jnp.where(dmin[3, 0, mid] > kf, time_step * (qs[8 + r:24 + r] + qs[7 + r:23 + r]), 0.0)
            for i, face in enumerate((ke, kw, kn, ks)):
                faces[k, 1 + i, rows] = face
            faces[k, 0, rows] = ct + (ke * (c_e - ct) + kw * (ct - c_w)) + (kn * (c_n - ct) + ks * (ct - c_s))
        return carry

    lax.fori_loop(0, levels, level, 0)

    def wait_red(buf, n, sem):
        pltpu.make_async_copy(buf.at[pl.ds(0, n - 1)], buf.at[pl.ds(0, n - 1)], sem).wait()

    wait_red(red1, n1, red_sem.at[1])
    sums = red1[...]
    sums, rest = folded_rows((sums, jnp.zeros_like(sums)))
    mom2[...] = (sums + roll_lanes(rest, 8))[0:1]
    red2[pl.ds(me2, 1)] = mom2[...]
    group2(lambda d: send(mom2, red2.at[pl.ds(me2, 1)], red_sem.at[2], red_sem.at[3], d).start())

    below = sorted(range(ngy - 1), key=lambda g: -min(nx - 1 - g // nc, g // nc + 1))

    @pl.when(top)
    def _():
        pltpu.make_async_copy(foldz.at[pl.ds(0, nz - 1)], foldz.at[pl.ds(0, nz - 1)], fold_sem.at[3]).wait()
        whole = ngx * LANES
        start = (seam - LANES - gx * LANES + 2 * whole) % whole
        blk, off = start // LANES, start % LANES
        after = (blk + 1) % ngx
        fold_stage[0] = foldz[blk % nz]
        fold_stage[1] = foldz[after % nz]
        fold_y[pl.ds(y, 1)] = fold_stage[...][None]

        @pl.loop(1, ny)
        def _(j):
            p = ((y + j) % ny) * nz + z
            send(fold_stage, fold_y.at[y], fold_sem.at[4], fold_sem.at[5], (p, gy)).start()

        others = all2.at[pl.ds(0, (ngx - 1) * 16)]
        pltpu.make_async_copy(others, others, fold_sem.at[1]).wait()

        def exact_dot(a, o):
            return lax.dot(a, o, precision=lax.Precision.HIGHEST, preferred_element_type=f32)

        col = lax.broadcasted_iota(jnp.int32, (2 * LANES, LANES), 1)
        src = lax.broadcasted_iota(jnp.int32, (2 * LANES, LANES), 0)
        pick = (src == off + (LANES - 1) - col).astype(f32)
        block = lax.broadcasted_iota(jnp.int32, (ngx, ngx), 0)
        source = lax.broadcasted_iota(jnp.int32, (ngx, ngx), 1)
        order = ((block + source - blk - gx + 2 * ngx) % ngx == 0).astype(f32)
        fields = [[all2[pl.ds(8 * f + q, ngx, stride=16)] for q in range(2, 8)] for f in range(2)]
        mirror = [fields[f][q] for f in range(2) for q in (5, 4, 3)]
        turned = exact_dot(order, jnp.concatenate(mirror, axis=1))
        turned = [turned[:, i * LANES:(i + 1) * LANES] for i in range(6)]
        turned = [jnp.concatenate([t, pltpu.roll(t, 1, 0)], axis=1) for t in turned]
        mir[...] = exact_dot(jnp.concatenate(turned, axis=0), pick)
        mirror = [mir[i * ngx:(i + 1) * ngx] for i in range(6)]
        values, depth = fields[0] + mirror[:3], fields[1] + mirror[3:]
        spot = lax.broadcasted_iota(jnp.int32, (ngx, LANES), 1)

        def beside(t):
            ahead, behind = roll_lanes(t, LANES - 1), roll_lanes(t, 1)
            return (
                jnp.where(spot == LANES - 1, pltpu.roll(ahead, ngx - 1, 0), ahead),
                jnp.where(spot == 0, pltpu.roll(behind, 1, 0), behind),
            )

        least = {
            i: [jnp.minimum(depth[i], t) for t in (*beside(depth[i]), depth[i + 1], depth[i - 1])]
            for i in range(1, 8)
        }

        def step(f, rows):
            out = {}
            for i in rows:
                total = jnp.zeros_like(f[i])
                for d, t in zip(least[i], (*beside(f[i]), f[i + 1], f[i - 1])):
                    total = total + d * (f[i] - t)
                out[i] = damping * f[i] + (1.0 / levels) * total
            return out

        band1 = step(values, range(1, 8))
        band2 = step(band1, range(2, 7))
        band3 = step(band2, range(3, 6))
        band[...] = moment_row(
            [jnp.concatenate([f[i] for i in (3, 4, 5)], axis=0) for f in (values, band1, band2, band3)]
        )
        red2[n2:n2 + 1] = band[...]
        for g in below:
            send(band, red2.at[pl.ds(n2, 1)], band_sem.at[0], band_sem.at[1], (gx, g)).start()

        for i in range(6):
            f, row = i // 3, PAD + ROWS + i % 3
            mine, ahead, behind = [mir[pl.ds(i * ngx + (gx + d) % ngx, 1)] for d in (0, 1, ngx - 1)]
            plane[f, row:row + 1] = mine
            wide[f, row:row + 1] = jnp.where(lane8[0:1] < 64, ahead, behind)
        least_depths()
        apply(plane.at[0], wide.at[0], vec1)
        apply(vec1.at[0], vec1.at[1], vec2)

        pltpu.make_async_copy(fold_y.at[pl.ds(0, ny - 1)], fold_y.at[pl.ds(0, ny - 1)], fold_sem.at[5]).wait()
        got_n[...] = exact_dot(jnp.concatenate([fold_y[blk // nz, 0], fold_y[after // nz, 1]], axis=1), pick)
        here = slice(ROWS - 1, ROWS)

        def across(k, carry):
            ct = cot[k, 7 + ROWS:8 + ROWS]
            half = 0.25 * v[k, here] + 0.5 * kap[k, here] - got_n[pl.ds(levels + k, 1)]
            kn = jnp.where(dmin[2, 0, 7 + ROWS:8 + ROWS] > k.astype(f32), time_step * half, 0.0)
            faces[k, 3, here] = kn
            faces[k, 0, here] += kn * (got_n[pl.ds(k, 1)] - ct)
            return carry

        lax.fori_loop(0, levels, across, 0)

    store = pltpu.make_async_copy(faces, faces_h, store_sem.at[0])
    store.start()

    wait_red(red2, n2, red_sem.at[3])

    @pl.when(gy != ngy - 1)
    def _():
        one = red2.at[pl.ds(n2, 1)]
        pltpu.make_async_copy(one, one, band_sem.at[1]).wait()

    sums = red2[...]
    sums, rest = folded_rows((sums, jnp.zeros_like(sums)))
    rest = rest + pltpu.roll(sums, LANES - 8, 1)
    parts = []
    for part in (sums, rest):
        part = jnp.sum(jnp.where(lane8 == sub8, part, 0.0), axis=1, keepdims=True)
        parts.append(jnp.broadcast_to(part, (8, LANES)))
    tot[0:8], tot[8:16] = renormal(parts)
    pairs = [[jnp.broadcast_to(tot[i:i + 1], (8, LANES)) for i in (j, 8 + j)] for j in range(6)]
    m = [high for high, low in pairs]
    lo, hi = 0.0999, 8.2
    rho = m[1] / m[0]
    rho_parts = split(rho)

    def centred(a, o):
        p, rest = two_product(rho_parts, split(o[0]))
        return renormal(pair_add(a, (-p, -(rest + rho * o[1]))))

    s1 = [centred(pairs[j + 1], pairs[j]) for j in range(5)]
    n = [centred(s1[j + 1], s1[j])[0] for j in range(4)]
    n[0] = jnp.maximum(n[0], 0.0)

    def bounded(t, least, most):
        return jnp.where(t >= least, jnp.minimum(t, most), least)

    e1 = n[0] / m[0]
    rho1 = bounded(n[1] / n[0], lo, hi)
    p1 = bounded(rho1 - e1 / rho, lo, hi)
    k0 = n[2] - rho1 * n[1] - e1 * n[0]
    k1 = n[3] - 2.0 * rho1 * n[2] + rho1 * rho1 * n[1] - 2.0 * e1 * rho * n[0] + e1 * e1 * m[1]
    e2 = bounded(k0 / n[0], 0.0, 70.0)
    rho2 = bounded(k1 / k0, lo, hi)
    p2 = bounded(rho2 - e2 / p1, lo, hi)
    z0 = 1.0 / rho
    z1 = -z0 / p1
    y2 = -z1 / p2
    y1 = z1 - e2 / p1 * y2
    y0 = z0 - e1 / rho * y1
    a0 = y0 - rho * y1 + (rho1 * rho - e1) * y2
    a1 = y1 - (rho + rho1) * y2

    def spread(a, rows):
        return jnp.broadcast_to(a[0:1], (rows, LANES))

    rows80 = [spread(a, 80) for a in (a0, a1, y2)]
    h_mid = rows80[0] * plane[0, body] + rows80[1] * vec1[0, body] + rows80[2] * vec2[0, body]
    h_side = rows80[0] * wide[0, body] + rows80[1] * vec1[1, body] + rows80[2] * vec2[1, body]
    hv[0, body] = h_mid
    inner_mid, inner_side = h_mid[8:8 + ROWS], h_side[8:8 + ROWS]
    h_e, h_w = neighbours(inner_mid, inner_side, ROWS)
    hv[1, inner] = h_e - inner_mid
    hv[2, inner] = inner_mid - h_w
    hv[3, inner] = hv[0, PAD + 1:PAD + 1 + ROWS] - inner_mid
    hv[4, inner] = inner_mid - hv[0, PAD - 1:PAD - 1 + ROWS]
    hv[5, inner] = plane[1, inner]
    height = pltpu.make_async_copy(hv.at[:, inner], height_h, store_sem.at[1])
    height.start()

    for halo in halos:
        halo.wait_send()
    for edge in edges:
        edge.wait_send()
    wait_red(red1, n1, red_sem.at[0])
    wait_red(red2, n2, red_sem.at[2])

    @pl.when(top)
    def _():
        others = all2.at[pl.ds(0, (ngx - 1) * 16)]
        pltpu.make_async_copy(others, others, fold_sem.at[0]).wait()
        some = red2.at[pl.ds(0, ngy - 1)]
        pltpu.make_async_copy(some, some, band_sem.at[0]).wait()
        pltpu.make_async_copy(foldz.at[pl.ds(0, nz - 1)], foldz.at[pl.ds(0, nz - 1)], fold_sem.at[2]).wait()
        pltpu.make_async_copy(fold_y.at[pl.ds(0, ny - 1)], fold_y.at[pl.ds(0, ny - 1)], fold_sem.at[4]).wait()

    height.wait()
    store.wait()


def finish(levels, group, faces_h, height_h, th_h, out_h, hadj_h, th, faces, height, out, sem):
    parts = [pl.ds(k, group) for k in range(0, levels, group)]
    first = [
        pltpu.make_async_copy(height_h, height, sem.at[0]),
        pltpu.make_async_copy(th_h, th, sem.at[1]),
    ]
    loads = [
        pltpu.make_async_copy(faces_h.at[p], faces.at[p], sem.at[2 + i]) for i, p in enumerate(parts)
    ]
    for load in first + loads:
        load.start()
    first[0].wait()
    stores = [pltpu.make_async_copy(height.at[0], hadj_h, sem.at[0])]
    stores[0].start()
    first[1].wait()
    for i, p in enumerate(parts):
        loads[i].wait()
        for r in range(0, ROWS, 8):
            rows = slice(r, r + 8)
            hc, de, dw, dn, ds_, wet = [height[j, rows] for j in range(6)]
            for k in range(i * group, (i + 1) * group):
                grown = (
                    jnp.where(wet > float(k), hc, 0.0)
                    + (faces[k, 1, rows] * de + faces[k, 2, rows] * dw)
                    + (faces[k, 3, rows] * dn + faces[k, 4, rows] * ds_)
                )
                out[k, rows] = faces[k, 0, rows] + th[k] * grown
        stores.append(pltpu.make_async_copy(out.at[p], out_h.at[p], sem.at[2 + i]))
        stores[-1].start()
    for store in stores:
        store.wait()


def solution(mesh):
    ngx, ngy = mesh.shape["gx"], mesh.shape["gy"]
    nc = 2
    nx = ngy // nc
    ny = 4 if ngx == 32 else 2
    nz = ngx // ny

    def local(cot, b, u, v, kap, th, dep, fp):
        levels = cot.shape[0]
        f32 = jnp.float32

        def vmem(*shape, dtype=f32):
            return pltpu.VMEM(shape, dtype)

        cube = (levels, ROWS, LANES)
        scratch = [
            pltpu.SMEM((LANES,), jnp.int32),
            vmem(levels, 80, LANES), vmem(*cube), vmem(*cube), vmem(*cube),
            vmem(ROWS, LANES, dtype=jnp.int32),
            vmem(2, 96, LANES), vmem(2, 96, LANES),
            vmem(ROWS, LANES), vmem(2, 80, LANES), vmem(4, 2, 80, LANES),
            vmem(2, 96, LANES), vmem(2, 96, LANES),
            vmem(ROWS, LANES), vmem(2, ROWS, LANES),
            vmem(FOLD, LANES), vmem(FOLD, LANES), vmem(FOLD, LANES), vmem(FOLD, LANES),
            vmem(16, LANES), vmem(ngx * 16, LANES), vmem(ngx * 6, LANES),
            vmem(nz, FOLD, LANES), vmem(2, FOLD, LANES), vmem(ny, 2, FOLD, LANES),
            vmem(ROWS, LANES),
            vmem(80, LANES), vmem(80, LANES),
            vmem(levels, 5, ROWS, LANES), vmem(6, 96, LANES),
            vmem(1, LANES), vmem(max(8, nz * nc), LANES), vmem(1, LANES), vmem(8 if nx * ny < 8 else 32, LANES), vmem(1, LANES), vmem(16, LANES),
            pltpu.SemaphoreType.DMA((7,)), pltpu.SemaphoreType.DMA((2,)),
            pltpu.SemaphoreType.DMA((12,)), pltpu.SemaphoreType.DMA((8,)),
            pltpu.SemaphoreType.DMA((4,)), pltpu.SemaphoreType.DMA((4,)),
            pltpu.SemaphoreType.DMA((6,)), pltpu.SemaphoreType.DMA((2,)),
            pltpu.SemaphoreType.REGULAR,
        ]
        hbm = pl.BlockSpec(memory_space=pltpu.HBM)
        limit = 62 * 1024 * 1024
        faces, height = pl.pallas_call(
            functools.partial(kernel, nz, ny, nc, nx, levels),
            out_shape=(
                jax.ShapeDtypeStruct((levels, 5, ROWS, LANES), f32),
                jax.ShapeDtypeStruct((6, ROWS, LANES), f32),
            ),
            in_specs=[hbm] * 7,
            out_specs=(hbm, hbm),
            scratch_shapes=scratch,
            compiler_params=pltpu.CompilerParams(
                collective_id=0, has_side_effects=True, vmem_limit_bytes=limit
            ),
        )(cot, b, u, v, kap, dep, fp)
        group = 5 if levels % 5 == 0 else 1
        return pl.pallas_call(
            functools.partial(finish, levels, group),
            out_shape=(jax.ShapeDtypeStruct(cube, f32), jax.ShapeDtypeStruct((ROWS, LANES), f32)),
            in_specs=[hbm] * 3,
            out_specs=(hbm, hbm),
            scratch_shapes=[
                pltpu.SMEM((levels,), f32), vmem(levels, 5, ROWS, LANES), vmem(6, ROWS, LANES), vmem(*cube),
                pltpu.SemaphoreType.DMA((2 + levels // group,)),
            ],
            compiler_params=pltpu.CompilerParams(vmem_limit_bytes=limit),
        )(faces, height, th)

    in_specs = (
        P(None, "gy", "gx"), P("gy", "gx"), P(None, "gy", "gx"), P(None, "gy", "gx"),
        P(None, "gy", "gx"), P(), P("gy", "gx"), P("gx"),
    )
    out_specs = (P(None, "gy", "gx"), P("gy", "gx"))
    return jax.shard_map(local, mesh=mesh, in_specs=in_specs, out_specs=out_specs, check_vma=False)
```

```python
import functools

import jax
import jax.numpy as jnp
from jax import lax
from jax.experimental import pallas as pl
from jax.experimental.pallas import tpu as pltpu
from jax.sharding import PartitionSpec as P

MESH = pl.DeviceIdType.MESH
damping = 0.1
time_step = 0.3
ROWS = 64
LANES = 128
PAD = 16
FOLD = 56


def roll_lanes(x, shift):
    return pltpu.roll(x, shift, 1)


def two_sum(a, b):
    total = a + b
    t = total - a
    return total, (a - (total - t)) + (b - t)


def split(a):
    t = 4097.0 * a
    high = t - (t - a)
    return a, high, a - high


def two_product(a, b):
    (a, ah, al), (b, bh, bl) = a, b
    p = a * b
    return p, ((ah * bh - p) + ah * bl + al * bh) + al * bl


def pair_add(a, b):
    total, rest = two_sum(a[0], b[0])
    return total, rest + (a[1] + b[1])


def renormal(a):
    total = a[0] + a[1]
    return total, a[1] - (total - a[0])


def folded_rows(a):
    rows = a[0].shape[0]
    while rows > 8:
        keep = rows // 2 if rows % 16 == 0 else rows - 8
        rest = pair_add([t[:rows - keep] for t in a], [t[keep:] for t in a])
        a = [jnp.concatenate([t, o[rows - keep:keep]]) if 2 * keep > rows else t for t, o in zip(rest, a)]
        rows = keep
    for shift in (4, 2, 1):
        a = pair_add(a, [pltpu.roll(t, shift, 0) for t in a])
    return a


def kernel(
    nz, ny, nc, nx, levels, group,
    cot_h, b_h, u_h, v_h, k_h, th_h, dep_h, fp_h, out_h, hadj_h,
    th_s, fp_s, cot, u, v, kap, dint, plane, wide, pack2, got2, dmin, vec1, vec2,
    edge_ew, got_ew, edge_n, edge_s, got_n, got_s,
    top2, all2, mir, foldz, fold_stage, fold_y, sides,
    qn, qs, faces, hv, outv,
    mom, red1, mom2, red2, band, tot,
    load_sem, store_sem, send_sem, halo_sem, edge_sem, red_sem, fold_sem, band_sem, ready_sem,
):
    gx, gy = lax.axis_index("gx"), lax.axis_index("gy")
    ngx, ngy = ny * nz, nx * nc
    y, z, x, c = gx // nz, gx % nz, gy // nc, gy % nc
    top = gy == ngy - 1
    lane = lax.broadcasted_iota(jnp.int32, (ROWS, LANES), 1)
    lane80 = lax.broadcasted_iota(jnp.int32, (80, LANES), 1)
    f32 = jnp.float32

    def at(dx, dy):
        return (gx + dx + ngx) % ngx, (gy + dy + ngy) % ngy

    compass = [(1, 0), (-1, 0), (0, 1), (0, -1), (1, 1), (-1, 1), (1, -1), (-1, -1)]

    loads = [
        pltpu.make_async_copy(b_h, plane.at[0, pl.ds(PAD, ROWS)], load_sem.at[0]),
        pltpu.make_async_copy(dep_h, dint, load_sem.at[1]),
        pltpu.make_async_copy(cot_h, cot.at[:, pl.ds(8, ROWS)], load_sem.at[2]),
        pltpu.make_async_copy(u_h, u, load_sem.at[3]),
        pltpu.make_async_copy(k_h, kap, load_sem.at[4]),
        pltpu.make_async_copy(v_h, v, load_sem.at[5]),
        pltpu.make_async_copy(fp_h, fp_s, load_sem.at[6]),
        pltpu.make_async_copy(th_h, th_s, load_sem.at[7]),
    ]
    for load in loads:
        load.start()

    barrier = pltpu.get_barrier_semaphore()

    def greet(device):
        pl.semaphore_signal(barrier, inc=1, device_id=device, device_id_type=MESH)

    def far_first(n):
        return sorted(range(n), key=lambda d: (-min(d, n - d), d))

    far_y = [((y + d) % ny) * nz for d in far_first(ny)]
    def ready(device):
        pl.semaphore_signal(ready_sem, inc=1, device_id=device, device_id_type=MESH)

    n1, n2 = nz * nc, nx * ny
    me1, me2 = z * nc + c, y * nx + x
    far_z = [(z + d) % nz for d in far_first(nz)]
    far_yx = sorted(
        [(d, e) for d in range(ny) for e in range(nx)],
        key=lambda t: -min(t[0], ny - t[0]) - min(t[1], nx - t[1]),
    )

    def group1(act):
        for d, pz in zip(far_first(nz), far_z):
            for e in range(nc - 1, -1, -1):
                if (d, e) != (0, 0):
                    act((y * nz + pz, x * nc + (c + e) % nc))

    def group2(act):
        for d, e in far_yx:
            if (d, e) != (0, 0):
                act(((y + d) % ny * nz + z, (x + e) % nx * nc + c))

    def everyone_on_top(act):
        for pz in far_z[:-1]:
            for py in far_y:
                act((py + pz, gy))
        for py in far_y[:-1]:
            act((py + z, gy))

    for d in compass:
        greet(at(*d))
    group1(greet)
    group2(greet)

    zero8 = jnp.zeros((8, LANES), f32)
    for part, n in ((red1, n1), (red2, n2 + 1)):
        if n < part.shape[0]:
            part[n:] = jnp.zeros((part.shape[0] - n, LANES), f32)
    for f in range(2):
        for part in (plane, wide, vec1, vec2):
            part[f, 0:8] = zero8
            part[f, 88:96] = zero8
    loads[0].wait()
    loads[1].wait()
    depth_f = dint[...].astype(f32)
    plane[1, PAD:PAD + ROWS] = depth_f
    pack2[...] = jnp.where(
        (lane < 32) | (lane >= 96), plane[0, PAD:PAD + ROWS], roll_lanes(depth_f, 64)
    )

    pl.semaphore_wait(barrier, 8 + n1 - 1 + n2 - 1)

    def send(src, dst, sem_out, sem_in, device):
        copy = pltpu.make_async_remote_copy(
            src_ref=src, dst_ref=dst, send_sem=sem_out, recv_sem=sem_in,
            device_id=device, device_id_type=MESH,
        )
        return copy

    first, last = pl.ds(PAD, 8), pl.ds(PAD + ROWS - 8, 8)
    south, north = pl.ds(PAD - 8, 8), pl.ds(PAD + ROWS, 8)
    halos = []
    for i, (dx, dy) in enumerate(compass):
        if dx == 0:
            src = plane.at[:, last if dy == 1 else first]
            dst = plane.at[:, south if dy == 1 else north]
        else:
            side = 0 if dx == 1 else 1
            if dy == 0:
                src, dst = pack2, got2.at[side, pl.ds(8, ROWS)]
            elif dy == 1:
                src, dst = pack2.at[pl.ds(ROWS - 8, 8)], got2.at[side, pl.ds(0, 8)]
            else:
                src, dst = pack2.at[pl.ds(0, 8)], got2.at[side, pl.ds(ROWS + 8, 8)]
        halos.append(send(src, dst, send_sem.at[i], halo_sem.at[i], at(dx, dy)))

    for halo in halos:
        halo.start()

    @pl.when(c == nc - 1)
    def _():
        @pl.when(top)
        def _():
            for d in range(1, ny):
                ready(((y + d) % ny * nz + z, gy))

        @pl.when(x < nx - 1)
        def _():
            ready((gx, ngy - 1))

    for load in loads[2:6]:
        load.wait()
    half = jnp.where(lane < 64, 0.5, -0.5).astype(f32)
    edge_n[2 * levels:FOLD] = jnp.zeros((FOLD - 2 * levels, LANES), f32)
    edge_s[2 * levels:FOLD] = jnp.zeros((FOLD - 2 * levels, LANES), f32)

    def pack_levels(g, acc):
        place = lane >> 1
        for k in [g * group + j for j in range(group)]:
            face = 0.25 * u[k] + half * kap[k]
            acc = jnp.where(place == k, roll_lanes(cot[k, 8:8 + ROWS], 2 * k + 1), acc)
            acc = jnp.where(place == k + 32, roll_lanes(face, 2 * k + 65), acc)
            edge_n[pl.ds(k, 1)] = cot[k, 7 + ROWS:8 + ROWS]
            edge_s[pl.ds(k, 1)] = cot[k, 8:9]
            edge_n[pl.ds(levels + k, 1)] = 0.25 * v[k, ROWS - 1:ROWS] - 0.5 * kap[k, ROWS - 1:ROWS]
            edge_s[pl.ds(levels + k, 1)] = 0.25 * v[k, 0:1] + 0.5 * kap[k, 0:1]
        return acc

    edge_ew[...] = lax.fori_loop(0, levels // group, pack_levels, jnp.zeros((ROWS, LANES), f32))
    edges = [
        send(edge_ew, got_ew.at[0], send_sem.at[8], edge_sem.at[0], at(1, 0)),
        send(edge_ew, got_ew.at[1], send_sem.at[9], edge_sem.at[1], at(-1, 0)),
        send(edge_n, got_s, send_sem.at[10], edge_sem.at[2], at(0, 1)),
        send(edge_s, got_n, send_sem.at[11], edge_sem.at[3], at(0, -1)),
    ]
    for edge in edges:
        edge.start()

    @pl.when(top)
    def _():
        pl.semaphore_wait(ready_sem, ny - 1 + nx - 1)
        top2[0:8] = plane[0, last]
        top2[8:16] = plane[1, last]
        mine = pl.ds(pl.multiple_of(gx * 16, 16), 16)
        all2[mine] = top2[...]
        everyone_on_top(lambda d: send(top2, all2.at[mine], fold_sem.at[0], fold_sem.at[1], d).start())

        foldz[pl.ds(z, 1)] = edge_n[...][None]

        @pl.loop(1, nz)
        def _(j):
            p = y * nz + (z + j) % nz
            send(edge_n, foldz.at[z], fold_sem.at[2], fold_sem.at[3], (p, gy)).start()

    for halo in halos:
        halo.wait_recv()
    hw, he = got2[0], got2[1]
    wide[0, 8:88] = jnp.where(lane80 < 64, he, hw)
    wide[1, 8:88] = roll_lanes(jnp.where(lane80 < 64, hw, he), 64)

    loads[6].wait()
    seam = fp_s[0] + gx * LANES + 1

    @pl.when(gy == 0)
    def _():
        plane[1, 8:16] = zero8
        wide[1, 8:16] = zero8

    first_lane, last_lane = lane80 == 0, lane80 == LANES - 1

    def neighbours(mid, beside, rows):
        return [
            jnp.where(last_lane[:rows], roll_lanes(beside, LANES - 1), roll_lanes(mid, LANES - 1)),
            jnp.where(first_lane[:rows], roll_lanes(beside, 1), roll_lanes(mid, 1)),
        ]

    def both(mid, beside):
        return neighbours(mid, beside, 80), neighbours(beside, mid, 80)

    body, up, down = pl.ds(8, 80), pl.ds(9, 80), pl.ds(7, 80)

    def least_depths():
        dm, db = plane[1, body], wide[1, body]
        (d_e, d_w), (db_e, db_w) = both(dm, db)
        for i, (a, o) in enumerate(
            [(d_e, db_e), (d_w, db_w), (plane[1, up], wide[1, up]), (plane[1, down], wide[1, down])]
        ):
            dmin[i, 0] = jnp.minimum(dm, a)
            dmin[i, 1] = jnp.minimum(db, o)

    def apply(mid_ref, beside_ref, out_ref):
        mid, beside = mid_ref[body], beside_ref[body]
        (m_e, m_w), (s_e, s_w) = both(mid, beside)
        for i, (centre, nbrs) in enumerate(
            [
                (mid, (m_e, m_w, mid_ref[up], mid_ref[down])),
                (beside, (s_e, s_w, beside_ref[up], beside_ref[down])),
            ]
        ):
            total = jnp.zeros_like(centre)
            for j in range(4):
                total = total + dmin[j, i] * (centre - nbrs[j])
            out_ref[i, body] = damping * centre + (1.0 / levels) * total

    least_depths()
    apply(plane.at[0], wide.at[0], vec1)
    apply(vec1.at[0], vec1.at[1], vec2)
    inner = pl.ds(PAD, ROWS)
    mid2 = vec2[0, inner]
    m_e, m_w = neighbours(mid2, vec2[1, inner], ROWS)
    nbrs = (m_e, m_w, vec2[0, PAD + 1:PAD + 1 + ROWS], vec2[0, PAD - 1:PAD - 1 + ROWS])
    mid3 = jnp.zeros_like(mid2)
    for j in range(4):
        mid3 = mid3 + dmin[j, 0, 8:8 + ROWS] * (mid2 - nbrs[j])
    mid3 = damping * mid2 + (1.0 / levels) * mid3
    mid0, mid1 = plane[0, inner], vec1[0, inner]

    sub8 = lax.broadcasted_iota(jnp.int32, (8, LANES), 0)
    lane8 = lax.broadcasted_iota(jnp.int32, (8, LANES), 1)

    def moment_row(fields):
        f0, f1, f2, f3 = [split(f) for f in fields]
        for j, (a, o) in enumerate([(f0, f0), (f0, f1), (f1, f1), (f1, f2), (f2, f2), (f2, f3)]):
            high, low = folded_rows(two_product(a, o))
            tot[j:j + 1] = high[0:1]
            tot[8 + j:9 + j] = low[0:1]
        tot[6:8] = jnp.zeros((2, LANES), f32)
        tot[14:16] = jnp.zeros((2, LANES), f32)
        high, low = tot[0:8], tot[8:16]
        scale = 256.0 * jnp.max(jnp.abs(high), axis=1, keepdims=True)
        coarse = (high + scale) - scale
        rest = jnp.sum((high - coarse) + low, axis=1, keepdims=True)
        high, low = renormal((jnp.sum(coarse, axis=1, keepdims=True), rest))
        row = jnp.where(lane8 == sub8, high, 0.0) + jnp.where(lane8 == sub8 + 8, low, 0.0)
        return jnp.sum(row, axis=0, keepdims=True)

    apart = top & (lax.broadcasted_iota(jnp.int32, (ROWS, LANES), 0) >= ROWS - 3)
    mom[...] = moment_row([jnp.where(apart, 0.0, f) for f in (mid0, mid1, mid2, mid3)])

    red1[pl.ds(me1, 1)] = mom[...]
    group1(lambda d: send(mom, red1.at[pl.ds(me1, 1)], red_sem.at[0], red_sem.at[1], d).start())

    for edge in edges:
        edge.wait_recv()

    sides[...] = jnp.where((lane & 1) == 1, got_ew[1], got_ew[0])
    lane16 = lax.broadcasted_iota(jnp.int32, (16, LANES), 1)

    def level_group(begin, end, g, carry):
        ks = [g * group + j for j in range(group)]
        for j, k in enumerate(ks):
            cot[k, 7:8] = got_s[pl.ds(k, 1)]
            cot[k, 8 + ROWS:9 + ROWS] = got_n[pl.ds(k, 1)]
            qs[j, 7:8] = got_s[pl.ds(levels + k, 1)]
            qn[j, 8 + ROWS:9 + ROWS] = got_n[pl.ds(levels + k, 1)]
            for r in range(max(begin - 8, 0), min(end + 8, ROWS), 8):
                rows = slice(r, r + 8)
                vq, kq = 0.25 * v[k, rows], 0.5 * kap[k, rows]
                qn[j, 8 + r:16 + r] = vq + kq
                qs[j, 8 + r:16 + r] = vq - kq
        for r in range(begin, end, 16):
            for j, k in enumerate(ks):
                kf = k.astype(f32)
                rows, mid = slice(r, r + 16), slice(8 + r, 24 + r)
                ct = cot[k, mid]
                uq, kq = 0.25 * u[k, rows], 0.5 * kap[k, rows]
                qe, qw = uq + kq, uq - kq
                edge = sides[rows]
                ec = roll_lanes(edge, (LANES - 1) - 2 * k)
                eq = roll_lanes(edge, 63 - 2 * k)
                c_e = roll_lanes(jnp.where(lane16 == 0, ec, ct), LANES - 1)
                c_w = roll_lanes(jnp.where(lane16 == LANES - 1, ec, ct), 1)
                q_e = roll_lanes(jnp.where(lane16 == 0, eq, qe), LANES - 1)
                q_w = roll_lanes(jnp.where(lane16 == LANES - 1, eq, qw), 1)
                c_n, c_s = cot[k, 9 + r:25 + r], cot[k, 7 + r:23 + r]
                ke = jnp.where(dmin[0, 0, mid] > kf, time_step * (qe + q_e), 0.0)
                kw = jnp.where(dmin[1, 0, mid] > kf, time_step * (qw + q_w), 0.0)
                kn = jnp.where(dmin[2, 0, mid] > kf, time_step * (qn[j, mid] + qn[j, 9 + r:25 + r]), 0.0)
                ks_ = jnp.where(dmin[3, 0, mid] > kf, time_step * (qs[j, mid] + qs[j, 7 + r:23 + r]), 0.0)
                for i, face in enumerate((ke, kw, kn, ks_)):
                    faces[k, 1 + i, rows] = face
                faces[k, 0, rows] = ct + (ke * (c_e - ct) + kw * (ct - c_w)) + (kn * (c_n - ct) + ks_ * (ct - c_s))
        return carry

    cut = 48
    lax.fori_loop(0, levels // group, functools.partial(level_group, 0, cut), 0)

    def wait_red(buf, n, sem):
        pltpu.make_async_copy(buf.at[pl.ds(0, n - 1)], buf.at[pl.ds(0, n - 1)], sem).wait()

    wait_red(red1, n1, red_sem.at[1])
    sums = red1[...]
    sums, rest = folded_rows((sums, jnp.zeros_like(sums)))
    mom2[...] = (sums + roll_lanes(rest, 8))[0:1]
    red2[pl.ds(me2, 1)] = mom2[...]
    group2(lambda d: send(mom2, red2.at[pl.ds(me2, 1)], red_sem.at[2], red_sem.at[3], d).start())

    below = sorted(range(ngy - 1), key=lambda g: -min(nx - 1 - g // nc, g // nc + 1))

    @pl.when(top)
    def _():
        whole = ngx * LANES
        start = (seam - LANES - gx * LANES + 2 * whole) % whole
        blk, off = start // LANES, start % LANES
        after = (blk + 1) % ngx

        pltpu.make_async_copy(foldz.at[pl.ds(0, nz - 1)], foldz.at[pl.ds(0, nz - 1)], fold_sem.at[3]).wait()
        fold_stage[0] = foldz[blk % nz]
        fold_stage[1] = foldz[after % nz]
        fold_y[pl.ds(y, 1)] = fold_stage[...][None]

        @pl.loop(1, ny)
        def _(j):
            p = ((y + j) % ny) * nz + z
            send(fold_stage, fold_y.at[y], fold_sem.at[4], fold_sem.at[5], (p, gy)).start()

        others = all2.at[pl.ds(0, (ngx - 1) * 16)]
        pltpu.make_async_copy(others, others, fold_sem.at[1]).wait()

        def exact_dot(a, o):
            return lax.dot(a, o, precision=lax.Precision.HIGHEST, preferred_element_type=f32)

        col = lax.broadcasted_iota(jnp.int32, (2 * LANES, LANES), 1)
        src = lax.broadcasted_iota(jnp.int32, (2 * LANES, LANES), 0)
        pick = (src == off + (LANES - 1) - col).astype(f32)
        block = lax.broadcasted_iota(jnp.int32, (ngx, ngx), 0)
        source = lax.broadcasted_iota(jnp.int32, (ngx, ngx), 1)
        order = ((block + source - blk - gx + 2 * ngx) % ngx == 0).astype(f32)
        fields = [[all2[pl.ds(8 * f + q, ngx, stride=16)] for q in range(2, 8)] for f in range(2)]
        mirror = [fields[f][q] for f in range(2) for q in (5, 4, 3)]
        turned = exact_dot(order, jnp.concatenate(mirror, axis=1))
        turned = [turned[:, i * LANES:(i + 1) * LANES] for i in range(6)]
        turned = [jnp.concatenate([t, pltpu.roll(t, 1, 0)], axis=1) for t in turned]
        mir[...] = exact_dot(jnp.concatenate(turned, axis=0), pick)
        mirror = [mir[i * ngx:(i + 1) * ngx] for i in range(6)]
        values, depth = fields[0] + mirror[:3], fields[1] + mirror[3:]
        spot = lax.broadcasted_iota(jnp.int32, (ngx, LANES), 1)

        def beside(t):
            ahead, behind = roll_lanes(t, LANES - 1), roll_lanes(t, 1)
            return (
                jnp.where(spot == LANES - 1, pltpu.roll(ahead, ngx - 1, 0), ahead),
                jnp.where(spot == 0, pltpu.roll(behind, 1, 0), behind),
            )

        least = {
            i: [jnp.minimum(depth[i], t) for t in (*beside(depth[i]), depth[i + 1], depth[i - 1])]
            for i in range(1, 8)
        }

        def step(f, rows):
            out = {}
            for i in rows:
                total = jnp.zeros_like(f[i])
                for d, t in zip(least[i], (*beside(f[i]), f[i + 1], f[i - 1])):
                    total = total + d * (f[i] - t)
                out[i] = damping * f[i] + (1.0 / levels) * total
            return out

        band1 = step(values, range(1, 8))
        band2 = step(band1, range(2, 7))
        band3 = step(band2, range(3, 6))
        band[...] = moment_row(
            [jnp.concatenate([f[i] for i in (3, 4, 5)], axis=0) for f in (values, band1, band2, band3)]
        )
        red2[n2:n2 + 1] = band[...]
        for g in below:
            send(band, red2.at[pl.ds(n2, 1)], band_sem.at[0], band_sem.at[1], (gx, g)).start()

        for i in range(6):
            f, row = i // 3, PAD + ROWS + i % 3
            mine, ahead, behind = [mir[pl.ds(i * ngx + (gx + d) % ngx, 1)] for d in (0, 1, ngx - 1)]
            plane[f, row:row + 1] = mine
            wide[f, row:row + 1] = jnp.where(lane8[0:1] < 64, ahead, behind)
        least_depths()
        apply(plane.at[0], wide.at[0], vec1)
        apply(vec1.at[0], vec1.at[1], vec2)

        pltpu.make_async_copy(fold_y.at[pl.ds(0, ny - 1)], fold_y.at[pl.ds(0, ny - 1)], fold_sem.at[5]).wait()
        got = exact_dot(jnp.concatenate([fold_y[blk // nz, 0], fold_y[after // nz, 1]], axis=1), pick)
        row = lax.broadcasted_iota(jnp.int32, (FOLD, LANES), 0)
        got_n[...] = jnp.where(row < levels, got, -got)

    lax.fori_loop(0, levels // group, functools.partial(level_group, cut, ROWS), 0)
    loads[7].wait()

    wait_red(red2, n2, red_sem.at[3])

    @pl.when(gy != ngy - 1)
    def _():
        one = red2.at[pl.ds(n2, 1)]
        pltpu.make_async_copy(one, one, band_sem.at[1]).wait()

    sums = red2[...]
    sums, rest = folded_rows((sums, jnp.zeros_like(sums)))
    rest = rest + pltpu.roll(sums, LANES - 8, 1)
    parts = []
    for part in (sums, rest):
        part = jnp.sum(jnp.where(lane8 == sub8, part, 0.0), axis=1, keepdims=True)
        parts.append(jnp.broadcast_to(part, (8, LANES)))
    tot[0:8], tot[8:16] = renormal(parts)
    pairs = [[jnp.broadcast_to(tot[i:i + 1], (8, LANES)) for i in (j, 8 + j)] for j in range(6)]
    m = [high for high, low in pairs]
    lo, hi = 0.0999, 8.2
    rho = m[1] / m[0]
    rho_parts = split(rho)

    def centred(a, o):
        p, rest = two_product(rho_parts, split(o[0]))
        return renormal(pair_add(a, (-p, -(rest + rho * o[1]))))

    s1 = [centred(pairs[j + 1], pairs[j]) for j in range(5)]
    n = [centred(s1[j + 1], s1[j])[0] for j in range(4)]
    n[0] = jnp.maximum(n[0], 0.0)

    def bounded(t, least, most):
        return jnp.where(t >= least, jnp.minimum(t, most), least)

    e1 = n[0] / m[0]
    rho1 = bounded(n[1] / n[0], lo, hi)
    p1 = bounded(rho1 - e1 / rho, lo, hi)
    k0 = n[2] - rho1 * n[1] - e1 * n[0]
    k1 = n[3] - 2.0 * rho1 * n[2] + rho1 * rho1 * n[1] - 2.0 * e1 * rho * n[0] + e1 * e1 * m[1]
    e2 = bounded(k0 / n[0], 0.0, 70.0)
    rho2 = bounded(k1 / k0, lo, hi)
    p2 = bounded(rho2 - e2 / p1, lo, hi)
    z0 = 1.0 / rho
    z1 = -z0 / p1
    y2 = -z1 / p2
    y1 = z1 - e2 / p1 * y2
    y0 = z0 - e1 / rho * y1
    a0 = y0 - rho * y1 + (rho1 * rho - e1) * y2
    a1 = y1 - (rho + rho1) * y2

    def spread(a, rows):
        return jnp.broadcast_to(a[0:1], (rows, LANES))

    rows80 = [spread(a, 80) for a in (a0, a1, y2)]
    h_mid = rows80[0] * plane[0, body] + rows80[1] * vec1[0, body] + rows80[2] * vec2[0, body]
    h_side = rows80[0] * wide[0, body] + rows80[1] * vec1[1, body] + rows80[2] * vec2[1, body]
    hv[0, body] = h_mid
    inner_mid, inner_side = h_mid[8:8 + ROWS], h_side[8:8 + ROWS]
    h_e, h_w = neighbours(inner_mid, inner_side, ROWS)
    hv[1, inner] = h_e - inner_mid
    hv[2, inner] = inner_mid - h_w
    hv[3, inner] = hv[0, PAD + 1:PAD + 1 + ROWS] - inner_mid
    hv[4, inner] = inner_mid - hv[0, PAD - 1:PAD - 1 + ROWS]
    hv[5, inner] = plane[1, inner]
    height = pltpu.make_async_copy(hv.at[0, inner], hadj_h, load_sem.at[0])
    height.start()

    def store_of(g):
        part = pl.ds(g * group, group)
        return pltpu.make_async_copy(outv.at[part], out_h.at[part], store_sem.at[g])

    def finish_levels(g, carry):
        for r in range(0, ROWS, 8):
            rows = slice(r, r + 8)
            hc, de, dw, dn, ds_, wet = [hv[i, PAD + r:PAD + r + 8] for i in range(6)]
            for k in [g * group + j for j in range(group)]:
                grown = (
                    jnp.where(wet > k.astype(f32), hc, 0.0)
                    + (faces[k, 1, rows] * de + faces[k, 2, rows] * dw)
                    + (faces[k, 3, rows] * dn + faces[k, 4, rows] * ds_)
                )
                outv[k, rows] = faces[k, 0, rows] + th_s[k] * grown
        store_of(g).start()
        return carry

    lax.fori_loop(0, levels // group, finish_levels, 0)

    for halo in halos:
        halo.wait_send()
    for edge in edges:
        edge.wait_send()
    wait_red(red1, n1, red_sem.at[0])
    wait_red(red2, n2, red_sem.at[2])

    @pl.when(top)
    def _():
        others = all2.at[pl.ds(0, (ngx - 1) * 16)]
        pltpu.make_async_copy(others, others, fold_sem.at[0]).wait()
        some = red2.at[pl.ds(0, ngy - 1)]
        pltpu.make_async_copy(some, some, band_sem.at[0]).wait()
        pltpu.make_async_copy(foldz.at[pl.ds(0, nz - 1)], foldz.at[pl.ds(0, nz - 1)], fold_sem.at[2]).wait()
        pltpu.make_async_copy(fold_y.at[pl.ds(0, ny - 1)], fold_y.at[pl.ds(0, ny - 1)], fold_sem.at[4]).wait()

    height.wait()
    for g in range(levels // group):
        store_of(g).wait()


def hand_on(levels, group, from_h, hfrom_h, out_h, hout_h, held, hheld, sem_in, sem_out):
    parts = [pl.ds(k, group) for k in range(0, levels, group)]
    last = len(parts)
    loads = [pltpu.make_async_copy(from_h.at[p], held.at[p], sem_in.at[i]) for i, p in enumerate(parts)]
    loads.append(pltpu.make_async_copy(hfrom_h, hheld, sem_in.at[last]))
    stores = [pltpu.make_async_copy(held.at[p], out_h.at[p], sem_out.at[i]) for i, p in enumerate(parts)]
    stores.append(pltpu.make_async_copy(hheld, hout_h, sem_out.at[last]))
    for load in loads:
        load.start()
    for load, store in zip(loads, stores):
        load.wait()
        store.start()
    for store in stores:
        store.wait()


def solution(mesh):
    ngx, ngy = mesh.shape["gx"], mesh.shape["gy"]
    nc = 2
    nx = ngy // nc
    ny = 4 if ngx == 32 else 2
    nz = ngx // ny

    def local(cot, b, u, v, kap, th, dep, fp):
        levels = cot.shape[0]
        f32 = jnp.float32

        def vmem(*shape, dtype=f32):
            return pltpu.VMEM(shape, dtype)

        cube = (levels, ROWS, LANES)
        group = 5 if levels % 5 == 0 else 1
        scratch = [
            pltpu.SMEM((levels,), f32), pltpu.SMEM((LANES,), jnp.int32),
            vmem(levels, 80, LANES), vmem(*cube), vmem(*cube), vmem(*cube),
            vmem(ROWS, LANES, dtype=jnp.int32),
            vmem(2, 96, LANES), vmem(2, 96, LANES),
            vmem(ROWS, LANES), vmem(2, 80, LANES), vmem(4, 2, 80, LANES),
            vmem(2, 96, LANES), vmem(2, 96, LANES),
            vmem(ROWS, LANES), vmem(2, ROWS, LANES),
            vmem(FOLD, LANES), vmem(FOLD, LANES), vmem(FOLD, LANES), vmem(FOLD, LANES),
            vmem(16, LANES), vmem(ngx * 16, LANES), vmem(ngx * 6, LANES),
            vmem(nz, FOLD, LANES), vmem(2, FOLD, LANES), vmem(ny, 2, FOLD, LANES),
            vmem(ROWS, LANES),
            vmem(group, 80, LANES), vmem(group, 80, LANES),
            vmem(levels, 5, ROWS, LANES), vmem(6, 96, LANES), vmem(*cube),
            vmem(1, LANES), vmem(max(8, nz * nc), LANES), vmem(1, LANES), vmem(8 if nx * ny < 8 else 32, LANES), vmem(1, LANES), vmem(16, LANES),
            pltpu.SemaphoreType.DMA((8,)), pltpu.SemaphoreType.DMA((levels // group,)),
            pltpu.SemaphoreType.DMA((12,)), pltpu.SemaphoreType.DMA((8,)),
            pltpu.SemaphoreType.DMA((4,)), pltpu.SemaphoreType.DMA((4,)),
            pltpu.SemaphoreType.DMA((6,)), pltpu.SemaphoreType.DMA((2,)),
            pltpu.SemaphoreType.REGULAR,
        ]
        hbm = pl.BlockSpec(memory_space=pltpu.HBM)
        limit = 62 * 1024 * 1024
        shapes = (jax.ShapeDtypeStruct(cube, f32), jax.ShapeDtypeStruct((ROWS, LANES), f32))
        results = pl.pallas_call(
            functools.partial(kernel, nz, ny, nc, nx, levels, group),
            out_shape=shapes,
            in_specs=[hbm] * 8,
            out_specs=(hbm, hbm),
            scratch_shapes=scratch,
            compiler_params=pltpu.CompilerParams(
                collective_id=0, has_side_effects=True, vmem_limit_bytes=limit
            ),
        )(cot, b, u, v, kap, th, dep, fp)
        parts = levels // group + 1
        return pl.pallas_call(
            functools.partial(hand_on, levels, group),
            out_shape=shapes,
            in_specs=[hbm] * 2,
            out_specs=(hbm, hbm),
            scratch_shapes=[
                vmem(*cube), vmem(ROWS, LANES),
                pltpu.SemaphoreType.DMA((parts,)), pltpu.SemaphoreType.DMA((parts,)),
            ],
            compiler_params=pltpu.CompilerParams(vmem_limit_bytes=limit),
        )(*results)

    in_specs = (
        P(None, "gy", "gx"), P("gy", "gx"), P(None, "gy", "gx"), P(None, "gy", "gx"),
        P(None, "gy", "gx"), P(), P("gy", "gx"), P("gx"),
    )
    out_specs = (P(None, "gy", "gx"), P("gy", "gx"))
    return jax.shard_map(local, mesh=mesh, in_specs=in_specs, out_specs=out_specs, check_vma=False)
```

```python
import functools

import jax
import jax.numpy as jnp
from jax import lax
from jax.experimental import pallas as pl
from jax.experimental.pallas import tpu as pltpu
from jax.sharding import PartitionSpec as P

MESH = pl.DeviceIdType.MESH
damping = 0.1
time_step = 0.3
ROWS = 64
LANES = 128
PAD = 16
FOLD = 56


def roll_lanes(x, shift):
    return pltpu.roll(x, shift, 1)


def two_sum(a, b):
    total = a + b
    t = total - a
    return total, (a - (total - t)) + (b - t)


def split(a):
    t = 4097.0 * a
    high = t - (t - a)
    return a, high, a - high


def two_product(a, b):
    (a, ah, al), (b, bh, bl) = a, b
    p = a * b
    return p, ((ah * bh - p) + ah * bl + al * bh) + al * bl


def pair_add(a, b):
    total, rest = two_sum(a[0], b[0])
    return total, rest + (a[1] + b[1])


def renormal(a):
    total = a[0] + a[1]
    return total, a[1] - (total - a[0])


def folded_rows(a):
    rows = a[0].shape[0]
    while rows > 8:
        keep = rows // 2 if rows % 16 == 0 else rows - 8
        rest = pair_add([t[:rows - keep] for t in a], [t[keep:] for t in a])
        a = [jnp.concatenate([t, o[rows - keep:keep]]) if 2 * keep > rows else t for t, o in zip(rest, a)]
        rows = keep
    for shift in (4, 2, 1):
        a = pair_add(a, [pltpu.roll(t, shift, 0) for t in a])
    return a


def kernel(
    nz, ny, nc, nx, levels, group,
    cot_h, b_h, u_h, v_h, k_h, th_h, dep_h, fp_h, out_h, hadj_h,
    th_s, fp_s, cot, u, v, kap, dint, plane, wide, pack2, got2, dmin, vec1, vec2,
    edge_ew, got_ew, edge_n, edge_s, got_n, got_s,
    top2, all2, mir, foldz, fold_stage, fold_y, sides,
    qn, qs, faces, hv,
    mom, red1, mom2, red2, band, tot,
    load_sem, send_sem, halo_sem, edge_sem, red_sem, fold_sem, band_sem, ready_sem,
):
    gx, gy = lax.axis_index("gx"), lax.axis_index("gy")
    ngx, ngy = ny * nz, nx * nc
    y, z, x, c = gx // nz, gx % nz, gy // nc, gy % nc
    top = gy == ngy - 1
    lane = lax.broadcasted_iota(jnp.int32, (ROWS, LANES), 1)
    lane80 = lax.broadcasted_iota(jnp.int32, (80, LANES), 1)
    f32 = jnp.float32

    def at(dx, dy):
        return (gx + dx + ngx) % ngx, (gy + dy + ngy) % ngy

    compass = [(1, 0), (-1, 0), (0, 1), (0, -1), (1, 1), (-1, 1), (1, -1), (-1, -1)]

    loads = [
        pltpu.make_async_copy(b_h, plane.at[0, pl.ds(PAD, ROWS)], load_sem.at[0]),
        pltpu.make_async_copy(dep_h, dint, load_sem.at[1]),
        pltpu.make_async_copy(cot_h, cot.at[:, pl.ds(8, ROWS)], load_sem.at[2]),
        pltpu.make_async_copy(u_h, u, load_sem.at[3]),
        pltpu.make_async_copy(k_h, kap, load_sem.at[4]),
        pltpu.make_async_copy(v_h, v, load_sem.at[5]),
        pltpu.make_async_copy(fp_h, fp_s, load_sem.at[6]),
        pltpu.make_async_copy(th_h, th_s, load_sem.at[7]),
    ]
    for load in loads:
        load.start()

    barrier = pltpu.get_barrier_semaphore()

    def greet(device):
        pl.semaphore_signal(barrier, inc=1, device_id=device, device_id_type=MESH)

    def far_first(n):
        return sorted(range(n), key=lambda d: (-min(d, n - d), d))

    far_y = [((y + d) % ny) * nz for d in far_first(ny)]
    def ready(device):
        pl.semaphore_signal(ready_sem, inc=1, device_id=device, device_id_type=MESH)

    n1, n2 = nz * nc, nx * ny
    me1, me2 = z * nc + c, y * nx + x
    far_z = [(z + d) % nz for d in far_first(nz)]
    far_yx = sorted(
        [(d, e) for d in range(ny) for e in range(nx)],
        key=lambda t: -min(t[0], ny - t[0]) - min(t[1], nx - t[1]),
    )

    def group1(act):
        for d, pz in zip(far_first(nz), far_z):
            for e in range(nc - 1, -1, -1):
                if (d, e) != (0, 0):
                    act((y * nz + pz, x * nc + (c + e) % nc))

    def group2(act):
        for d, e in far_yx:
            if (d, e) != (0, 0):
                act(((y + d) % ny * nz + z, (x + e) % nx * nc + c))

    def everyone_on_top(act):
        for pz in far_z[:-1]:
            for py in far_y:
                act((py + pz, gy))
        for py in far_y[:-1]:
            act((py + z, gy))

    for d in compass:
        greet(at(*d))
    group1(greet)
    group2(greet)

    zero8 = jnp.zeros((8, LANES), f32)
    for part, n in ((red1, n1), (red2, n2 + 1)):
        if n < part.shape[0]:
            part[n:] = jnp.zeros((part.shape[0] - n, LANES), f32)
    for f in range(2):
        for part in (plane, wide, vec1, vec2):
            part[f, 0:8] = zero8
            part[f, 88:96] = zero8
    loads[0].wait()
    loads[1].wait()
    depth_f = dint[...].astype(f32)
    plane[1, PAD:PAD + ROWS] = depth_f
    pack2[...] = jnp.where(
        (lane < 32) | (lane >= 96), plane[0, PAD:PAD + ROWS], roll_lanes(depth_f, 64)
    )

    pl.semaphore_wait(barrier, 8 + n1 - 1 + n2 - 1)

    def send(src, dst, sem_out, sem_in, device):
        copy = pltpu.make_async_remote_copy(
            src_ref=src, dst_ref=dst, send_sem=sem_out, recv_sem=sem_in,
            device_id=device, device_id_type=MESH,
        )
        return copy

    first, last = pl.ds(PAD, 8), pl.ds(PAD + ROWS - 8, 8)
    south, north = pl.ds(PAD - 8, 8), pl.ds(PAD + ROWS, 8)
    halos = []
    for i, (dx, dy) in enumerate(compass):
        if dx == 0:
            src = plane.at[:, last if dy == 1 else first]
            dst = plane.at[:, south if dy == 1 else north]
        else:
            side = 0 if dx == 1 else 1
            if dy == 0:
                src, dst = pack2, got2.at[side, pl.ds(8, ROWS)]
            elif dy == 1:
                src, dst = pack2.at[pl.ds(ROWS - 8, 8)], got2.at[side, pl.ds(0, 8)]
            else:
                src, dst = pack2.at[pl.ds(0, 8)], got2.at[side, pl.ds(ROWS + 8, 8)]
        halos.append(send(src, dst, send_sem.at[i], halo_sem.at[i], at(dx, dy)))

    for halo in halos:
        halo.start()

    @pl.when(c == nc - 1)
    def _():
        @pl.when(top)
        def _():
            for d in range(1, ny):
                ready(((y + d) % ny * nz + z, gy))

        @pl.when(x < nx - 1)
        def _():
            ready((gx, ngy - 1))

    for load in loads[2:6]:
        load.wait()
    half = jnp.where(lane < 64, 0.5, -0.5).astype(f32)
    edge_n[2 * levels:FOLD] = jnp.zeros((FOLD - 2 * levels, LANES), f32)
    edge_s[2 * levels:FOLD] = jnp.zeros((FOLD - 2 * levels, LANES), f32)

    def pack_levels(g, acc):
        place = lane >> 1
        for k in [g * group + j for j in range(group)]:
            face = 0.25 * u[k] + half * kap[k]
            acc = jnp.where(place == k, roll_lanes(cot[k, 8:8 + ROWS], 2 * k + 1), acc)
            acc = jnp.where(place == k + 32, roll_lanes(face, 2 * k + 65), acc)
            edge_n[pl.ds(k, 1)] = cot[k, 7 + ROWS:8 + ROWS]
            edge_s[pl.ds(k, 1)] = cot[k, 8:9]
            edge_n[pl.ds(levels + k, 1)] = 0.25 * v[k, ROWS - 1:ROWS] - 0.5 * kap[k, ROWS - 1:ROWS]
            edge_s[pl.ds(levels + k, 1)] = 0.25 * v[k, 0:1] + 0.5 * kap[k, 0:1]
        return acc

    edge_ew[...] = lax.fori_loop(0, levels // group, pack_levels, jnp.zeros((ROWS, LANES), f32))
    edges = [
        send(edge_ew, got_ew.at[0], send_sem.at[8], edge_sem.at[0], at(1, 0)),
        send(edge_ew, got_ew.at[1], send_sem.at[9], edge_sem.at[1], at(-1, 0)),
        send(edge_n, got_s, send_sem.at[10], edge_sem.at[2], at(0, 1)),
        send(edge_s, got_n, send_sem.at[11], edge_sem.at[3], at(0, -1)),
    ]
    for edge in edges:
        edge.start()

    @pl.when(top)
    def _():
        pl.semaphore_wait(ready_sem, ny - 1 + nx - 1)
        top2[0:8] = plane[0, last]
        top2[8:16] = plane[1, last]
        mine = pl.ds(pl.multiple_of(gx * 16, 16), 16)
        all2[mine] = top2[...]
        everyone_on_top(lambda d: send(top2, all2.at[mine], fold_sem.at[0], fold_sem.at[1], d).start())

        foldz[pl.ds(z, 1)] = edge_n[...][None]

        @pl.loop(1, nz)
        def _(j):
            p = y * nz + (z + j) % nz
            send(edge_n, foldz.at[z], fold_sem.at[2], fold_sem.at[3], (p, gy)).start()

    for halo in halos:
        halo.wait_recv()
    hw, he = got2[0], got2[1]
    wide[0, 8:88] = jnp.where(lane80 < 64, he, hw)
    wide[1, 8:88] = roll_lanes(jnp.where(lane80 < 64, hw, he), 64)

    loads[6].wait()
    seam = fp_s[0] + gx * LANES + 1

    @pl.when(gy == 0)
    def _():
        plane[1, 8:16] = zero8
        wide[1, 8:16] = zero8

    first_lane, last_lane = lane80 == 0, lane80 == LANES - 1

    def neighbours(mid, beside, rows):
        return [
            jnp.where(last_lane[:rows], roll_lanes(beside, LANES - 1), roll_lanes(mid, LANES - 1)),
            jnp.where(first_lane[:rows], roll_lanes(beside, 1), roll_lanes(mid, 1)),
        ]

    def both(mid, beside):
        return neighbours(mid, beside, 80), neighbours(beside, mid, 80)

    body, up, down = pl.ds(8, 80), pl.ds(9, 80), pl.ds(7, 80)

    def least_depths():
        dm, db = plane[1, body], wide[1, body]
        (d_e, d_w), (db_e, db_w) = both(dm, db)
        for i, (a, o) in enumerate(
            [(d_e, db_e), (d_w, db_w), (plane[1, up], wide[1, up]), (plane[1, down], wide[1, down])]
        ):
            dmin[i, 0] = jnp.minimum(dm, a)
            dmin[i, 1] = jnp.minimum(db, o)

    def apply(mid_ref, beside_ref, out_ref):
        mid, beside = mid_ref[body], beside_ref[body]
        (m_e, m_w), (s_e, s_w) = both(mid, beside)
        for i, (centre, nbrs) in enumerate(
            [
                (mid, (m_e, m_w, mid_ref[up], mid_ref[down])),
                (beside, (s_e, s_w, beside_ref[up], beside_ref[down])),
            ]
        ):
            total = jnp.zeros_like(centre)
            for j in range(4):
                total = total + dmin[j, i] * (centre - nbrs[j])
            out_ref[i, body] = damping * centre + (1.0 / levels) * total

    least_depths()
    apply(plane.at[0], wide.at[0], vec1)
    apply(vec1.at[0], vec1.at[1], vec2)
    inner = pl.ds(PAD, ROWS)
    mid2 = vec2[0, inner]
    m_e, m_w = neighbours(mid2, vec2[1, inner], ROWS)
    nbrs = (m_e, m_w, vec2[0, PAD + 1:PAD + 1 + ROWS], vec2[0, PAD - 1:PAD - 1 + ROWS])
    mid3 = jnp.zeros_like(mid2)
    for j in range(4):
        mid3 = mid3 + dmin[j, 0, 8:8 + ROWS] * (mid2 - nbrs[j])
    mid3 = damping * mid2 + (1.0 / levels) * mid3
    mid0, mid1 = plane[0, inner], vec1[0, inner]

    sub8 = lax.broadcasted_iota(jnp.int32, (8, LANES), 0)
    lane8 = lax.broadcasted_iota(jnp.int32, (8, LANES), 1)

    def moment_row(fields):
        f0, f1, f2, f3 = [split(f) for f in fields]
        for j, (a, o) in enumerate([(f0, f0), (f0, f1), (f1, f1), (f1, f2), (f2, f2), (f2, f3)]):
            high, low = folded_rows(two_product(a, o))
            tot[j:j + 1] = high[0:1]
            tot[8 + j:9 + j] = low[0:1]
        tot[6:8] = jnp.zeros((2, LANES), f32)
        tot[14:16] = jnp.zeros((2, LANES), f32)
        high, low = tot[0:8], tot[8:16]
        scale = 256.0 * jnp.max(jnp.abs(high), axis=1, keepdims=True)
        coarse = (high + scale) - scale
        rest = jnp.sum((high - coarse) + low, axis=1, keepdims=True)
        high, low = renormal((jnp.sum(coarse, axis=1, keepdims=True), rest))
        row = jnp.where(lane8 == sub8, high, 0.0) + jnp.where(lane8 == sub8 + 8, low, 0.0)
        return jnp.sum(row, axis=0, keepdims=True)

    apart = top & (lax.broadcasted_iota(jnp.int32, (ROWS, LANES), 0) >= ROWS - 3)
    mom[...] = moment_row([jnp.where(apart, 0.0, f) for f in (mid0, mid1, mid2, mid3)])

    red1[pl.ds(me1, 1)] = mom[...]
    group1(lambda d: send(mom, red1.at[pl.ds(me1, 1)], red_sem.at[0], red_sem.at[1], d).start())

    for edge in edges:
        edge.wait_recv()

    sides[...] = jnp.where((lane & 1) == 1, got_ew[1], got_ew[0])
    lane16 = lax.broadcasted_iota(jnp.int32, (16, LANES), 1)

    def level_group(begin, end, g, carry):
        ks = [g * group + j for j in range(group)]
        for j, k in enumerate(ks):
            cot[k, 7:8] = got_s[pl.ds(k, 1)]
            cot[k, 8 + ROWS:9 + ROWS] = got_n[pl.ds(k, 1)]
            qs[j, 7:8] = got_s[pl.ds(levels + k, 1)]
            qn[j, 8 + ROWS:9 + ROWS] = got_n[pl.ds(levels + k, 1)]
            for r in range(max(begin - 8, 0), min(end + 8, ROWS), 8):
                rows = slice(r, r + 8)
                vq, kq = 0.25 * v[k, rows], 0.5 * kap[k, rows]
                qn[j, 8 + r:16 + r] = vq + kq
                qs[j, 8 + r:16 + r] = vq - kq
        for r in range(begin, end, 16):
            for j, k in enumerate(ks):
                kf = k.astype(f32)
                rows, mid = slice(r, r + 16), slice(8 + r, 24 + r)
                ct = cot[k, mid]
                uq, kq = 0.25 * u[k, rows], 0.5 * kap[k, rows]
                qe, qw = uq + kq, uq - kq
                edge = sides[rows]
                ec = roll_lanes(edge, (LANES - 1) - 2 * k)
                eq = roll_lanes(edge, 63 - 2 * k)
                c_e = roll_lanes(jnp.where(lane16 == 0, ec, ct), LANES - 1)
                c_w = roll_lanes(jnp.where(lane16 == LANES - 1, ec, ct), 1)
                q_e = roll_lanes(jnp.where(lane16 == 0, eq, qe), LANES - 1)
                q_w = roll_lanes(jnp.where(lane16 == LANES - 1, eq, qw), 1)
                c_n, c_s = cot[k, 9 + r:25 + r], cot[k, 7 + r:23 + r]
                ke = jnp.where(dmin[0, 0, mid] > kf, time_step * (qe + q_e), 0.0)
                kw = jnp.where(dmin[1, 0, mid] > kf, time_step * (qw + q_w), 0.0)
                kn = jnp.where(dmin[2, 0, mid] > kf, time_step * (qn[j, mid] + qn[j, 9 + r:25 + r]), 0.0)
                ks_ = jnp.where(dmin[3, 0, mid] > kf, time_step * (qs[j, mid] + qs[j, 7 + r:23 + r]), 0.0)
                for i, face in enumerate((ke, kw, kn, ks_)):
                    faces[k, 1 + i, rows] = face
                faces[k, 0, rows] = ct + (ke * (c_e - ct) + kw * (ct - c_w)) + (kn * (c_n - ct) + ks_ * (ct - c_s))
        return carry

    cut = 48
    lax.fori_loop(0, levels // group, functools.partial(level_group, 0, cut), 0)

    def wait_red(buf, n, sem):
        pltpu.make_async_copy(buf.at[pl.ds(0, n - 1)], buf.at[pl.ds(0, n - 1)], sem).wait()

    wait_red(red1, n1, red_sem.at[1])
    sums = red1[...]
    sums, rest = folded_rows((sums, jnp.zeros_like(sums)))
    mom2[...] = (sums + roll_lanes(rest, 8))[0:1]
    red2[pl.ds(me2, 1)] = mom2[...]
    group2(lambda d: send(mom2, red2.at[pl.ds(me2, 1)], red_sem.at[2], red_sem.at[3], d).start())

    below = sorted(range(ngy - 1), key=lambda g: -min(nx - 1 - g // nc, g // nc + 1))

    @pl.when(top)
    def _():
        whole = ngx * LANES
        start = (seam - LANES - gx * LANES + 2 * whole) % whole
        blk, off = start // LANES, start % LANES
        after = (blk + 1) % ngx

        pltpu.make_async_copy(foldz.at[pl.ds(0, nz - 1)], foldz.at[pl.ds(0, nz - 1)], fold_sem.at[3]).wait()
        fold_stage[0] = foldz[blk % nz]
        fold_stage[1] = foldz[after % nz]
        fold_y[pl.ds(y, 1)] = fold_stage[...][None]

        @pl.loop(1, ny)
        def _(j):
            p = ((y + j) % ny) * nz + z
            send(fold_stage, fold_y.at[y], fold_sem.at[4], fold_sem.at[5], (p, gy)).start()

        others = all2.at[pl.ds(0, (ngx - 1) * 16)]
        pltpu.make_async_copy(others, others, fold_sem.at[1]).wait()

        def exact_dot(a, o):
            return lax.dot(a, o, precision=lax.Precision.HIGHEST, preferred_element_type=f32)

        col = lax.broadcasted_iota(jnp.int32, (2 * LANES, LANES), 1)
        src = lax.broadcasted_iota(jnp.int32, (2 * LANES, LANES), 0)
        pick = (src == off + (LANES - 1) - col).astype(f32)
        block = lax.broadcasted_iota(jnp.int32, (ngx, ngx), 0)
        source = lax.broadcasted_iota(jnp.int32, (ngx, ngx), 1)
        order = ((block + source - blk - gx + 2 * ngx) % ngx == 0).astype(f32)
        fields = [[all2[pl.ds(8 * f + q, ngx, stride=16)] for q in range(2, 8)] for f in range(2)]
        mirror = [fields[f][q] for f in range(2) for q in (5, 4, 3)]
        turned = exact_dot(order, jnp.concatenate(mirror, axis=1))
        turned = [turned[:, i * LANES:(i + 1) * LANES] for i in range(6)]
        turned = [jnp.concatenate([t, pltpu.roll(t, 1, 0)], axis=1) for t in turned]
        mir[...] = exact_dot(jnp.concatenate(turned, axis=0), pick)
        mirror = [mir[i * ngx:(i + 1) * ngx] for i in range(6)]
        values, depth = fields[0] + mirror[:3], fields[1] + mirror[3:]
        spot = lax.broadcasted_iota(jnp.int32, (ngx, LANES), 1)

        def beside(t):
            ahead, behind = roll_lanes(t, LANES - 1), roll_lanes(t, 1)
            return (
                jnp.where(spot == LANES - 1, pltpu.roll(ahead, ngx - 1, 0), ahead),
                jnp.where(spot == 0, pltpu.roll(behind, 1, 0), behind),
            )

        least = {
            i: [jnp.minimum(depth[i], t) for t in (*beside(depth[i]), depth[i + 1], depth[i - 1])]
            for i in range(1, 8)
        }

        def step(f, rows):
            out = {}
            for i in rows:
                total = jnp.zeros_like(f[i])
                for d, t in zip(least[i], (*beside(f[i]), f[i + 1], f[i - 1])):
                    total = total + d * (f[i] - t)
                out[i] = damping * f[i] + (1.0 / levels) * total
            return out

        band1 = step(values, range(1, 8))
        band2 = step(band1, range(2, 7))
        band3 = step(band2, range(3, 6))
        band[...] = moment_row(
            [jnp.concatenate([f[i] for i in (3, 4, 5)], axis=0) for f in (values, band1, band2, band3)]
        )
        red2[n2:n2 + 1] = band[...]
        for g in below:
            send(band, red2.at[pl.ds(n2, 1)], band_sem.at[0], band_sem.at[1], (gx, g)).start()

        for i in range(6):
            f, row = i // 3, PAD + ROWS + i % 3
            mine, ahead, behind = [mir[pl.ds(i * ngx + (gx + d) % ngx, 1)] for d in (0, 1, ngx - 1)]
            plane[f, row:row + 1] = mine
            wide[f, row:row + 1] = jnp.where(lane8[0:1] < 64, ahead, behind)
        least_depths()
        apply(plane.at[0], wide.at[0], vec1)
        apply(vec1.at[0], vec1.at[1], vec2)

        pltpu.make_async_copy(fold_y.at[pl.ds(0, ny - 1)], fold_y.at[pl.ds(0, ny - 1)], fold_sem.at[5]).wait()
        got = exact_dot(jnp.concatenate([fold_y[blk // nz, 0], fold_y[after // nz, 1]], axis=1), pick)
        row = lax.broadcasted_iota(jnp.int32, (FOLD, LANES), 0)
        got_n[...] = jnp.where(row < levels, got, -got)

    lax.fori_loop(0, levels // group, functools.partial(level_group, cut, ROWS), 0)
    loads[7].wait()

    wait_red(red2, n2, red_sem.at[3])

    @pl.when(gy != ngy - 1)
    def _():
        one = red2.at[pl.ds(n2, 1)]
        pltpu.make_async_copy(one, one, band_sem.at[1]).wait()

    sums = red2[...]
    sums, rest = folded_rows((sums, jnp.zeros_like(sums)))
    rest = rest + pltpu.roll(sums, LANES - 8, 1)
    parts = []
    for part in (sums, rest):
        part = jnp.sum(jnp.where(lane8 == sub8, part, 0.0), axis=1, keepdims=True)
        parts.append(jnp.broadcast_to(part, (8, LANES)))
    tot[0:8], tot[8:16] = renormal(parts)
    pairs = [[jnp.broadcast_to(tot[i:i + 1], (8, LANES)) for i in (j, 8 + j)] for j in range(6)]
    m = [high for high, low in pairs]
    lo, hi = 0.0999, 8.2
    rho = m[1] / m[0]
    rho_parts = split(rho)

    def centred(a, o):
        p, rest = two_product(rho_parts, split(o[0]))
        return renormal(pair_add(a, (-p, -(rest + rho * o[1]))))

    s1 = [centred(pairs[j + 1], pairs[j]) for j in range(5)]
    n = [centred(s1[j + 1], s1[j])[0] for j in range(4)]
    n[0] = jnp.maximum(n[0], 0.0)

    def bounded(t, least, most):
        return jnp.where(t >= least, jnp.minimum(t, most), least)

    e1 = n[0] / m[0]
    rho1 = bounded(n[1] / n[0], lo, hi)
    p1 = bounded(rho1 - e1 / rho, lo, hi)
    k0 = n[2] - rho1 * n[1] - e1 * n[0]
    k1 = n[3] - 2.0 * rho1 * n[2] + rho1 * rho1 * n[1] - 2.0 * e1 * rho * n[0] + e1 * e1 * m[1]
    e2 = bounded(k0 / n[0], 0.0, 70.0)
    rho2 = bounded(k1 / k0, lo, hi)
    p2 = bounded(rho2 - e2 / p1, lo, hi)
    z0 = 1.0 / rho
    z1 = -z0 / p1
    y2 = -z1 / p2
    y1 = z1 - e2 / p1 * y2
    y0 = z0 - e1 / rho * y1
    a0 = y0 - rho * y1 + (rho1 * rho - e1) * y2
    a1 = y1 - (rho + rho1) * y2

    def spread(a, rows):
        return jnp.broadcast_to(a[0:1], (rows, LANES))

    rows80 = [spread(a, 80) for a in (a0, a1, y2)]
    h_mid = rows80[0] * plane[0, body] + rows80[1] * vec1[0, body] + rows80[2] * vec2[0, body]
    h_side = rows80[0] * wide[0, body] + rows80[1] * vec1[1, body] + rows80[2] * vec2[1, body]
    hv[0, body] = h_mid
    inner_mid, inner_side = h_mid[8:8 + ROWS], h_side[8:8 + ROWS]
    h_e, h_w = neighbours(inner_mid, inner_side, ROWS)
    hv[1, inner] = h_e - inner_mid
    hv[2, inner] = inner_mid - h_w
    hv[3, inner] = hv[0, PAD + 1:PAD + 1 + ROWS] - inner_mid
    hv[4, inner] = inner_mid - hv[0, PAD - 1:PAD - 1 + ROWS]
    hv[5, inner] = plane[1, inner]
    hadj_h[...] = inner_mid

    def finish_levels(g, carry):
        for r in range(0, ROWS, 8):
            rows = slice(r, r + 8)
            hc, de, dw, dn, ds_, wet = [hv[i, PAD + r:PAD + r + 8] for i in range(6)]
            for k in [g * group + j for j in range(group)]:
                grown = (
                    jnp.where(wet > k.astype(f32), hc, 0.0)
                    + (faces[k, 1, rows] * de + faces[k, 2, rows] * dw)
                    + (faces[k, 3, rows] * dn + faces[k, 4, rows] * ds_)
                )
                out_h[k, rows] = faces[k, 0, rows] + th_s[k] * grown
        return carry

    lax.fori_loop(0, levels // group, finish_levels, 0)

    for halo in halos:
        halo.wait_send()
    for edge in edges:
        edge.wait_send()
    wait_red(red1, n1, red_sem.at[0])
    wait_red(red2, n2, red_sem.at[2])

    @pl.when(top)
    def _():
        others = all2.at[pl.ds(0, (ngx - 1) * 16)]
        pltpu.make_async_copy(others, others, fold_sem.at[0]).wait()
        some = red2.at[pl.ds(0, ngy - 1)]
        pltpu.make_async_copy(some, some, band_sem.at[0]).wait()
        pltpu.make_async_copy(foldz.at[pl.ds(0, nz - 1)], foldz.at[pl.ds(0, nz - 1)], fold_sem.at[2]).wait()
        pltpu.make_async_copy(fold_y.at[pl.ds(0, ny - 1)], fold_y.at[pl.ds(0, ny - 1)], fold_sem.at[4]).wait()


def hand_on(from_v, hfrom_v, out_h, hout_h, sem):
    stores = [
        pltpu.make_async_copy(from_v, out_h, sem.at[0]),
        pltpu.make_async_copy(hfrom_v, hout_h, sem.at[1]),
    ]
    for store in stores:
        store.start()
    for store in stores:
        store.wait()


def solution(mesh):
    ngx, ngy = mesh.shape["gx"], mesh.shape["gy"]
    nc = 2
    nx = ngy // nc
    ny = 4 if ngx == 32 else 2
    nz = ngx // ny

    def local(cot, b, u, v, kap, th, dep, fp):
        levels = cot.shape[0]
        f32 = jnp.float32

        def vmem(*shape, dtype=f32):
            return pltpu.VMEM(shape, dtype)

        cube = (levels, ROWS, LANES)
        group = 5 if levels % 5 == 0 else 1
        scratch = [
            pltpu.SMEM((levels,), f32), pltpu.SMEM((LANES,), jnp.int32),
            vmem(levels, 80, LANES), vmem(*cube), vmem(*cube), vmem(*cube),
            vmem(ROWS, LANES, dtype=jnp.int32),
            vmem(2, 96, LANES), vmem(2, 96, LANES),
            vmem(ROWS, LANES), vmem(2, 80, LANES), vmem(4, 2, 80, LANES),
            vmem(2, 96, LANES), vmem(2, 96, LANES),
            vmem(ROWS, LANES), vmem(2, ROWS, LANES),
            vmem(FOLD, LANES), vmem(FOLD, LANES), vmem(FOLD, LANES), vmem(FOLD, LANES),
            vmem(16, LANES), vmem(ngx * 16, LANES), vmem(ngx * 6, LANES),
            vmem(nz, FOLD, LANES), vmem(2, FOLD, LANES), vmem(ny, 2, FOLD, LANES),
            vmem(ROWS, LANES),
            vmem(group, 80, LANES), vmem(group, 80, LANES),
            vmem(levels, 5, ROWS, LANES), vmem(6, 96, LANES),
            vmem(1, LANES), vmem(max(8, nz * nc), LANES), vmem(1, LANES), vmem(8 if nx * ny < 8 else 32, LANES), vmem(1, LANES), vmem(16, LANES),
            pltpu.SemaphoreType.DMA((8,)),
            pltpu.SemaphoreType.DMA((12,)), pltpu.SemaphoreType.DMA((8,)),
            pltpu.SemaphoreType.DMA((4,)), pltpu.SemaphoreType.DMA((4,)),
            pltpu.SemaphoreType.DMA((6,)), pltpu.SemaphoreType.DMA((2,)),
            pltpu.SemaphoreType.REGULAR,
        ]
        hbm = pl.BlockSpec(memory_space=pltpu.HBM)
        limit = 48 * 1024 * 1024
        shapes = (jax.ShapeDtypeStruct(cube, f32), jax.ShapeDtypeStruct((ROWS, LANES), f32))
        inputs = [pltpu.with_memory_space_constraint(a, pltpu.HBM) for a in (cot, b, u, v, kap, th, dep, fp)]
        held = pl.BlockSpec(memory_space=pltpu.VMEM)
        results = pl.pallas_call(
            functools.partial(kernel, nz, ny, nc, nx, levels, group),
            out_shape=shapes,
            in_specs=[hbm] * 8,
            out_specs=(held, held),
            scratch_shapes=scratch,
            compiler_params=pltpu.CompilerParams(
                collective_id=0, has_side_effects=True, vmem_limit_bytes=limit
            ),
        )(*inputs)
        return pl.pallas_call(
            hand_on,
            out_shape=shapes,
            in_specs=[held, held],
            out_specs=(hbm, hbm),
            scratch_shapes=[pltpu.SemaphoreType.DMA((2,))],
            compiler_params=pltpu.CompilerParams(vmem_limit_bytes=limit),
        )(*results)

    in_specs = (
        P(None, "gy", "gx"), P("gy", "gx"), P(None, "gy", "gx"), P(None, "gy", "gx"),
        P(None, "gy", "gx"), P(), P("gy", "gx"), P("gx"),
    )
    out_specs = (P(None, "gy", "gx"), P("gy", "gx"))
    return jax.shard_map(local, mesh=mesh, in_specs=in_specs, out_specs=out_specs, check_vma=False)
```

```python
import functools

import jax
import jax.numpy as jnp
from jax import lax
from jax.experimental import pallas as pl
from jax.experimental.pallas import tpu as pltpu
from jax.sharding import PartitionSpec as P

MESH = pl.DeviceIdType.MESH
damping = 0.1
time_step = 0.3
ROWS = 64
LANES = 128
PAD = 16
FOLD = 56


def roll_lanes(x, shift):
    return pltpu.roll(x, shift, 1)


def two_sum(a, b):
    total = a + b
    t = total - a
    return total, (a - (total - t)) + (b - t)


def split(a):
    t = 4097.0 * a
    high = t - (t - a)
    return a, high, a - high


def two_product(a, b):
    (a, ah, al), (b, bh, bl) = a, b
    p = a * b
    return p, ((ah * bh - p) + ah * bl + al * bh) + al * bl


def pair_add(a, b):
    total, rest = two_sum(a[0], b[0])
    return total, rest + (a[1] + b[1])


def renormal(a):
    total = a[0] + a[1]
    return total, a[1] - (total - a[0])


def folded_rows(a):
    rows = a[0].shape[0]
    while rows > 8:
        keep = rows // 2 if rows % 16 == 0 else rows - 8
        rest = pair_add([t[:rows - keep] for t in a], [t[keep:] for t in a])
        a = [jnp.concatenate([t, o[rows - keep:keep]]) if 2 * keep > rows else t for t, o in zip(rest, a)]
        rows = keep
    for shift in (4, 2, 1):
        a = pair_add(a, [pltpu.roll(t, shift, 0) for t in a])
    return a


def kernel(
    nz, ny, nc, nx, levels, group,
    cot_h, b_h, u_h, v_h, k_h, th_h, dep_h, fp_h, faces, hv,
    th_s, fp_s, cot, u, v, kap, dint, plane, wide, pack2, got2, dmin, vec1, vec2,
    edge_ew, got_ew, edge_n, edge_s, got_n, got_s,
    top2, all2, mir, foldz, fold_stage, fold_y, sides,
    qn, qs, tall,
    mom, red1, mom2, red2, band, tot,
    load_sem, send_sem, halo_sem, edge_sem, red_sem, fold_sem, band_sem, ready_sem,
):
    gx, gy = lax.axis_index("gx"), lax.axis_index("gy")
    ngx, ngy = ny * nz, nx * nc
    y, z, x, c = gx // nz, gx % nz, gy // nc, gy % nc
    top = gy == ngy - 1
    lane = lax.broadcasted_iota(jnp.int32, (ROWS, LANES), 1)
    lane80 = lax.broadcasted_iota(jnp.int32, (80, LANES), 1)
    f32 = jnp.float32

    def at(dx, dy):
        return (gx + dx + ngx) % ngx, (gy + dy + ngy) % ngy

    compass = [(1, 0), (-1, 0), (0, 1), (0, -1), (1, 1), (-1, 1), (1, -1), (-1, -1)]

    loads = [
        pltpu.make_async_copy(b_h, plane.at[0, pl.ds(PAD, ROWS)], load_sem.at[0]),
        pltpu.make_async_copy(dep_h, dint, load_sem.at[1]),
        pltpu.make_async_copy(cot_h, cot.at[:, pl.ds(8, ROWS)], load_sem.at[2]),
        pltpu.make_async_copy(u_h, u, load_sem.at[3]),
        pltpu.make_async_copy(k_h, kap, load_sem.at[4]),
        pltpu.make_async_copy(v_h, v, load_sem.at[5]),
        pltpu.make_async_copy(fp_h, fp_s, load_sem.at[6]),
        pltpu.make_async_copy(th_h, th_s, load_sem.at[7]),
    ]
    for load in loads[:2]:
        load.start()

    barrier = pltpu.get_barrier_semaphore()

    def greet(device):
        pl.semaphore_signal(barrier, inc=1, device_id=device, device_id_type=MESH)

    def far_first(n):
        return sorted(range(n), key=lambda d: (-min(d, n - d), d))

    far_y = [((y + d) % ny) * nz for d in far_first(ny)]
    def ready(device):
        pl.semaphore_signal(ready_sem, inc=1, device_id=device, device_id_type=MESH)

    n1, n2 = nz * nc, nx * ny
    me1, me2 = z * nc + c, y * nx + x
    far_z = [(z + d) % nz for d in far_first(nz)]
    far_yx = sorted(
        [(d, e) for d in range(ny) for e in range(nx)],
        key=lambda t: -min(t[0], ny - t[0]) - min(t[1], nx - t[1]),
    )

    def group1(act):
        for d, pz in zip(far_first(nz), far_z):
            for e in range(nc - 1, -1, -1):
                if (d, e) != (0, 0):
                    act((y * nz + pz, x * nc + (c + e) % nc))

    def group2(act):
        for d, e in far_yx:
            if (d, e) != (0, 0):
                act(((y + d) % ny * nz + z, (x + e) % nx * nc + c))

    def everyone_on_top(act):
        for pz in far_z[:-1]:
            for py in far_y:
                act((py + pz, gy))
        for py in far_y[:-1]:
            act((py + z, gy))

    for d in compass:
        greet(at(*d))
    group1(greet)
    group2(greet)

    for load in loads[2:]:
        load.start()

    zero8 = jnp.zeros((8, LANES), f32)
    for part, n in ((red1, n1), (red2, n2 + 1)):
        if n < part.shape[0]:
            part[n:] = jnp.zeros((part.shape[0] - n, LANES), f32)
    for f in range(2):
        for part in (plane, wide, vec1, vec2):
            part[f, 0:8] = zero8
            part[f, 88:96] = zero8
    loads[0].wait()
    loads[1].wait()
    depth_f = dint[...].astype(f32)
    plane[1, PAD:PAD + ROWS] = depth_f
    lane16 = lax.broadcasted_iota(jnp.int32, (16, LANES), 1)
    packed = jnp.zeros((16, LANES), f32)
    for i in range(4):
        some = slice(PAD + 16 * i, PAD + 16 * i + 16)
        part = jnp.where(
            (lane16 & 31) < 20,
            roll_lanes(plane[0, some], 16 + 32 * i),
            roll_lanes(plane[1, some], (24 + 32 * i) % LANES),
        )
        packed = jnp.where(lane16 >> 5 == i, part, packed)
    pack2[...] = packed

    pl.semaphore_wait(barrier, 8 + n1 - 1 + n2 - 1)

    def send(src, dst, sem_out, sem_in, device):
        copy = pltpu.make_async_remote_copy(
            src_ref=src, dst_ref=dst, send_sem=sem_out, recv_sem=sem_in,
            device_id=device, device_id_type=MESH,
        )
        return copy

    first, last = pl.ds(PAD, 8), pl.ds(PAD + ROWS - 8, 8)
    south, north = pl.ds(PAD - 8, 8), pl.ds(PAD + ROWS, 8)
    halos = []
    for i, (dx, dy) in enumerate(compass):
        if dx == 0:
            src = plane.at[:, last if dy == 1 else first]
            dst = plane.at[:, south if dy == 1 else north]
        else:
            side = 0 if dx == 1 else 1
            if dy == 0:
                src, dst = pack2, got2.at[side, pl.ds(8, 16)]
            elif dy == 1:
                src, dst = pack2.at[pl.ds(8, 8)], got2.at[side, pl.ds(0, 8)]
            else:
                src, dst = pack2.at[pl.ds(0, 8)], got2.at[side, pl.ds(24, 8)]
        halos.append(send(src, dst, send_sem.at[i], halo_sem.at[i], at(dx, dy)))

    for halo in halos:
        halo.start()

    @pl.when(c == nc - 1)
    def _():
        @pl.when(top)
        def _():
            for d in range(1, ny):
                ready(((y + d) % ny * nz + z, gy))

        @pl.when(x < nx - 1)
        def _():
            ready((gx, ngy - 1))

    for load in loads[2:6]:
        load.wait()
    half = jnp.where(lane < 64, 0.5, -0.5).astype(f32)
    edge_n[2 * levels:FOLD] = jnp.zeros((FOLD - 2 * levels, LANES), f32)
    edge_s[2 * levels:FOLD] = jnp.zeros((FOLD - 2 * levels, LANES), f32)

    def pack_levels(g, acc):
        place = lane >> 1
        for k in [g * group + j for j in range(group)]:
            face = 0.25 * u[k] + half * kap[k]
            acc = jnp.where(place == k, roll_lanes(cot[k, 8:8 + ROWS], 2 * k + 1), acc)
            acc = jnp.where(place == k + 32, roll_lanes(face, 2 * k + 65), acc)
            edge_n[pl.ds(k, 1)] = cot[k, 7 + ROWS:8 + ROWS]
            edge_s[pl.ds(k, 1)] = cot[k, 8:9]
            edge_n[pl.ds(levels + k, 1)] = 0.25 * v[k, ROWS - 1:ROWS] - 0.5 * kap[k, ROWS - 1:ROWS]
            edge_s[pl.ds(levels + k, 1)] = 0.25 * v[k, 0:1] + 0.5 * kap[k, 0:1]
        return acc

    edge_ew[...] = lax.fori_loop(0, levels // group, pack_levels, jnp.zeros((ROWS, LANES), f32))
    edges = [
        send(edge_ew, got_ew.at[0], send_sem.at[8], edge_sem.at[0], at(1, 0)),
        send(edge_ew, got_ew.at[1], send_sem.at[9], edge_sem.at[1], at(-1, 0)),
        send(edge_n, got_s, send_sem.at[10], edge_sem.at[2], at(0, 1)),
        send(edge_s, got_n, send_sem.at[11], edge_sem.at[3], at(0, -1)),
    ]
    for edge in edges:
        edge.start()

    @pl.when(top)
    def _():
        pl.semaphore_wait(ready_sem, ny - 1 + nx - 1)
        top2[0:8] = plane[0, last]
        top2[8:16] = plane[1, last]
        mine = pl.ds(pl.multiple_of(gx * 16, 16), 16)
        all2[mine] = top2[...]
        everyone_on_top(lambda d: send(top2, all2.at[mine], fold_sem.at[0], fold_sem.at[1], d).start())

        foldz[pl.ds(z, 1)] = edge_n[...][None]

        @pl.loop(1, nz)
        def _(j):
            p = y * nz + (z + j) % nz
            send(edge_n, foldz.at[z], fold_sem.at[2], fold_sem.at[3], (p, gy)).start()

    for halo in halos:
        halo.wait_recv()
    for rows, to, i in [((0, 8), 8, 3), *(((8, 24), PAD + 16 * i, i) for i in range(4)), ((24, 32), PAD + ROWS, 0)]:
        west, east = got2[0, slice(*rows)], got2[1, slice(*rows)]
        spot = lane16[:rows[1] - rows[0]] & 31
        there = slice(to, to + rows[1] - rows[0])
        wide[0, there] = roll_lanes(jnp.where(spot < 16, west, east), (LANES - 16 - 32 * i) % LANES)
        wide[1, there] = roll_lanes(jnp.where(spot < 24, west, east), (LANES - 24 - 32 * i) % LANES)

    loads[6].wait()
    seam = fp_s[0] + gx * LANES + 1

    @pl.when(gy == 0)
    def _():
        plane[1, 8:16] = zero8
        wide[1, 8:16] = zero8

    first_lane, last_lane = lane80 == 0, lane80 == LANES - 1

    def neighbours(mid, beside, rows):
        return [
            jnp.where(last_lane[:rows], roll_lanes(beside, LANES - 1), roll_lanes(mid, LANES - 1)),
            jnp.where(first_lane[:rows], roll_lanes(beside, 1), roll_lanes(mid, 1)),
        ]

    def both(mid, beside):
        return neighbours(mid, beside, 80), neighbours(beside, mid, 80)

    body, up, down = pl.ds(8, 80), pl.ds(9, 80), pl.ds(7, 80)

    def least_depths():
        dm, db = plane[1, body], wide[1, body]
        (d_e, d_w), (db_e, db_w) = both(dm, db)
        for i, (a, o) in enumerate(
            [(d_e, db_e), (d_w, db_w), (plane[1, up], wide[1, up]), (plane[1, down], wide[1, down])]
        ):
            dmin[i, 0] = jnp.minimum(dm, a)
            dmin[i, 1] = jnp.minimum(db, o)

    def apply(mid_ref, beside_ref, out_ref):
        mid, beside = mid_ref[body], beside_ref[body]
        (m_e, m_w), (s_e, s_w) = both(mid, beside)
        for i, (centre, nbrs) in enumerate(
            [
                (mid, (m_e, m_w, mid_ref[up], mid_ref[down])),
                (beside, (s_e, s_w, beside_ref[up], beside_ref[down])),
            ]
        ):
            total = jnp.zeros_like(centre)
            for j in range(4):
                total = total + dmin[j, i] * (centre - nbrs[j])
            out_ref[i, body] = damping * centre + (1.0 / levels) * total

    least_depths()
    apply(plane.at[0], wide.at[0], vec1)
    apply(vec1.at[0], vec1.at[1], vec2)
    inner = pl.ds(PAD, ROWS)
    mid2 = vec2[0, inner]
    m_e, m_w = neighbours(mid2, vec2[1, inner], ROWS)
    nbrs = (m_e, m_w, vec2[0, PAD + 1:PAD + 1 + ROWS], vec2[0, PAD - 1:PAD - 1 + ROWS])
    mid3 = jnp.zeros_like(mid2)
    for j in range(4):
        mid3 = mid3 + dmin[j, 0, 8:8 + ROWS] * (mid2 - nbrs[j])
    mid3 = damping * mid2 + (1.0 / levels) * mid3
    mid0, mid1 = plane[0, inner], vec1[0, inner]

    sub8 = lax.broadcasted_iota(jnp.int32, (8, LANES), 0)
    lane8 = lax.broadcasted_iota(jnp.int32, (8, LANES), 1)

    def moment_row(fields):
        f0, f1, f2, f3 = [split(f) for f in fields]
        for j, (a, o) in enumerate([(f0, f0), (f0, f1), (f1, f1), (f1, f2), (f2, f2), (f2, f3)]):
            high, low = folded_rows(two_product(a, o))
            tot[j:j + 1] = high[0:1]
            tot[8 + j:9 + j] = low[0:1]
        tot[6:8] = jnp.zeros((2, LANES), f32)
        tot[14:16] = jnp.zeros((2, LANES), f32)
        high, low = tot[0:8], tot[8:16]
        scale = 256.0 * jnp.max(jnp.abs(high), axis=1, keepdims=True)
        coarse = (high + scale) - scale
        rest = jnp.sum((high - coarse) + low, axis=1, keepdims=True)
        high, low = renormal((jnp.sum(coarse, axis=1, keepdims=True), rest))
        row = jnp.where(lane8 == sub8, high, 0.0) + jnp.where(lane8 == sub8 + 8, low, 0.0)
        return jnp.sum(row, axis=0, keepdims=True)

    apart = top & (lax.broadcasted_iota(jnp.int32, (ROWS, LANES), 0) >= ROWS - 3)
    mom[...] = moment_row([jnp.where(apart, 0.0, f) for f in (mid0, mid1, mid2, mid3)])

    red1[pl.ds(me1, 1)] = mom[...]
    group1(lambda d: send(mom, red1.at[pl.ds(me1, 1)], red_sem.at[0], red_sem.at[1], d).start())

    for edge in edges:
        edge.wait_recv()

    sides[...] = jnp.where((lane & 1) == 1, got_ew[1], got_ew[0])

    def level_group(begin, end, g, carry):
        ks = [g * group + j for j in range(group)]
        for j, k in enumerate(ks):
            cot[k, 7:8] = got_s[pl.ds(k, 1)]
            cot[k, 8 + ROWS:9 + ROWS] = got_n[pl.ds(k, 1)]
            qs[j, 7:8] = got_s[pl.ds(levels + k, 1)]
            qn[j, 8 + ROWS:9 + ROWS] = got_n[pl.ds(levels + k, 1)]
            for r in range(max(begin - 8, 0), min(end + 8, ROWS), 8):
                rows = slice(r, r + 8)
                vq, kq = 0.25 * v[k, rows], 0.5 * kap[k, rows]
                qn[j, 8 + r:16 + r] = vq + kq
                qs[j, 8 + r:16 + r] = vq - kq
        for r in range(begin, end, 16):
            for j, k in enumerate(ks):
                kf = k.astype(f32)
                rows, mid = slice(r, r + 16), slice(8 + r, 24 + r)
                ct = cot[k, mid]
                uq, kq = 0.25 * u[k, rows], 0.5 * kap[k, rows]
                qe, qw = uq + kq, uq - kq
                edge = sides[rows]
                ec = roll_lanes(edge, (LANES - 1) - 2 * k)
                eq = roll_lanes(edge, 63 - 2 * k)
                c_e = roll_lanes(jnp.where(lane16 == 0, ec, ct), LANES - 1)
                c_w = roll_lanes(jnp.where(lane16 == LANES - 1, ec, ct), 1)
                q_e = roll_lanes(jnp.where(lane16 == 0, eq, qe), LANES - 1)
                q_w = roll_lanes(jnp.where(lane16 == LANES - 1, eq, qw), 1)
                c_n, c_s = cot[k, 9 + r:25 + r], cot[k, 7 + r:23 + r]
                ke = jnp.where(dmin[0, 0, mid] > kf, time_step * (qe + q_e), 0.0)
                kw = jnp.where(dmin[1, 0, mid] > kf, time_step * (qw + q_w), 0.0)
                kn = jnp.where(dmin[2, 0, mid] > kf, time_step * (qn[j, mid] + qn[j, 9 + r:25 + r]), 0.0)
                ks_ = jnp.where(dmin[3, 0, mid] > kf, time_step * (qs[j, mid] + qs[j, 7 + r:23 + r]), 0.0)
                heavy = th_s[k]
                for i, face in enumerate((ke, kw, kn, ks_)):
                    faces[k, 1 + i, rows] = heavy * face
                faces[k, 5, rows] = jnp.where(plane[1, PAD + r:PAD + r + 16] > kf, heavy, 0.0)
                faces[k, 0, rows] = ct + (ke * (c_e - ct) + kw * (ct - c_w)) + (kn * (c_n - ct) + ks_ * (ct - c_s))
        return carry

    loads[7].wait()
    cut = 48
    lax.fori_loop(0, levels // group, functools.partial(level_group, 0, cut), 0)

    def wait_red(buf, n, sem):
        pltpu.make_async_copy(buf.at[pl.ds(0, n - 1)], buf.at[pl.ds(0, n - 1)], sem).wait()

    wait_red(red1, n1, red_sem.at[1])
    sums = red1[...]
    sums, rest = folded_rows((sums, jnp.zeros_like(sums)))
    mom2[...] = (sums + roll_lanes(rest, 8))[0:1]
    red2[pl.ds(me2, 1)] = mom2[...]
    group2(lambda d: send(mom2, red2.at[pl.ds(me2, 1)], red_sem.at[2], red_sem.at[3], d).start())

    below = sorted(range(ngy - 1), key=lambda g: -min(nx - 1 - g // nc, g // nc + 1))

    @pl.when(top)
    def _():
        whole = ngx * LANES
        start = (seam - LANES - gx * LANES + 2 * whole) % whole
        blk, off = start // LANES, start % LANES
        after = (blk + 1) % ngx

        pltpu.make_async_copy(foldz.at[pl.ds(0, nz - 1)], foldz.at[pl.ds(0, nz - 1)], fold_sem.at[3]).wait()
        fold_stage[0] = foldz[blk % nz]
        fold_stage[1] = foldz[after % nz]
        fold_y[pl.ds(y, 1)] = fold_stage[...][None]

        @pl.loop(1, ny)
        def _(j):
            p = ((y + j) % ny) * nz + z
            send(fold_stage, fold_y.at[y], fold_sem.at[4], fold_sem.at[5], (p, gy)).start()

        others = all2.at[pl.ds(0, (ngx - 1) * 16)]
        pltpu.make_async_copy(others, others, fold_sem.at[1]).wait()

        def exact_dot(a, o):
            return lax.dot(a, o, precision=lax.Precision.HIGHEST, preferred_element_type=f32)

        col = lax.broadcasted_iota(jnp.int32, (2 * LANES, LANES), 1)
        src = lax.broadcasted_iota(jnp.int32, (2 * LANES, LANES), 0)
        pick = (src == off + (LANES - 1) - col).astype(f32)
        block = lax.broadcasted_iota(jnp.int32, (ngx, ngx), 0)
        source = lax.broadcasted_iota(jnp.int32, (ngx, ngx), 1)
        order = ((block + source - blk - gx + 2 * ngx) % ngx == 0).astype(f32)
        fields = [[all2[pl.ds(8 * f + q, ngx, stride=16)] for q in range(2, 8)] for f in range(2)]
        mirror = [fields[f][q] for f in range(2) for q in (5, 4, 3)]
        turned = exact_dot(order, jnp.concatenate(mirror, axis=1))
        turned = [turned[:, i * LANES:(i + 1) * LANES] for i in range(6)]
        turned = [jnp.concatenate([t, pltpu.roll(t, 1, 0)], axis=1) for t in turned]
        mir[...] = exact_dot(jnp.concatenate(turned, axis=0), pick)
        mirror = [mir[i * ngx:(i + 1) * ngx] for i in range(6)]
        values, depth = fields[0] + mirror[:3], fields[1] + mirror[3:]
        spot = lax.broadcasted_iota(jnp.int32, (ngx, LANES), 1)

        def beside(t):
            ahead, behind = roll_lanes(t, LANES - 1), roll_lanes(t, 1)
            return (
                jnp.where(spot == LANES - 1, pltpu.roll(ahead, ngx - 1, 0), ahead),
                jnp.where(spot == 0, pltpu.roll(behind, 1, 0), behind),
            )

        least = {
            i: [jnp.minimum(depth[i], t) for t in (*beside(depth[i]), depth[i + 1], depth[i - 1])]
            for i in range(1, 8)
        }

        def step(f, rows):
            out = {}
            for i in rows:
                total = jnp.zeros_like(f[i])
                for d, t in zip(least[i], (*beside(f[i]), f[i + 1], f[i - 1])):
                    total = total + d * (f[i] - t)
                out[i] = damping * f[i] + (1.0 / levels) * total
            return out

        band1 = step(values, range(1, 8))
        band2 = step(band1, range(2, 7))
        band3 = step(band2, range(3, 6))
        band[...] = moment_row(
            [jnp.concatenate([f[i] for i in (3, 4, 5)], axis=0) for f in (values, band1, band2, band3)]
        )
        red2[n2:n2 + 1] = band[...]
        for g in below:
            send(band, red2.at[pl.ds(n2, 1)], band_sem.at[0], band_sem.at[1], (gx, g)).start()

        for i in range(6):
            f, row = i // 3, PAD + ROWS + i % 3
            mine, ahead, behind = [mir[pl.ds(i * ngx + (gx + d) % ngx, 1)] for d in (0, 1, ngx - 1)]
            plane[f, row:row + 1] = mine
            wide[f, row:row + 1] = jnp.where(lane8[0:1] < 64, ahead, behind)
        least_depths()
        apply(plane.at[0], wide.at[0], vec1)
        apply(vec1.at[0], vec1.at[1], vec2)

        pltpu.make_async_copy(fold_y.at[pl.ds(0, ny - 1)], fold_y.at[pl.ds(0, ny - 1)], fold_sem.at[5]).wait()
        got = exact_dot(jnp.concatenate([fold_y[blk // nz, 0], fold_y[after // nz, 1]], axis=1), pick)
        row = lax.broadcasted_iota(jnp.int32, (FOLD, LANES), 0)
        got_n[...] = jnp.where(row < levels, got, -got)

    lax.fori_loop(0, levels // group, functools.partial(level_group, cut, ROWS), 0)
    wait_red(red2, n2, red_sem.at[3])

    @pl.when(gy != ngy - 1)
    def _():
        one = red2.at[pl.ds(n2, 1)]
        pltpu.make_async_copy(one, one, band_sem.at[1]).wait()

    sums = red2[...]
    sums, rest = folded_rows((sums, jnp.zeros_like(sums)))
    rest = rest + pltpu.roll(sums, LANES - 8, 1)
    parts = []
    for part in (sums, rest):
        part = jnp.sum(jnp.where(lane8 == sub8, part, 0.0), axis=1, keepdims=True)
        parts.append(jnp.broadcast_to(part, (8, LANES)))
    tot[0:8], tot[8:16] = renormal(parts)
    pairs = [[jnp.broadcast_to(tot[i:i + 1], (8, LANES)) for i in (j, 8 + j)] for j in range(6)]
    m = [high for high, low in pairs]
    lo, hi = 0.0999, 8.2
    rho = m[1] / m[0]
    rho_parts = split(rho)

    def centred(a, o):
        p, rest = two_product(rho_parts, split(o[0]))
        return renormal(pair_add(a, (-p, -(rest + rho * o[1]))))

    s1 = [centred(pairs[j + 1], pairs[j]) for j in range(5)]
    n = [centred(s1[j + 1], s1[j])[0] for j in range(4)]
    n[0] = jnp.maximum(n[0], 0.0)

    def bounded(t, least, most):
        return jnp.where(t >= least, jnp.minimum(t, most), least)

    e1 = n[0] / m[0]
    rho1 = bounded(n[1] / n[0], lo, hi)
    p1 = bounded(rho1 - e1 / rho, lo, hi)
    k0 = n[2] - rho1 * n[1] - e1 * n[0]
    k1 = n[3] - 2.0 * rho1 * n[2] + rho1 * rho1 * n[1] - 2.0 * e1 * rho * n[0] + e1 * e1 * m[1]
    e2 = bounded(k0 / n[0], 0.0, 70.0)
    rho2 = bounded(k1 / k0, lo, hi)
    p2 = bounded(rho2 - e2 / p1, lo, hi)
    z0 = 1.0 / rho
    z1 = -z0 / p1
    y2 = -z1 / p2
    y1 = z1 - e2 / p1 * y2
    y0 = z0 - e1 / rho * y1
    a0 = y0 - rho * y1 + (rho1 * rho - e1) * y2
    a1 = y1 - (rho + rho1) * y2

    def spread(a, rows):
        return jnp.broadcast_to(a[0:1], (rows, LANES))

    rows80 = [spread(a, 80) for a in (a0, a1, y2)]
    h_mid = rows80[0] * plane[0, body] + rows80[1] * vec1[0, body] + rows80[2] * vec2[0, body]
    h_side = rows80[0] * wide[0, body] + rows80[1] * vec1[1, body] + rows80[2] * vec2[1, body]
    tall[body] = h_mid
    inner_mid, inner_side = h_mid[8:8 + ROWS], h_side[8:8 + ROWS]
    h_e, h_w = neighbours(inner_mid, inner_side, ROWS)
    hv[0] = inner_mid
    hv[1] = h_e - inner_mid
    hv[2] = inner_mid - h_w
    hv[3] = tall[PAD + 1:PAD + 1 + ROWS] - inner_mid
    hv[4] = inner_mid - tall[PAD - 1:PAD - 1 + ROWS]

    for halo in halos:
        halo.wait_send()
    for edge in edges:
        edge.wait_send()
    wait_red(red1, n1, red_sem.at[0])
    wait_red(red2, n2, red_sem.at[2])

    @pl.when(top)
    def _():
        others = all2.at[pl.ds(0, (ngx - 1) * 16)]
        pltpu.make_async_copy(others, others, fold_sem.at[0]).wait()
        some = red2.at[pl.ds(0, ngy - 1)]
        pltpu.make_async_copy(some, some, band_sem.at[0]).wait()
        pltpu.make_async_copy(foldz.at[pl.ds(0, nz - 1)], foldz.at[pl.ds(0, nz - 1)], fold_sem.at[2]).wait()
        pltpu.make_async_copy(fold_y.at[pl.ds(0, ny - 1)], fold_y.at[pl.ds(0, ny - 1)], fold_sem.at[4]).wait()


def finish(levels, group, faces, hv, out_h, hadj_h, out, sem):
    stores = [pltpu.make_async_copy(hv.at[0], hadj_h, sem.at[0])]
    stores[0].start()
    for g in range(levels // group):
        for r in range(0, ROWS, 8):
            rows = slice(r, r + 8)
            hc, de, dw, dn, ds_ = [hv[i, rows] for i in range(5)]
            for k in range(g * group, (g + 1) * group):
                out[k, rows] = (
                    (faces[k, 0, rows] + faces[k, 5, rows] * hc)
                    + (faces[k, 1, rows] * de + faces[k, 2, rows] * dw)
                    + (faces[k, 3, rows] * dn + faces[k, 4, rows] * ds_)
                )
        part = pl.ds(g * group, group)
        stores.append(pltpu.make_async_copy(out.at[part], out_h.at[part], sem.at[1 + g]))
        stores[-1].start()
    for store in stores:
        store.wait()


def solution(mesh):
    ngx, ngy = mesh.shape["gx"], mesh.shape["gy"]
    nc = 2
    nx = ngy // nc
    ny = 4 if ngx == 32 else 2
    nz = ngx // ny

    def local(cot, b, u, v, kap, th, dep, fp):
        levels = cot.shape[0]
        f32 = jnp.float32

        def vmem(*shape, dtype=f32):
            return pltpu.VMEM(shape, dtype)

        cube = (levels, ROWS, LANES)
        group = 5 if levels % 5 == 0 else 1
        scratch = [
            pltpu.SMEM((levels,), f32), pltpu.SMEM((LANES,), jnp.int32),
            vmem(levels, 80, LANES), vmem(*cube), vmem(*cube), vmem(*cube),
            vmem(ROWS, LANES, dtype=jnp.int32),
            vmem(2, 96, LANES), vmem(2, 96, LANES),
            vmem(16, LANES), vmem(2, 32, LANES), vmem(4, 2, 80, LANES),
            vmem(2, 96, LANES), vmem(2, 96, LANES),
            vmem(ROWS, LANES), vmem(2, ROWS, LANES),
            vmem(FOLD, LANES), vmem(FOLD, LANES), vmem(FOLD, LANES), vmem(FOLD, LANES),
            vmem(16, LANES), vmem(ngx * 16, LANES), vmem(ngx * 6, LANES),
            vmem(nz, FOLD, LANES), vmem(2, FOLD, LANES), vmem(ny, 2, FOLD, LANES),
            vmem(ROWS, LANES),
            vmem(group, 80, LANES), vmem(group, 80, LANES),
            vmem(96, LANES),
            vmem(1, LANES), vmem(max(8, nz * nc), LANES), vmem(1, LANES), vmem(8 if nx * ny < 8 else 32, LANES), vmem(1, LANES), vmem(16, LANES),
            pltpu.SemaphoreType.DMA((8,)),
            pltpu.SemaphoreType.DMA((12,)), pltpu.SemaphoreType.DMA((8,)),
            pltpu.SemaphoreType.DMA((4,)), pltpu.SemaphoreType.DMA((4,)),
            pltpu.SemaphoreType.DMA((6,)), pltpu.SemaphoreType.DMA((2,)),
            pltpu.SemaphoreType.REGULAR,
        ]
        hbm = pl.BlockSpec(memory_space=pltpu.HBM)
        limit = 48 * 1024 * 1024
        shapes = (jax.ShapeDtypeStruct(cube, f32), jax.ShapeDtypeStruct((ROWS, LANES), f32))
        inputs = [pltpu.with_memory_space_constraint(a, pltpu.HBM) for a in (cot, b, u, v, kap, th, dep, fp)]
        held = pl.BlockSpec(memory_space=pltpu.VMEM)
        results = pl.pallas_call(
            functools.partial(kernel, nz, ny, nc, nx, levels, group),
            out_shape=(
                jax.ShapeDtypeStruct((levels, 6, ROWS, LANES), f32),
                jax.ShapeDtypeStruct((5, ROWS, LANES), f32),
            ),
            in_specs=[hbm] * 8,
            out_specs=(held, held),
            scratch_shapes=scratch,
            compiler_params=pltpu.CompilerParams(
                collective_id=0, has_side_effects=True, vmem_limit_bytes=limit
            ),
        )(*inputs)
        return pl.pallas_call(
            functools.partial(finish, levels, group),
            out_shape=shapes,
            in_specs=[held, held],
            out_specs=(hbm, hbm),
            scratch_shapes=[vmem(*cube), pltpu.SemaphoreType.DMA((1 + levels // group,))],
            compiler_params=pltpu.CompilerParams(vmem_limit_bytes=limit),
        )(*results)

    in_specs = (
        P(None, "gy", "gx"), P("gy", "gx"), P(None, "gy", "gx"), P(None, "gy", "gx"),
        P(None, "gy", "gx"), P(), P("gy", "gx"), P("gx"),
    )
    out_specs = (P(None, "gy", "gx"), P("gy", "gx"))
    return jax.shard_map(local, mesh=mesh, in_specs=in_specs, out_specs=out_specs, check_vma=False)
```

```python
import functools

import jax
import jax.numpy as jnp
from jax import lax
from jax.experimental import pallas as pl
from jax.experimental.pallas import tpu as pltpu
from jax.sharding import PartitionSpec as P

MESH = pl.DeviceIdType.MESH
damping = 0.1
time_step = 0.3
ROWS = 64
LANES = 128
PAD = 16
FOLD = 56


def roll_lanes(x, shift):
    return pltpu.roll(x, shift, 1)


def two_sum(a, b):
    total = a + b
    t = total - a
    return total, (a - (total - t)) + (b - t)


def split(a):
    t = 4097.0 * a
    high = t - (t - a)
    return a, high, a - high


def two_product(a, b):
    (a, ah, al), (b, bh, bl) = a, b
    p = a * b
    return p, ((ah * bh - p) + ah * bl + al * bh) + al * bl


def pair_add(a, b):
    total, rest = two_sum(a[0], b[0])
    return total, rest + (a[1] + b[1])


def renormal(a):
    total = a[0] + a[1]
    return total, a[1] - (total - a[0])


def folded_rows(a):
    rows = a[0].shape[0]
    while rows > 8:
        keep = rows // 2 if rows % 16 == 0 else rows - 8
        rest = pair_add([t[:rows - keep] for t in a], [t[keep:] for t in a])
        a = [jnp.concatenate([t, o[rows - keep:keep]]) if 2 * keep > rows else t for t, o in zip(rest, a)]
        rows = keep
    for shift in (4, 2, 1):
        a = pair_add(a, [pltpu.roll(t, shift, 0) for t in a])
    return a


def kernel(
    nz, ny, nc, nx, levels, group,
    cot_h, b_h, u_h, v_h, k_h, th_h, dep_h, fp_h, faces, hv,
    th_s, fp_s, cot, u, v, kap, dint, plane, wide, pack2, got2, dmin, vec1, vec2,
    edge_ew, got_ew, edge_n, edge_s, got_n, got_s,
    top2, all2, mir, foldz, fold_stage, fold_y, sides,
    qn, qs, tall,
    mom, red1, mom2, red2, band, tot,
    load_sem, send_sem, halo_sem, edge_sem, red_sem, fold_sem, band_sem, ready_sem,
):
    gx, gy = lax.axis_index("gx"), lax.axis_index("gy")
    ngx, ngy = ny * nz, nx * nc
    y, z, x, c = gx // nz, gx % nz, gy // nc, gy % nc
    top = gy == ngy - 1
    lane = lax.broadcasted_iota(jnp.int32, (ROWS, LANES), 1)
    lane80 = lax.broadcasted_iota(jnp.int32, (80, LANES), 1)
    f32 = jnp.float32

    def at(dx, dy):
        return (gx + dx + ngx) % ngx, (gy + dy + ngy) % ngy

    compass = [(1, 0), (-1, 0), (0, 1), (0, -1), (1, 1), (-1, 1), (1, -1), (-1, -1)]

    loads = [
        pltpu.make_async_copy(b_h, plane.at[0, pl.ds(PAD, ROWS)], load_sem.at[0]),
        pltpu.make_async_copy(dep_h, dint, load_sem.at[1]),
        pltpu.make_async_copy(cot_h, cot.at[:, pl.ds(8, ROWS)], load_sem.at[2]),
        pltpu.make_async_copy(u_h, u, load_sem.at[3]),
        pltpu.make_async_copy(k_h, kap, load_sem.at[4]),
        pltpu.make_async_copy(v_h, v, load_sem.at[5]),
        pltpu.make_async_copy(fp_h, fp_s, load_sem.at[6]),
        pltpu.make_async_copy(th_h, th_s, load_sem.at[7]),
    ]
    for load in loads[:2]:
        load.start()

    barrier = pltpu.get_barrier_semaphore()

    def greet(device):
        pl.semaphore_signal(barrier, inc=1, device_id=device, device_id_type=MESH)

    def far_first(n):
        return sorted(range(n), key=lambda d: (-min(d, n - d), d))

    far_y = [((y + d) % ny) * nz for d in far_first(ny)]
    def ready(device):
        pl.semaphore_signal(ready_sem, inc=1, device_id=device, device_id_type=MESH)

    n1, n2 = nz * nc, nx * ny
    me1, me2 = z * nc + c, y * nx + x
    far_z = [(z + d) % nz for d in far_first(nz)]
    far_yx = sorted(
        [(d, e) for d in range(ny) for e in range(nx)],
        key=lambda t: -min(t[0], ny - t[0]) - min(t[1], nx - t[1]),
    )

    def group1(act):
        for d, pz in zip(far_first(nz), far_z):
            for e in range(nc - 1, -1, -1):
                if (d, e) != (0, 0):
                    act((y * nz + pz, x * nc + (c + e) % nc))

    def group2(act):
        for d, e in far_yx:
            if (d, e) != (0, 0):
                act(((y + d) % ny * nz + z, (x + e) % nx * nc + c))

    group1, group2, n1, n2, me1, me2 = group2, group1, n2, n1, me2, me1

    def everyone_on_top(act):
        for pz in far_z[:-1]:
            for py in far_y:
                act((py + pz, gy))
        for py in far_y[:-1]:
            act((py + z, gy))

    group1(greet)
    group2(greet)
    for d in compass:
        greet(at(*d))

    for load in loads[2:]:
        load.start()

    zero8 = jnp.zeros((8, LANES), f32)
    for part, n in ((red1, n1), (red2, n2 + 1)):
        if n < part.shape[0]:
            part[n:] = jnp.zeros((part.shape[0] - n, LANES), f32)
    for f in range(2):
        for part in (plane, wide, vec1, vec2):
            part[f, 0:8] = zero8
            part[f, 88:96] = zero8
    loads[0].wait()
    loads[1].wait()
    depth_f = dint[...].astype(f32)
    plane[1, PAD:PAD + ROWS] = depth_f
    lane16 = lax.broadcasted_iota(jnp.int32, (16, LANES), 1)
    packed = jnp.zeros((16, LANES), f32)
    for i in range(4):
        some = slice(PAD + 16 * i, PAD + 16 * i + 16)
        part = jnp.where(
            (lane16 & 31) < 20,
            roll_lanes(plane[0, some], 16 + 32 * i),
            roll_lanes(plane[1, some], (24 + 32 * i) % LANES),
        )
        packed = jnp.where(lane16 >> 5 == i, part, packed)
    pack2[...] = packed

    pl.semaphore_wait(barrier, 8 + n1 - 1 + n2 - 1)

    def send(src, dst, sem_out, sem_in, device):
        copy = pltpu.make_async_remote_copy(
            src_ref=src, dst_ref=dst, send_sem=sem_out, recv_sem=sem_in,
            device_id=device, device_id_type=MESH,
        )
        return copy

    first, last = pl.ds(PAD, 8), pl.ds(PAD + ROWS - 8, 8)
    south, north = pl.ds(PAD - 8, 8), pl.ds(PAD + ROWS, 8)
    halos = []
    for i, (dx, dy) in enumerate(compass):
        if dx == 0:
            src = plane.at[:, last if dy == 1 else first]
            dst = plane.at[:, south if dy == 1 else north]
        else:
            side = 0 if dx == 1 else 1
            if dy == 0:
                src, dst = pack2, got2.at[side, pl.ds(8, 16)]
            elif dy == 1:
                src, dst = pack2.at[pl.ds(8, 8)], got2.at[side, pl.ds(0, 8)]
            else:
                src, dst = pack2.at[pl.ds(0, 8)], got2.at[side, pl.ds(24, 8)]
        halos.append(send(src, dst, send_sem.at[i], halo_sem.at[i], at(dx, dy)))

    for halo in halos:
        halo.start()

    @pl.when(c == nc - 1)
    def _():
        @pl.when(top)
        def _():
            for d in range(1, ny):
                ready(((y + d) % ny * nz + z, gy))

        @pl.when(x < nx - 1)
        def _():
            ready((gx, ngy - 1))

    for load in loads[2:6]:
        load.wait()
    half = jnp.where(lane < 64, 0.5, -0.5).astype(f32)
    edge_n[2 * levels:FOLD] = jnp.zeros((FOLD - 2 * levels, LANES), f32)
    edge_s[2 * levels:FOLD] = jnp.zeros((FOLD - 2 * levels, LANES), f32)

    def pack_levels(g, acc):
        place = lane >> 1
        for k in [g * group + j for j in range(group)]:
            face = 0.25 * u[k] + half * kap[k]
            acc = jnp.where(place == k, roll_lanes(cot[k, 8:8 + ROWS], 2 * k + 1), acc)
            acc = jnp.where(place == k + 32, roll_lanes(face, 2 * k + 65), acc)
            edge_n[pl.ds(k, 1)] = cot[k, 7 + ROWS:8 + ROWS]
            edge_s[pl.ds(k, 1)] = cot[k, 8:9]
            edge_n[pl.ds(levels + k, 1)] = 0.25 * v[k, ROWS - 1:ROWS] - 0.5 * kap[k, ROWS - 1:ROWS]
            edge_s[pl.ds(levels + k, 1)] = 0.25 * v[k, 0:1] + 0.5 * kap[k, 0:1]
        return acc

    edge_ew[...] = lax.fori_loop(0, levels // group, pack_levels, jnp.zeros((ROWS, LANES), f32))
    edges = [
        send(edge_ew, got_ew.at[0], send_sem.at[8], edge_sem.at[0], at(1, 0)),
        send(edge_ew, got_ew.at[1], send_sem.at[9], edge_sem.at[1], at(-1, 0)),
        send(edge_n, got_s, send_sem.at[10], edge_sem.at[2], at(0, 1)),
        send(edge_s, got_n, send_sem.at[11], edge_sem.at[3], at(0, -1)),
    ]
    for edge in edges:
        edge.start()

    @pl.when(top)
    def _():
        pl.semaphore_wait(ready_sem, ny - 1 + nx - 1)
        top2[0:8] = plane[0, last]
        top2[8:16] = plane[1, last]
        mine = pl.ds(pl.multiple_of(gx * 16, 16), 16)
        all2[mine] = top2[...]
        everyone_on_top(lambda d: send(top2, all2.at[mine], fold_sem.at[0], fold_sem.at[1], d).start())

        foldz[pl.ds(z, 1)] = edge_n[...][None]

        @pl.loop(1, nz)
        def _(j):
            p = y * nz + (z + j) % nz
            send(edge_n, foldz.at[z], fold_sem.at[2], fold_sem.at[3], (p, gy)).start()

    for halo in halos:
        halo.wait_recv()
    for rows, to, i in [((0, 8), 8, 3), *(((8, 24), PAD + 16 * i, i) for i in range(4)), ((24, 32), PAD + ROWS, 0)]:
        west, east = got2[0, slice(*rows)], got2[1, slice(*rows)]
        spot = lane16[:rows[1] - rows[0]] & 31
        there = slice(to, to + rows[1] - rows[0])
        wide[0, there] = roll_lanes(jnp.where(spot < 16, west, east), (LANES - 16 - 32 * i) % LANES)
        wide[1, there] = roll_lanes(jnp.where(spot < 24, west, east), (LANES - 24 - 32 * i) % LANES)

    loads[6].wait()
    seam = fp_s[0] + gx * LANES + 1

    @pl.when(gy == 0)
    def _():
        plane[1, 8:16] = zero8
        wide[1, 8:16] = zero8

    first_lane, last_lane = lane80 == 0, lane80 == LANES - 1

    def neighbours(mid, beside, rows):
        return [
            jnp.where(last_lane[:rows], roll_lanes(beside, LANES - 1), roll_lanes(mid, LANES - 1)),
            jnp.where(first_lane[:rows], roll_lanes(beside, 1), roll_lanes(mid, 1)),
        ]

    def both(mid, beside):
        return neighbours(mid, beside, 80), neighbours(beside, mid, 80)

    body, up, down = pl.ds(8, 80), pl.ds(9, 80), pl.ds(7, 80)

    def least_depths():
        dm, db = plane[1, body], wide[1, body]
        (d_e, d_w), (db_e, db_w) = both(dm, db)
        for i, (a, o) in enumerate(
            [(d_e, db_e), (d_w, db_w), (plane[1, up], wide[1, up]), (plane[1, down], wide[1, down])]
        ):
            dmin[i, 0] = jnp.minimum(dm, a)
            dmin[i, 1] = jnp.minimum(db, o)

    def apply(mid_ref, beside_ref, out_ref):
        mid, beside = mid_ref[body], beside_ref[body]
        (m_e, m_w), (s_e, s_w) = both(mid, beside)
        for i, (centre, nbrs) in enumerate(
            [
                (mid, (m_e, m_w, mid_ref[up], mid_ref[down])),
                (beside, (s_e, s_w, beside_ref[up], beside_ref[down])),
            ]
        ):
            total = jnp.zeros_like(centre)
            for j in range(4):
                total = total + dmin[j, i] * (centre - nbrs[j])
            out_ref[i, body] = damping * centre + (1.0 / levels) * total

    least_depths()
    apply(plane.at[0], wide.at[0], vec1)
    apply(vec1.at[0], vec1.at[1], vec2)
    inner = pl.ds(PAD, ROWS)
    mid2 = vec2[0, inner]
    m_e, m_w = neighbours(mid2, vec2[1, inner], ROWS)
    nbrs = (m_e, m_w, vec2[0, PAD + 1:PAD + 1 + ROWS], vec2[0, PAD - 1:PAD - 1 + ROWS])
    mid3 = jnp.zeros_like(mid2)
    for j in range(4):
        mid3 = mid3 + dmin[j, 0, 8:8 + ROWS] * (mid2 - nbrs[j])
    mid3 = damping * mid2 + (1.0 / levels) * mid3
    mid0, mid1 = plane[0, inner], vec1[0, inner]

    sub8 = lax.broadcasted_iota(jnp.int32, (8, LANES), 0)
    lane8 = lax.broadcasted_iota(jnp.int32, (8, LANES), 1)

    def moment_row(fields):
        f0, f1, f2, f3 = [split(f) for f in fields]
        for j, (a, o) in enumerate([(f0, f0), (f0, f1), (f1, f1), (f1, f2), (f2, f2), (f2, f3)]):
            high, low = folded_rows(two_product(a, o))
            tot[j:j + 1] = high[0:1]
            tot[8 + j:9 + j] = low[0:1]
        tot[6:8] = jnp.zeros((2, LANES), f32)
        tot[14:16] = jnp.zeros((2, LANES), f32)
        high, low = tot[0:8], tot[8:16]
        scale = 256.0 * jnp.max(jnp.abs(high), axis=1, keepdims=True)
        coarse = (high + scale) - scale
        rest = jnp.sum((high - coarse) + low, axis=1, keepdims=True)
        high, low = renormal((jnp.sum(coarse, axis=1, keepdims=True), rest))
        row = jnp.where(lane8 == sub8, high, 0.0) + jnp.where(lane8 == sub8 + 8, low, 0.0)
        return jnp.sum(row, axis=0, keepdims=True)

    apart = top & (lax.broadcasted_iota(jnp.int32, (ROWS, LANES), 0) >= ROWS - 3)
    mom[...] = moment_row([jnp.where(apart, 0.0, f) for f in (mid0, mid1, mid2, mid3)])

    red1[pl.ds(me1, 1)] = mom[...]
    group1(lambda d: send(mom, red1.at[pl.ds(me1, 1)], red_sem.at[0], red_sem.at[1], d).start())

    for edge in edges:
        edge.wait_recv()

    sides[...] = jnp.where((lane & 1) == 1, got_ew[1], got_ew[0])

    def level_group(begin, end, g, carry):
        ks = [g * group + j for j in range(group)]
        for j, k in enumerate(ks):
            cot[k, 7:8] = got_s[pl.ds(k, 1)]
            cot[k, 8 + ROWS:9 + ROWS] = got_n[pl.ds(k, 1)]
            qs[j, 7:8] = got_s[pl.ds(levels + k, 1)]
            qn[j, 8 + ROWS:9 + ROWS] = got_n[pl.ds(levels + k, 1)]
            for r in range(max(begin - 8, 0), min(end + 8, ROWS), 8):
                rows = slice(r, r + 8)
                vq, kq = 0.25 * v[k, rows], 0.5 * kap[k, rows]
                qn[j, 8 + r:16 + r] = vq + kq
                qs[j, 8 + r:16 + r] = vq - kq
        for r in range(begin, end, 16):
            for j, k in enumerate(ks):
                kf = k.astype(f32)
                rows, mid = slice(r, r + 16), slice(8 + r, 24 + r)
                ct = cot[k, mid]
                uq, kq = 0.25 * u[k, rows], 0.5 * kap[k, rows]
                qe, qw = uq + kq, uq - kq
                edge = sides[rows]
                ec = roll_lanes(edge, (LANES - 1) - 2 * k)
                eq = roll_lanes(edge, 63 - 2 * k)
                c_e = roll_lanes(jnp.where(lane16 == 0, ec, ct), LANES - 1)
                c_w = roll_lanes(jnp.where(lane16 == LANES - 1, ec, ct), 1)
                q_e = roll_lanes(jnp.where(lane16 == 0, eq, qe), LANES - 1)
                q_w = roll_lanes(jnp.where(lane16 == LANES - 1, eq, qw), 1)
                c_n, c_s = cot[k, 9 + r:25 + r], cot[k, 7 + r:23 + r]
                ke = jnp.where(dmin[0, 0, mid] > kf, time_step * (qe + q_e), 0.0)
                kw = jnp.where(dmin[1, 0, mid] > kf, time_step * (qw + q_w), 0.0)
                kn = jnp.where(dmin[2, 0, mid] > kf, time_step * (qn[j, mid] + qn[j, 9 + r:25 + r]), 0.0)
                ks_ = jnp.where(dmin[3, 0, mid] > kf, time_step * (qs[j, mid] + qs[j, 7 + r:23 + r]), 0.0)
                heavy = th_s[k]
                for i, face in enumerate((ke, kw, kn, ks_)):
                    faces[k, 1 + i, rows] = heavy * face
                faces[k, 5, rows] = jnp.where(plane[1, PAD + r:PAD + r + 16] > kf, heavy, 0.0)
                faces[k, 0, rows] = ct + (ke * (c_e - ct) + kw * (ct - c_w)) + (kn * (c_n - ct) + ks_ * (ct - c_s))
        return carry

    loads[7].wait()
    cut = 48
    lax.fori_loop(0, levels // group, functools.partial(level_group, 0, cut), 0)

    def wait_red(buf, n, sem):
        pltpu.make_async_copy(buf.at[pl.ds(0, n - 1)], buf.at[pl.ds(0, n - 1)], sem).wait()

    wait_red(red1, n1, red_sem.at[1])
    sums = red1[...]
    sums, rest = folded_rows((sums, jnp.zeros_like(sums)))
    mom2[...] = (sums + roll_lanes(rest, 8))[0:1]
    red2[pl.ds(me2, 1)] = mom2[...]
    group2(lambda d: send(mom2, red2.at[pl.ds(me2, 1)], red_sem.at[2], red_sem.at[3], d).start())

    below = sorted(range(ngy - 1), key=lambda g: -min(nx - 1 - g // nc, g // nc + 1))

    @pl.when(top)
    def _():
        whole = ngx * LANES
        start = (seam - LANES - gx * LANES + 2 * whole) % whole
        blk, off = start // LANES, start % LANES
        after = (blk + 1) % ngx

        pltpu.make_async_copy(foldz.at[pl.ds(0, nz - 1)], foldz.at[pl.ds(0, nz - 1)], fold_sem.at[3]).wait()
        fold_stage[0] = foldz[blk % nz]
        fold_stage[1] = foldz[after % nz]
        fold_y[pl.ds(y, 1)] = fold_stage[...][None]

        @pl.loop(1, ny)
        def _(j):
            p = ((y + j) % ny) * nz + z
            send(fold_stage, fold_y.at[y], fold_sem.at[4], fold_sem.at[5], (p, gy)).start()

        others = all2.at[pl.ds(0, (ngx - 1) * 16)]
        pltpu.make_async_copy(others, others, fold_sem.at[1]).wait()

        def exact_dot(a, o):
            return lax.dot(a, o, precision=lax.Precision.HIGHEST, preferred_element_type=f32)

        col = lax.broadcasted_iota(jnp.int32, (2 * LANES, LANES), 1)
        src = lax.broadcasted_iota(jnp.int32, (2 * LANES, LANES), 0)
        pick = (src == off + (LANES - 1) - col).astype(f32)
        block = lax.broadcasted_iota(jnp.int32, (ngx, ngx), 0)
        source = lax.broadcasted_iota(jnp.int32, (ngx, ngx), 1)
        order = ((block + source - blk - gx + 2 * ngx) % ngx == 0).astype(f32)
        fields = [[all2[pl.ds(8 * f + q, ngx, stride=16)] for q in range(2, 8)] for f in range(2)]
        mirror = [fields[f][q] for f in range(2) for q in (5, 4, 3)]
        turned = exact_dot(order, jnp.concatenate(mirror, axis=1))
        turned = [turned[:, i * LANES:(i + 1) * LANES] for i in range(6)]
        turned = [jnp.concatenate([t, pltpu.roll(t, 1, 0)], axis=1) for t in turned]
        mir[...] = exact_dot(jnp.concatenate(turned, axis=0), pick)
        mirror = [mir[i * ngx:(i + 1) * ngx] for i in range(6)]
        values, depth = fields[0] + mirror[:3], fields[1] + mirror[3:]
        spot = lax.broadcasted_iota(jnp.int32, (ngx, LANES), 1)

        def beside(t):
            ahead, behind = roll_lanes(t, LANES - 1), roll_lanes(t, 1)
            return (
                jnp.where(spot == LANES - 1, pltpu.roll(ahead, ngx - 1, 0), ahead),
                jnp.where(spot == 0, pltpu.roll(behind, 1, 0), behind),
            )

        least = {
            i: [jnp.minimum(depth[i], t) for t in (*beside(depth[i]), depth[i + 1], depth[i - 1])]
            for i in range(1, 8)
        }

        def step(f, rows):
            out = {}
            for i in rows:
                total = jnp.zeros_like(f[i])
                for d, t in zip(least[i], (*beside(f[i]), f[i + 1], f[i - 1])):
                    total = total + d * (f[i] - t)
                out[i] = damping * f[i] + (1.0 / levels) * total
            return out

        band1 = step(values, range(1, 8))
        band2 = step(band1, range(2, 7))
        band3 = step(band2, range(3, 6))
        band[...] = moment_row(
            [jnp.concatenate([f[i] for i in (3, 4, 5)], axis=0) for f in (values, band1, band2, band3)]
        )
        red2[n2:n2 + 1] = band[...]
        for g in below:
            send(band, red2.at[pl.ds(n2, 1)], band_sem.at[0], band_sem.at[1], (gx, g)).start()

        for i in range(6):
            f, row = i // 3, PAD + ROWS + i % 3
            mine, ahead, behind = [mir[pl.ds(i * ngx + (gx + d) % ngx, 1)] for d in (0, 1, ngx - 1)]
            plane[f, row:row + 1] = mine
            wide[f, row:row + 1] = jnp.where(lane8[0:1] < 64, ahead, behind)
        least_depths()
        apply(plane.at[0], wide.at[0], vec1)
        apply(vec1.at[0], vec1.at[1], vec2)

        pltpu.make_async_copy(fold_y.at[pl.ds(0, ny - 1)], fold_y.at[pl.ds(0, ny - 1)], fold_sem.at[5]).wait()
        got = exact_dot(jnp.concatenate([fold_y[blk // nz, 0], fold_y[after // nz, 1]], axis=1), pick)
        row = lax.broadcasted_iota(jnp.int32, (FOLD, LANES), 0)
        got_n[...] = jnp.where(row < levels, got, -got)

    lax.fori_loop(0, levels // group, functools.partial(level_group, cut, ROWS), 0)
    wait_red(red2, n2, red_sem.at[3])

    @pl.when(gy != ngy - 1)
    def _():
        one = red2.at[pl.ds(n2, 1)]
        pltpu.make_async_copy(one, one, band_sem.at[1]).wait()

    sums = red2[...]
    sums, rest = folded_rows((sums, jnp.zeros_like(sums)))
    rest = rest + pltpu.roll(sums, LANES - 8, 1)
    parts = []
    for part in (sums, rest):
        part = jnp.sum(jnp.where(lane8 == sub8, part, 0.0), axis=1, keepdims=True)
        parts.append(jnp.broadcast_to(part, (8, LANES)))
    tot[0:8], tot[8:16] = renormal(parts)
    pairs = [[jnp.broadcast_to(tot[i:i + 1], (8, LANES)) for i in (j, 8 + j)] for j in range(6)]
    m = [high for high, low in pairs]
    lo, hi = 0.0999, 8.2
    rho = m[1] / m[0]
    rho_parts = split(rho)

    def centred(a, o):
        p, rest = two_product(rho_parts, split(o[0]))
        return renormal(pair_add(a, (-p, -(rest + rho * o[1]))))

    s1 = [centred(pairs[j + 1], pairs[j]) for j in range(5)]
    n = [centred(s1[j + 1], s1[j])[0] for j in range(4)]
    n[0] = jnp.maximum(n[0], 0.0)

    def bounded(t, least, most):
        return jnp.where(t >= least, jnp.minimum(t, most), least)

    e1 = n[0] / m[0]
    rho1 = bounded(n[1] / n[0], lo, hi)
    p1 = bounded(rho1 - e1 / rho, lo, hi)
    k0 = n[2] - rho1 * n[1] - e1 * n[0]
    k1 = n[3] - 2.0 * rho1 * n[2] + rho1 * rho1 * n[1] - 2.0 * e1 * rho * n[0] + e1 * e1 * m[1]
    e2 = bounded(k0 / n[0], 0.0, 70.0)
    rho2 = bounded(k1 / k0, lo, hi)
    p2 = bounded(rho2 - e2 / p1, lo, hi)
    z0 = 1.0 / rho
    z1 = -z0 / p1
    y2 = -z1 / p2
    y1 = z1 - e2 / p1 * y2
    y0 = z0 - e1 / rho * y1
    a0 = y0 - rho * y1 + (rho1 * rho - e1) * y2
    a1 = y1 - (rho + rho1) * y2

    def spread(a, rows):
        return jnp.broadcast_to(a[0:1], (rows, LANES))

    rows80 = [spread(a, 80) for a in (a0, a1, y2)]
    h_mid = rows80[0] * plane[0, body] + rows80[1] * vec1[0, body] + rows80[2] * vec2[0, body]
    h_side = rows80[0] * wide[0, body] + rows80[1] * vec1[1, body] + rows80[2] * vec2[1, body]
    tall[body] = h_mid
    inner_mid, inner_side = h_mid[8:8 + ROWS], h_side[8:8 + ROWS]
    h_e, h_w = neighbours(inner_mid, inner_side, ROWS)
    hv[0] = inner_mid
    hv[1] = h_e - inner_mid
    hv[2] = inner_mid - h_w
    hv[3] = tall[PAD + 1:PAD + 1 + ROWS] - inner_mid
    hv[4] = inner_mid - tall[PAD - 1:PAD - 1 + ROWS]

    for halo in halos:
        halo.wait_send()
    for edge in edges:
        edge.wait_send()
    wait_red(red1, n1, red_sem.at[0])
    wait_red(red2, n2, red_sem.at[2])

    @pl.when(top)
    def _():
        others = all2.at[pl.ds(0, (ngx - 1) * 16)]
        pltpu.make_async_copy(others, others, fold_sem.at[0]).wait()
        some = red2.at[pl.ds(0, ngy - 1)]
        pltpu.make_async_copy(some, some, band_sem.at[0]).wait()
        pltpu.make_async_copy(foldz.at[pl.ds(0, nz - 1)], foldz.at[pl.ds(0, nz - 1)], fold_sem.at[2]).wait()
        pltpu.make_async_copy(fold_y.at[pl.ds(0, ny - 1)], fold_y.at[pl.ds(0, ny - 1)], fold_sem.at[4]).wait()


def finish(levels, group, faces, hv, out_h, hadj_h, out, sem):
    stores = [pltpu.make_async_copy(hv.at[0], hadj_h, sem.at[0])]
    stores[0].start()
    for g in range(levels // group):
        for r in range(0, ROWS, 8):
            rows = slice(r, r + 8)
            hc, de, dw, dn, ds_ = [hv[i, rows] for i in range(5)]
            for k in range(g * group, (g + 1) * group):
                out[k, rows] = (
                    (faces[k, 0, rows] + faces[k, 5, rows] * hc)
                    + (faces[k, 1, rows] * de + faces[k, 2, rows] * dw)
                    + (faces[k, 3, rows] * dn + faces[k, 4, rows] * ds_)
                )
        part = pl.ds(g * group, group)
        stores.append(pltpu.make_async_copy(out.at[part], out_h.at[part], sem.at[1 + g]))
        stores[-1].start()
    for store in stores:
        store.wait()


def solution(mesh):
    ngx, ngy = mesh.shape["gx"], mesh.shape["gy"]
    nc = 2
    nx = ngy // nc
    ny = 4 if ngx == 32 else 2
    nz = ngx // ny

    def local(cot, b, u, v, kap, th, dep, fp):
        levels = cot.shape[0]
        f32 = jnp.float32

        def vmem(*shape, dtype=f32):
            return pltpu.VMEM(shape, dtype)

        cube = (levels, ROWS, LANES)
        group = 5 if levels % 5 == 0 else 1
        scratch = [
            pltpu.SMEM((levels,), f32), pltpu.SMEM((LANES,), jnp.int32),
            vmem(levels, 80, LANES), vmem(*cube), vmem(*cube), vmem(*cube),
            vmem(ROWS, LANES, dtype=jnp.int32),
            vmem(2, 96, LANES), vmem(2, 96, LANES),
            vmem(16, LANES), vmem(2, 32, LANES), vmem(4, 2, 80, LANES),
            vmem(2, 96, LANES), vmem(2, 96, LANES),
            vmem(ROWS, LANES), vmem(2, ROWS, LANES),
            vmem(FOLD, LANES), vmem(FOLD, LANES), vmem(FOLD, LANES), vmem(FOLD, LANES),
            vmem(16, LANES), vmem(ngx * 16, LANES), vmem(ngx * 6, LANES),
            vmem(nz, FOLD, LANES), vmem(2, FOLD, LANES), vmem(ny, 2, FOLD, LANES),
            vmem(ROWS, LANES),
            vmem(group, 80, LANES), vmem(group, 80, LANES),
            vmem(96, LANES),
            vmem(1, LANES), vmem(max(8, nz * nc), LANES), vmem(1, LANES), vmem(8 if nx * ny < 8 else 32, LANES), vmem(1, LANES), vmem(16, LANES),
            pltpu.SemaphoreType.DMA((8,)),
            pltpu.SemaphoreType.DMA((12,)), pltpu.SemaphoreType.DMA((8,)),
            pltpu.SemaphoreType.DMA((4,)), pltpu.SemaphoreType.DMA((4,)),
            pltpu.SemaphoreType.DMA((6,)), pltpu.SemaphoreType.DMA((2,)),
            pltpu.SemaphoreType.REGULAR,
        ]
        hbm = pl.BlockSpec(memory_space=pltpu.HBM)
        limit = 48 * 1024 * 1024
        shapes = (jax.ShapeDtypeStruct(cube, f32), jax.ShapeDtypeStruct((ROWS, LANES), f32))
        inputs = [pltpu.with_memory_space_constraint(a, pltpu.HBM) for a in (cot, b, u, v, kap, th, dep, fp)]
        held = pl.BlockSpec(memory_space=pltpu.VMEM)
        results = pl.pallas_call(
            functools.partial(kernel, nz, ny, nc, nx, levels, group),
            out_shape=(
                jax.ShapeDtypeStruct((levels, 6, ROWS, LANES), f32),
                jax.ShapeDtypeStruct((5, ROWS, LANES), f32),
            ),
            in_specs=[hbm] * 8,
            out_specs=(held, held),
            scratch_shapes=scratch,
            compiler_params=pltpu.CompilerParams(
                collective_id=0, has_side_effects=True, vmem_limit_bytes=limit
            ),
        )(*inputs)
        return pl.pallas_call(
            functools.partial(finish, levels, group),
            out_shape=shapes,
            in_specs=[held, held],
            out_specs=(hbm, hbm),
            scratch_shapes=[vmem(*cube), pltpu.SemaphoreType.DMA((1 + levels // group,))],
            compiler_params=pltpu.CompilerParams(vmem_limit_bytes=limit),
        )(*results)

    in_specs = (
        P(None, "gy", "gx"), P("gy", "gx"), P(None, "gy", "gx"), P(None, "gy", "gx"),
        P(None, "gy", "gx"), P(), P("gy", "gx"), P("gx"),
    )
    out_specs = (P(None, "gy", "gx"), P("gy", "gx"))
    return jax.shard_map(local, mesh=mesh, in_specs=in_specs, out_specs=out_specs, check_vma=False)
```
